128 devices in a mesh: head: 4 (over y), dp: 32 (over x, z, core).
Axes of the slice: x: 4, y: 4, z: 4, core: 2. Of those that a mesh axis runs over, the one named last changes fastest.
Arguments:
- tokens: bfloat16 [32, 1024, 768], P('dp', 'head'), may hold values from -6 to 6
- lengths: int32 [32], P('dp'), may hold values from 64 to 1024, as said below
- cotangent: bfloat16 [32, 1024, 768], P('dp', 'head'), may hold values from -6 to 6
- gains: float32 [2, 768], replicated, may hold values from 0.2 to 5.1
- conv: float32 [3, 3, 768], replicated, may hold values from -3.6 to 3.6
- w_qkv: float32 [3, 768, 768], P(None, 'dp', 'head'), may hold values from -0.21875 to 0.21875
- w_out: float32 [768, 768], P('head', 'dp'), may hold values from -2.0412415 to 2.0412415
- ffn_weights: float32 [2, 3072, 768], P(None, ('head', 'dp')), may hold values from -0.36084392 to 0.36084392
- mom_qkv: float32 [3, 768, 768], P(None, 'dp', 'head'), may hold values from -0.005859375 to 0.005859375
- mom_out: float32 [768, 768], P('head', 'dp'), may hold values from -0.005859375 to 0.005859375
- mom_ffn: float32 [2, 3072, 768], P(None, ('head', 'dp')), may hold values from -0.005859375 to 0.005859375
- gain_first: float32 [2, 768], replicated, may hold values from -0.001953125 to 0.001953125
- gain_second: float32 [2, 768], replicated, may hold values from 1.2715657e-09 to 5.086263e-09
- conv_first: float32 [3, 3, 768], replicated, may hold values from -0.001953125 to 0.001953125
- conv_second: float32 [3, 3, 768], replicated, may hold values from 1.2715657e-09 to 5.086263e-09
Outputs:
- output: float32 [32, 1024, 768], P('dp', 'head')
- input_grad: float32 [32, 1024, 768], P('dp', 'head')
- grad_gains: float32 [2, 768], replicated
- grad_conv: float32 [3, 3, 768], replicated
- grad_qkv: float32 [3, 768, 768], P(None, 'dp', 'head')
- grad_out: float32 [768, 768], P('head', 'dp')
- grad_ffn: float32 [2, 3072, 768], P(None, ('head', 'dp'))
- grad_norm: float32 [], replicated
- new_mom_qkv: float32 [3, 768, 768], P(None, 'dp', 'head')
- new_mom_out: float32 [768, 768], P('head', 'dp')
- new_mom_ffn: float32 [2, 3072, 768], P(None, ('head', 'dp'))
- new_gain_first: float32 [2, 768], replicated
- new_gain_second: float32 [2, 768], replicated
- new_conv_first: float32 [3, 3, 768], replicated
- new_conv_second: float32 [3, 3, 768], replicated
- new_gains: float32 [2, 768], replicated
- new_conv: float32 [3, 3, 768], replicated
- new_qkv: float32 [3, 768, 768], P(None, 'dp', 'head')
- new_out: float32 [768, 768], P('head', 'dp')
- new_ffn: float32 [2, 3072, 768], P(None, ('head', 'dp'))
The draws below stay inside these ranges and needn't reach their ends.
Inputs may be any that keep to these rules, and one draw needn't show every extreme that they name: Sequence s has real tokens at positions below lengths[s]; one of the last 1 sequence has exactly 1024.
All inputs are finite; a program needn't handle non-finite values.
Results may differ from the reference program's by a relative error of at most 0.023.
The reference program's roundings to bfloat16 on the way count: a program that leaves them out, or rounds other values in their place, can miss the bound.
Values may be sent and summed in bfloat16 or wider, within the bound.
A program may use at most 128 MiB of HBM per device.

```python
import math
import jax
import jax.numpy as jnp
from jax import lax

D = 768
HEADS = 12
HEAD_DIM = 64
FF = 3072
KW = 3
SEQ_LEN = 1024
MIN_LEN = 64
SEQ_DEV = 1
NS_ITERS = 5
STEP = 10
SEQS = 32


def rise_profile(count, bottom, span):
    return bottom + span * jnp.arange(count, dtype=jnp.float32) / (count - 1)


def draw_gains(key, part):
    key = jax.random.fold_in(key, 3)
    bottom, span = (0.6, 1.2)
    levels = jnp.exp(jax.random.uniform(key, (2, D), jnp.float32, -0.7, 0.7))
    return levels * rise_profile(D, bottom, span)[None, :]


def draw_w_out(key, part):
    key = jax.random.fold_in(key, 5)
    bottom, span = (0.6, 1.2)
    base = jax.random.truncated_normal(key, -4.0, 4.0, (D, D), jnp.float32)
    return base * (32.0 / D) ** 0.5 * rise_profile(D, bottom, span)[:, None]


def draw_ffn_weights(key, part):
    key = jax.random.fold_in(key, 7)
    first_key, second_key = jax.random.split(key)
    bottom, span = (0.6, 1.2)
    w_in = jax.random.truncated_normal(first_key, -4.0, 4.0, (FF, D), jnp.float32) * D ** (-0.5)
    w_back = jax.random.truncated_normal(second_key, -4.0, 4.0, (FF, D), jnp.float32) * FF ** (-0.5)
    w_back = w_back * rise_profile(FF, bottom, span)[:, None]
    return jnp.stack([w_in, w_back])


def draw_lengths(key, part):
    key = jax.random.fold_in(key, 11)
    first_key, second_key = jax.random.split(key)
    ticks = jax.random.randint(first_key, (SEQS,), 0, 1025)
    base = MIN_LEN + (SEQ_LEN - MIN_LEN) * (ticks * ticks // 1024) // 1024
    ramp = jnp.arange(SEQS, dtype=jnp.int32)
    grown = base + (SEQ_LEN - base) * ramp // (2 * SEQS)
    chosen = SEQS - SEQ_DEV + jax.random.randint(second_key, (), 0, SEQ_DEV)
    return jnp.where(jnp.arange(SEQS) == chosen, SEQ_LEN, grown).astype(jnp.int32)


def block_scale(key, extent, pieces, smallest, top_value):
    factor_of = 1.0
    for dim, parts in pieces:
        steps = jax.random.uniform(jax.random.fold_in(jax.random.fold_in(key, 6), dim), (parts,), jnp.float32, smallest / len(pieces), top_value / len(pieces))
        factor_of = factor_of * jnp.repeat(jnp.exp(steps), extent[dim] // parts).reshape((-1,) + (1,) * (len(extent) - 1 - dim))
    return factor_of


def bell_draw(own_key, dims, deviation, most, shards=(), kind=jnp.bfloat16):
    drawn = deviation * jax.random.normal(own_key, dims, jnp.float32)
    if shards:
        drawn = drawn * block_scale(own_key, dims, shards, -0.22, 0.18)
    return jnp.clip(drawn, -most, most).astype(kind)


def setup_inputs(seed: int = 0) -> dict:
    seeds = jax.random.split(jax.random.key(seed), 16)
    tokens = bell_draw(seeds[0], (SEQS, SEQ_LEN, D), 1.0, 6.0, ((0, 32), (1, 4)))
    lengths = draw_lengths(jax.random.fold_in(seeds[15], 71), 0)
    cotangent = bell_draw(seeds[2], (SEQS, SEQ_LEN, D), 1.0, 6.0, ((0, 32), (1, 4)))
    gains = draw_gains(jax.random.fold_in(seeds[15], 71), 0)
    conv = bell_draw(seeds[4], (KW, 3, D), 0.6, 3.6, (), jnp.float32)
    w_qkv = bell_draw(seeds[5], (3, D, D), D ** -0.5, 0.21875, ((1, 32), (2, 4)), jnp.float32)
    w_out = draw_w_out(jax.random.fold_in(seeds[15], 71), 0)
    ffn_weights = draw_ffn_weights(jax.random.fold_in(seeds[15], 71), 0)
    mom_qkv = bell_draw(seeds[8], (3, D, D), ((4 * D * D + 2 * D * FF) ** -0.5), 0.005859375, ((1, 32), (2, 4)), jnp.float32)
    mom_out = bell_draw(seeds[9], (D, D), ((4 * D * D + 2 * D * FF) ** -0.5), 0.005859375, ((0, 4), (1, 32)), jnp.float32)
    mom_ffn = bell_draw(seeds[10], (2, FF, D), ((4 * D * D + 2 * D * FF) ** -0.5), 0.005859375, ((1, 128),), jnp.float32)
    gain_first = bell_draw(seeds[11], (2, D), (0.33 * (4 * D * D + 2 * D * FF) ** -0.5), 0.001953125, (), jnp.float32)
    gain_second = jnp.clip(jnp.exp(jax.random.uniform(seeds[12], (2, D), jnp.float32, math.log(1.2715657415895976e-09), math.log(5.08626296635839e-09))), 1.2715657415895976e-09, 5.08626296635839e-09)
    conv_first = bell_draw(seeds[13], (KW, 3, D), (0.33 * (4 * D * D + 2 * D * FF) ** -0.5), 0.001953125, (), jnp.float32)
    conv_second = jnp.clip(jnp.exp(jax.random.uniform(seeds[14], (KW, 3, D), jnp.float32, math.log(1.2715657415895976e-09), math.log(5.08626296635839e-09))), 1.2715657415895976e-09, 5.08626296635839e-09)
    return {"tokens": tokens, "lengths": lengths, "cotangent": cotangent, "gains": gains, "conv": conv, "w_qkv": w_qkv, "w_out": w_out, "ffn_weights": ffn_weights, "mom_qkv": mom_qkv, "mom_out": mom_out, "mom_ffn": mom_ffn, "gain_first": gain_first, "gain_second": gain_second, "conv_first": conv_first, "conv_second": conv_second}


NORM_EPS = 1e-06
NEG_FILL = -1e+30
CLIP_NORM = 1.0
MOMENTUM = 0.95
RATE_IN = 0.02
RATE_OUT = 0.15
ADAM_RATE = 0.5
BETA_ONE = 0.9
BETA_TWO = 0.999
ADAM_EPS = 1e-08
NS_EPS = 1e-07
COEF_A = 3.4445
COEF_B = -4.775
COEF_C = 2.0315
PRECISE = lax.Precision.HIGHEST

@jax.custom_vjp
def low(v):
    return lax.optimization_barrier(v.astype(jnp.bfloat16)).astype(jnp.float32)

@jax.custom_vjp
def low_back(v):
    return v

def low_keep(v):
    return (low(v), None)

def low_pass(kept, grad):
    return (grad,)

def back_keep(v):
    return (v, None)

def back_low(kept, grad):
    return (low(grad),)
low.defvjp(low_keep, low_pass)
low_back.defvjp(back_keep, back_low)

def rms_norm(values, gain):
    return values * lax.rsqrt(lax.optimization_barrier(jnp.mean(values * values, axis=-1, keepdims=True)) + NORM_EPS) * gain

def causal_conv(values, kernel):
    summed = kernel[0] * values
    for offset in range(1, KW):
        delayed = jnp.pad(values, ((offset, 0), (0, 0)))[:values.shape[0]]
        summed = summed + kernel[offset] * delayed
    return summed

def softmax_rows(scores):
    row_max = lax.optimization_barrier(jnp.max(scores, axis=-1, keepdims=True))
    lifted = jnp.exp(scores - row_max)
    return lifted / lax.optimization_barrier(jnp.sum(lifted, axis=-1, keepdims=True))

def layer(params, sequence, length):
    gains, conv, w_qkv, w_out, ffn_weights = params
    seq_count = sequence.shape[0]
    normalized_rows = low(rms_norm(sequence, gains[0]))
    streams = []
    for kind_index in range(3):
        projected_rows = low_back(jnp.dot(normalized_rows, low(w_qkv[kind_index]), precision=PRECISE))
        streams.append(low_back(low(causal_conv(projected_rows, conv[:, kind_index]))))
    queries, keys_all, values_all = [stream.reshape(seq_count, HEADS, HEAD_DIM) for stream in streams]
    raw_scores = low_back(jnp.einsum('qhd,khd->hqk', queries, keys_all, precision=PRECISE))
    places = jnp.arange(seq_count)
    allowed = (places[None, :] <= places[:, None]) & (places[None, :] < length)
    scores = jnp.where(allowed[None], raw_scores * HEAD_DIM ** (-0.5), NEG_FILL)
    weight_collection = low(softmax_rows(scores))
    attended = jnp.einsum('hqk,khd->qhd', weight_collection, values_all, precision=PRECISE).reshape(seq_count, D)
    attended = low_back(low(attended))
    middle = sequence + low_back(jnp.dot(attended, low(w_out), precision=PRECISE))
    normed_two = low(rms_norm(middle, gains[1]))
    hidden_state_rows = low_back(jnp.dot(normed_two, low(ffn_weights[0]).T, precision=PRECISE))
    relu_active_rows = low(jnp.square(jnp.maximum(hidden_state_rows, 0.0)))
    return middle + low_back(jnp.dot(relu_active_rows, low(ffn_weights[1]), precision=PRECISE))

def orthogonal(moment):
    magnitude = jnp.sqrt(lax.optimization_barrier(jnp.sum(moment * moment, axis=(-2, -1), keepdims=True)))
    iterate = moment / (magnitude + NS_EPS)
    for sweep in range(NS_ITERS):
        gram_matrix = jnp.einsum('...nd,...ne->...de', iterate, iterate, precision=PRECISE)
        polynomial = COEF_B * gram_matrix + COEF_C * jnp.einsum('...de,...ef->...df', gram_matrix, gram_matrix, precision=PRECISE)
        iterate = COEF_A * iterate + jnp.einsum('...nd,...de->...ne', iterate, polynomial, precision=PRECISE)
    return iterate

def adam_step(weight, gradient, moment_one, moment_two):
    first_new = BETA_ONE * moment_one + (1.0 - BETA_ONE) * gradient
    second_new = BETA_TWO * moment_two + (1.0 - BETA_TWO) * gradient * gradient
    stepped = first_new / (1.0 - BETA_ONE ** STEP) / (jnp.sqrt(second_new / (1.0 - BETA_TWO ** STEP)) + ADAM_EPS)
    return (first_new, second_new, weight - ADAM_RATE * stepped)

def reference(tokens, lengths, cotangent, gains, conv, w_qkv, w_out, ffn_weights, mom_qkv, mom_out, mom_ffn, gain_first, gain_second, conv_first, conv_second):
    inputs = tokens.astype(jnp.float32)
    params = (gains, conv, w_qkv, w_out, ffn_weights)

    def whole(param_set, sequences):

        def one_sequence(pair):
            return layer(param_set, pair[0], pair[1])
        return lax.map(jax.checkpoint(one_sequence), (sequences, lengths))
    output, pullback = jax.vjp(whole, params, inputs)
    places = jnp.arange(SEQ_LEN)
    real_rows = (places[None, :] < lengths[:, None]).astype(jnp.float32)
    grads, input_grad = pullback(cotangent.astype(jnp.float32) * real_rows[:, :, None])
    squares = jnp.zeros((), jnp.float32)
    for leaf in grads:
        squares = squares + jnp.sum(leaf * leaf)
    grad_norm = jnp.sqrt(squares)
    factor = CLIP_NORM / jnp.maximum(grad_norm, CLIP_NORM)
    grad_gains, grad_conv, grad_qkv, grad_out, grad_ffn = [leaf * factor for leaf in grads]
    new_mom_qkv = MOMENTUM * mom_qkv + grad_qkv
    new_mom_out = MOMENTUM * mom_out + grad_out
    new_mom_ffn = MOMENTUM * mom_ffn + grad_ffn
    ffn_orth = orthogonal(new_mom_ffn)
    blocks = jnp.concatenate([new_mom_qkv.reshape(3, D, HEADS, HEAD_DIM).transpose(0, 2, 1, 3), new_mom_out.reshape(HEADS, HEAD_DIM, D).transpose(0, 2, 1)[None]], 0)
    block_orth = orthogonal(blocks)
    qkv_orth = block_orth[:3].transpose(0, 2, 1, 3).reshape(3, D, D)
    out_orth = block_orth[3].transpose(0, 2, 1).reshape(D, D)
    new_qkv = w_qkv - RATE_IN * jnp.sqrt(jnp.float32(D)) * qkv_orth
    new_out = w_out - RATE_OUT * jnp.sqrt(jnp.float32(D)) * out_orth
    new_ffn = ffn_weights - RATE_IN * jnp.sqrt(jnp.float32(max(FF, D))) * ffn_orth
    new_gain_first, new_gain_second, new_gains = adam_step(gains, grad_gains, gain_first, gain_second)
    new_conv_first, new_conv_second, new_conv = adam_step(conv, grad_conv, conv_first, conv_second)
    return (output, input_grad, grad_gains, grad_conv, grad_qkv, grad_out, grad_ffn, grad_norm, new_mom_qkv, new_mom_out, new_mom_ffn, new_gain_first, new_gain_second, new_conv_first, new_conv_second, new_gains, new_conv, new_qkv, new_out, new_ffn)
```

```python
import math

import jax
import jax.numpy as jnp
from jax import lax
from jax.sharding import PartitionSpec as P

D = 768
HEADS = 12
HEAD_DIM = 64
FF = 3072
KW = 3
NS_ITERS = 5
STEP = 10


NORM_EPS = 1e-06
NEG_FILL = -1e30
CLIP_NORM = 1.0
MOMENTUM = 0.95
RATE_IN = 0.02
RATE_OUT = 0.15
ADAM_RATE = 0.5
BETA_ONE = 0.9
BETA_TWO = 0.999
ADAM_EPS = 1e-08
NS_EPS = 1e-07
COEF_A = 3.4445
COEF_B = -4.775
COEF_C = 2.0315
PRECISE = lax.Precision.HIGHEST


def norm_parts(values, gain):
    inverse = lax.rsqrt(jnp.mean(values * values, axis=-1, keepdims=True) + NORM_EPS)
    unit_rows = values * inverse
    return (unit_rows, inverse, (unit_rows * gain).astype(jnp.bfloat16))


def norm_back(upstream, unit_rows, inverse, gain):
    scaled = upstream * gain
    centred = scaled - unit_rows * jnp.mean(scaled * unit_rows, axis=-1, keepdims=True)
    return (inverse * centred, jnp.sum(upstream * unit_rows, axis=(0, 1)))


def shift_down(values, offset):
    return jnp.pad(values, ((0, 0), (0, 0), (offset, 0), (0, 0)))[:, :, : values.shape[2]]


def shift_up(values, offset):
    return jnp.pad(values, ((0, 0), (0, 0), (0, offset), (0, 0)))[:, :, offset:]


def conv_forward(projected_rows, kernel):
    summed = kernel[0][:, None, None, :] * projected_rows
    for offset in range(1, KW):
        summed = summed + kernel[offset][:, None, None, :] * shift_down(projected_rows, offset)
    return summed


def conv_back(upstream_lower_rows, projected_rows, kernel):
    upstream = upstream_lower_rows.astype(jnp.float32)
    summed = kernel[0][:, None, None, :] * upstream
    pieces = [jnp.sum(upstream * projected_rows, axis=(1, 2))]
    for offset in range(1, KW):
        summed = summed + kernel[offset][:, None, None, :] * shift_up(upstream, offset)
        pieces.append(jnp.sum(upstream * shift_down(projected_rows, offset), axis=(1, 2)))
    return (summed, jnp.stack(pieces))


def masked_scores(query_rows, keys_all, start_row, length):
    raw_scores = jnp.einsum(
        "qhd,khd->hqk", query_rows, keys_all, preferred_element_type=jnp.float32
    )
    row_ids = start_row + jnp.arange(query_rows.shape[0])
    col_ids = jnp.arange(keys_all.shape[0])
    allowed = (col_ids[None, :] <= row_ids[:, None]) & (col_ids[None, :] < length)
    return jnp.where(allowed[None], raw_scores * HEAD_DIM ** (-0.5), NEG_FILL)


def attend_forward(queries, keys_all, values_all, length):
    seq_count = queries.shape[0]
    block_rows = min(512, seq_count)
    outputs, maxima, totals = ([], [], [])
    for start_row in range(0, seq_count, block_rows):
        scores = masked_scores(
            queries[start_row : start_row + block_rows], keys_all, start_row, length
        )
        row_max = jnp.max(scores, axis=-1, keepdims=True)
        lifted = jnp.exp(scores - row_max)
        row_sum = jnp.sum(lifted, axis=-1, keepdims=True)
        weight_collection = (lifted / row_sum).astype(jnp.bfloat16)
        outputs.append(
            jnp.einsum(
                "hqk,khd->qhd", weight_collection, values_all, preferred_element_type=jnp.float32
            )
        )
        maxima.append(row_max)
        totals.append(row_sum)
    return (jnp.concatenate(outputs, 0), jnp.concatenate(maxima, 1), jnp.concatenate(totals, 1))


def attend_back(queries, keys_all, values_all, length, maxima, totals, upstream):
    seq_count = queries.shape[0]
    block_rows = min(512, seq_count)
    query_grads = []
    key_grad = jnp.zeros(keys_all.shape, jnp.float32)
    value_grad = jnp.zeros(values_all.shape, jnp.float32)
    for start_row in range(0, seq_count, block_rows):
        stop_row = start_row + block_rows
        query_rows = queries[start_row:stop_row]
        upstream_rows = upstream[start_row:stop_row]
        scores = masked_scores(query_rows, keys_all, start_row, length)
        probs_full = jnp.exp(scores - maxima[:, start_row:stop_row]) / totals[:, start_row:stop_row]
        prob_grad = jnp.einsum(
            "qhd,khd->hqk", upstream_rows, values_all, preferred_element_type=jnp.float32
        )
        centre = jnp.sum(prob_grad * probs_full, axis=-1, keepdims=True)
        score_grad = (probs_full * (prob_grad - centre) * HEAD_DIM ** (-0.5)).astype(jnp.bfloat16)
        query_grads.append(
            jnp.einsum("hqk,khd->qhd", score_grad, keys_all, preferred_element_type=jnp.float32)
        )
        key_grad = key_grad + jnp.einsum(
            "hqk,qhd->khd", score_grad, query_rows, preferred_element_type=jnp.float32
        )
        value_grad = value_grad + jnp.einsum(
            "hqk,qhd->khd",
            probs_full.astype(jnp.bfloat16),
            upstream_rows,
            preferred_element_type=jnp.float32,
        )
    return (jnp.concatenate(query_grads, 0), key_grad, value_grad)


def ffn_forward(normalized_rows, weight_collection):
    hidden_state_rows = jnp.einsum(
        "cbv,jv->cbj", normalized_rows, weight_collection[0], preferred_element_type=jnp.float32
    )
    relu_active_rows = jnp.square(jnp.maximum(hidden_state_rows, 0.0)).astype(jnp.bfloat16)
    return (
        hidden_state_rows,
        relu_active_rows,
        jnp.einsum(
            "gen,nc->gec",
            relu_active_rows,
            weight_collection[1],
            preferred_element_type=jnp.float32,
        ),
    )


def ffn_back(
    normalized_rows, weight_collection, hidden_state_rows, relu_active_rows, upstream_lower_rows
):
    grad_back_w = jnp.einsum(
        "vgq,vgh->qh", relu_active_rows, upstream_lower_rows, preferred_element_type=jnp.float32
    )
    grad_active = jnp.einsum(
        "cbv,jv->cbj", upstream_lower_rows, weight_collection[1], preferred_element_type=jnp.float32
    )
    hidden_state_gradient = (grad_active * 2.0 * jnp.maximum(hidden_state_rows, 0.0)).astype(
        jnp.bfloat16
    )
    input_weight_gradient = jnp.einsum(
        "vgq,vgh->qh", hidden_state_gradient, normalized_rows, preferred_element_type=jnp.float32
    )
    grad_normed = jnp.einsum(
        "gen,nc->gec",
        hidden_state_gradient,
        weight_collection[0],
        preferred_element_type=jnp.float32,
    )
    return (grad_normed, jnp.stack([input_weight_gradient, grad_back_w]))


def ns_chain(iterate, gram_matrix):
    identity = jnp.eye(gram_matrix.shape[-1], dtype=jnp.float32)

    def times(left, right):
        return jnp.einsum("...de,...ef->...df", left, right, precision=lax.Precision.HIGH)

    for sweep in range(NS_ITERS):
        factor = COEF_A * identity + COEF_B * gram_matrix + COEF_C * times(gram_matrix, gram_matrix)
        iterate = times(iterate, factor)
        if sweep < NS_ITERS - 1:
            gram_matrix = times(times(factor, gram_matrix), factor)
    return iterate


def adam_step(weight, gradient, moment_one, moment_two):
    first_new = BETA_ONE * moment_one + (1.0 - BETA_ONE) * gradient
    second_new = BETA_TWO * moment_two + (1.0 - BETA_TWO) * gradient * gradient
    stepped = (
        first_new
        / (1.0 - BETA_ONE**STEP)
        / (jnp.sqrt(second_new / (1.0 - BETA_TWO**STEP)) + ADAM_EPS)
    )
    return (first_new, second_new, weight - ADAM_RATE * stepped)


def per_device(
    tokens,
    lengths,
    cotangent,
    gains,
    conv,
    w_qkv,
    w_out,
    ffn_weights,
    mom_qkv,
    mom_out,
    mom_ffn,
    gain_first,
    gain_second,
    conv_first,
    conv_second,
):
    heads_axis = lax.axis_size("head")
    head_at = lax.axis_index("head")
    seq_here, rows_here, width = tokens.shape
    seq_length = rows_here * heads_axis
    cols_here = w_qkv.shape[2]
    heads_local = cols_here // HEAD_DIM
    positions = head_at * rows_here + jnp.arange(rows_here)
    real_rows = (positions[None, :] < lengths[:, None]).astype(jnp.float32)[:, :, None]
    kernel = lax.dynamic_slice_in_dim(conv, head_at * cols_here, cols_here, 2)
    query_key_value_lower, output_lower_rows, ffn_low = (
        lax.all_gather(w_qkv.astype(jnp.bfloat16), "dp", axis=1, tiled=True),
        lax.all_gather(w_out.astype(jnp.bfloat16), "dp", axis=1, tiled=True),
        lax.all_gather(ffn_weights.astype(jnp.bfloat16), "dp", axis=1, tiled=True),
    )
    resid_in = tokens.astype(jnp.float32)
    unit_one, inverse_one, normed_one = norm_parts(resid_in, gains[0])
    normalized_every_row = lax.all_gather(normed_one, "head", axis=1, tiled=True)
    projected_rows = jnp.einsum(
        "vru,jua->jvra",
        normalized_every_row,
        query_key_value_lower,
        preferred_element_type=jnp.float32,
    )
    streams = conv_forward(projected_rows, kernel).astype(jnp.bfloat16)
    shaped = streams.reshape(3, seq_here, seq_length, heads_local, HEAD_DIM)

    def forward_one(bundle):
        return attend_forward(bundle[0], bundle[1], bundle[2], bundle[3])

    attended, maxima, totals = lax.map(forward_one, (shaped[0], shaped[1], shaped[2], lengths))
    attended_lower_rows = attended.reshape(seq_here, seq_length, cols_here).astype(jnp.bfloat16)
    projection_portion = jnp.einsum(
        "azp,pm->azm", attended_lower_rows, output_lower_rows, preferred_element_type=jnp.float32
    )
    attn_rows = lax.psum_scatter(projection_portion, "head", scatter_dimension=1, tiled=True)
    middle = resid_in + attn_rows
    unit_two, inverse_two, normed_two = norm_parts(middle, gains[1])
    upstream = cotangent.astype(jnp.float32) * real_rows
    upstream_lower_rows = upstream.astype(jnp.bfloat16)
    normed_wide = lax.all_gather(normed_two, "head", axis=1, tiled=True)
    hidden_state_rows, relu_active_rows, ffn_part = ffn_forward(normed_wide, ffn_low)
    ffn_rows_out = lax.psum_scatter(
        ffn_part.astype(jnp.bfloat16), "head", scatter_dimension=1, tiled=True
    ).astype(jnp.float32)
    output = middle + ffn_rows_out
    upstream_wide = lax.all_gather(upstream_lower_rows, "head", axis=1, tiled=True)
    grad_normed_part, ffn_grad = ffn_back(
        normed_wide, ffn_low, hidden_state_rows, relu_active_rows, upstream_wide
    )
    grad_normed_two = lax.psum_scatter(grad_normed_part, "head", scatter_dimension=1, tiled=True)
    grad_norm_two, gain_two_grad = norm_back(grad_normed_two, unit_two, inverse_two, gains[1])
    grad_middle = upstream + grad_norm_two
    attention_wide_gradient = lax.all_gather(
        grad_middle.astype(jnp.bfloat16), "head", axis=1, tiled=True
    )
    out_grad = jnp.einsum(
        "tzu,tzx->ux",
        attended_lower_rows,
        attention_wide_gradient,
        preferred_element_type=jnp.float32,
    )
    grad_attended = jnp.einsum(
        "kmh,uh->kmu",
        attention_wide_gradient,
        output_lower_rows,
        preferred_element_type=jnp.float32,
    ).astype(jnp.bfloat16)
    grad_shaped = grad_attended.reshape(seq_here, seq_length, heads_local, HEAD_DIM)

    def back_one(bundle):
        return attend_back(
            bundle[0], bundle[1], bundle[2], bundle[3], bundle[4], bundle[5], bundle[6]
        )

    query_grad, key_grad, value_grad = lax.map(
        back_one, (shaped[0], shaped[1], shaped[2], lengths, maxima, totals, grad_shaped)
    )
    grad_streams = (
        jnp.stack([query_grad, key_grad, value_grad])
        .reshape(3, seq_here, seq_length, cols_here)
        .astype(jnp.bfloat16)
    )
    grad_projected, kernel_grad = conv_back(grad_streams, projected_rows, kernel)
    projected_lower_gradient = grad_projected.astype(jnp.bfloat16)
    qkv_grad = jnp.einsum(
        "uvm,buvh->bmh",
        normalized_every_row,
        projected_lower_gradient,
        preferred_element_type=jnp.float32,
    )
    grad_normed_part_one = jnp.einsum(
        "rptv,rov->pto",
        projected_lower_gradient,
        query_key_value_lower,
        preferred_element_type=jnp.float32,
    )
    grad_normed_one = lax.psum_scatter(
        grad_normed_part_one.astype(jnp.bfloat16), "head", scatter_dimension=1, tiled=True
    ).astype(jnp.float32)
    grad_norm_one, gain_one_grad = norm_back(grad_normed_one, unit_one, inverse_one, gains[0])
    input_grad = grad_middle + grad_norm_one
    qkv_part, out_part, ffn_part_grad = (
        lax.psum_scatter(
            qkv_grad.astype(jnp.bfloat16), "dp", scatter_dimension=1, tiled=True
        ).astype(jnp.float32),
        lax.psum_scatter(
            out_grad.astype(jnp.bfloat16), "dp", scatter_dimension=1, tiled=True
        ).astype(jnp.float32),
        lax.psum_scatter(
            ffn_grad.astype(jnp.bfloat16), "dp", scatter_dimension=1, tiled=True
        ).astype(jnp.float32),
    )
    conv_placed = lax.dynamic_update_slice_in_dim(
        jnp.zeros(conv.shape, jnp.float32), kernel_grad, head_at * cols_here, 2
    )
    squares = (
        jnp.sum(qkv_part * qkv_part)
        + jnp.sum(out_part * out_part)
        + jnp.sum(ffn_part_grad * ffn_part_grad)
    )
    gain_sum, conv_sum, square_sum = lax.psum(
        (jnp.stack([gain_one_grad, gain_two_grad]), conv_placed, squares), ("head", "dp")
    )
    grad_norm = jnp.sqrt(square_sum + jnp.sum(gain_sum * gain_sum) + jnp.sum(conv_sum * conv_sum))
    factor = CLIP_NORM / jnp.maximum(grad_norm, CLIP_NORM)
    grad_gains = gain_sum * factor
    grad_conv = conv_sum * factor
    grad_qkv = qkv_part * factor
    grad_out = out_part * factor
    grad_ffn = ffn_part_grad * factor
    new_mom_qkv = MOMENTUM * mom_qkv + grad_qkv
    new_mom_out = MOMENTUM * mom_out + grad_out
    new_mom_ffn = MOMENTUM * mom_ffn + grad_ffn
    shard_rows = w_qkv.shape[1]
    head_iter = jnp.concatenate(
        [
            new_mom_qkv.reshape(3, shard_rows, heads_local, HEAD_DIM).transpose(0, 2, 1, 3),
            new_mom_out.reshape(heads_local, HEAD_DIM, shard_rows).transpose(0, 2, 1)[None],
        ],
        0,
    )
    ffn_iter = new_mom_ffn
    head_offset = head_at * heads_local
    local_ffn = jnp.einsum("knd,kne->kde", ffn_iter, ffn_iter, precision=PRECISE)
    local_heads = jnp.einsum("kgnd,kgne->kgde", head_iter, head_iter, precision=PRECISE)
    placed = lax.dynamic_update_slice_in_dim(
        jnp.zeros((4, HEADS, HEAD_DIM, HEAD_DIM), jnp.float32), local_heads, head_offset, 1
    )
    gram_ffn, gram_placed = lax.psum((local_ffn, placed), ("head", "dp"))
    gram_heads = lax.dynamic_slice_in_dim(gram_placed, head_offset, heads_local, 1)
    ffn_scale = 1.0 / (jnp.sqrt(jnp.trace(gram_ffn, axis1=1, axis2=2)) + NS_EPS)
    head_scale = 1.0 / (jnp.sqrt(jnp.trace(gram_heads, axis1=2, axis2=3)) + NS_EPS)
    ffn_iter = ns_chain(
        ffn_iter * ffn_scale[:, None, None], gram_ffn * jnp.square(ffn_scale)[:, None, None]
    )
    head_iter = ns_chain(
        head_iter * head_scale[:, :, None, None],
        gram_heads * jnp.square(head_scale)[:, :, None, None],
    )
    qkv_orth = head_iter[:3].transpose(0, 2, 1, 3).reshape(3, shard_rows, cols_here)
    out_orth = head_iter[3].transpose(0, 2, 1).reshape(cols_here, shard_rows)
    new_qkv = w_qkv - RATE_IN * math.sqrt(D) * qkv_orth
    new_out = w_out - RATE_OUT * math.sqrt(D) * out_orth
    new_ffn = ffn_weights - RATE_IN * math.sqrt(max(FF, D)) * ffn_iter
    new_gain_first, new_gain_second, new_gains = adam_step(
        gains, grad_gains, gain_first, gain_second
    )
    new_conv_first, new_conv_second, new_conv = adam_step(conv, grad_conv, conv_first, conv_second)
    return (
        output,
        input_grad,
        grad_gains,
        grad_conv,
        grad_qkv,
        grad_out,
        grad_ffn,
        grad_norm,
        new_mom_qkv,
        new_mom_out,
        new_mom_ffn,
        new_gain_first,
        new_gain_second,
        new_conv_first,
        new_conv_second,
        new_gains,
        new_conv,
        new_qkv,
        new_out,
        new_ffn,
    )


def solution(mesh):
    placed = (
        P("dp", "head", None),
        P("dp"),
        P("dp", "head", None),
        P(),
        P(),
        P(None, "dp", "head"),
        P("head", "dp"),
        P(None, ("head", "dp"), None),
        P(None, "dp", "head"),
        P("head", "dp"),
        P(None, ("head", "dp"), None),
        P(),
        P(),
        P(),
        P(),
    )
    return jax.shard_map(
        per_device,
        mesh=mesh,
        in_specs=placed,
        out_specs=(
            P("dp", "head", None),
            P("dp", "head", None),
            P(),
            P(),
            P(None, "dp", "head"),
            P("head", "dp"),
            P(None, ("head", "dp"), None),
            P(),
            P(None, "dp", "head"),
            P("head", "dp"),
            P(None, ("head", "dp"), None),
            P(),
            P(),
            P(),
            P(),
            P(),
            P(),
            P(None, "dp", "head"),
            P("head", "dp"),
            P(None, ("head", "dp"), None),
        ),
        check_vma=False,
    )
```

```python
import math

import jax
import jax.numpy as jnp
from jax import lax
from jax.experimental import pallas as pl
from jax.experimental.pallas import tpu as pltpu
from jax.sharding import PartitionSpec as P

D = 768
HEADS = 12
HEAD_DIM = 64
FF = 3072
KW = 3
NS_ITERS = 5
STEP = 10


NORM_EPS = 1e-06
NEG_FILL = -1e30
CLIP_NORM = 1.0
MOMENTUM = 0.95
RATE_IN = 0.02
RATE_OUT = 0.15
ADAM_RATE = 0.5
BETA_ONE = 0.9
BETA_TWO = 0.999
ADAM_EPS = 1e-08
NS_EPS = 1e-07
COEF_A = 3.4445
COEF_B = -4.775
COEF_C = 2.0315
PRECISE = lax.Precision.HIGHEST


def norm_parts(values, gain):
    inverse = lax.rsqrt(jnp.mean(values * values, axis=-1, keepdims=True) + NORM_EPS)
    unit_rows = values * inverse
    return (unit_rows, inverse, (unit_rows * gain).astype(jnp.bfloat16))


def norm_back(upstream, unit_rows, inverse, gain):
    scaled = upstream * gain
    centred = scaled - unit_rows * jnp.mean(scaled * unit_rows, axis=-1, keepdims=True)
    return (inverse * centred, jnp.sum(upstream * unit_rows, axis=(0, 1)))


def shift_down(values, offset):
    return jnp.pad(values, ((0, 0), (0, 0), (offset, 0), (0, 0)))[:, :, : values.shape[2]]


def shift_up(values, offset):
    return jnp.pad(values, ((0, 0), (0, 0), (0, offset), (0, 0)))[:, :, offset:]


def conv_forward(projected_rows, kernel):
    summed = kernel[0][:, None, None, :] * projected_rows
    for offset in range(1, KW):
        summed = summed + kernel[offset][:, None, None, :] * shift_down(projected_rows, offset)
    return summed


def conv_back(upstream_lower_rows, projected_rows, kernel):
    upstream = upstream_lower_rows.astype(jnp.float32)
    summed = kernel[0][:, None, None, :] * upstream
    pieces = [jnp.sum(upstream * projected_rows, axis=(1, 2))]
    for offset in range(1, KW):
        summed = summed + kernel[offset][:, None, None, :] * shift_up(upstream, offset)
        pieces.append(jnp.sum(upstream * shift_down(projected_rows, offset), axis=(1, 2)))
    return (summed, jnp.stack(pieces))


def masked_scores(query_rows, keys_all, start_row, length):
    raw_scores = jnp.einsum(
        "qhd,khd->hqk", query_rows, keys_all, preferred_element_type=jnp.float32
    )
    row_ids = start_row + jnp.arange(query_rows.shape[0])
    col_ids = jnp.arange(keys_all.shape[0])
    allowed = (col_ids[None, :] <= row_ids[:, None]) & (col_ids[None, :] < length)
    return jnp.where(allowed[None], raw_scores * HEAD_DIM ** (-0.5), NEG_FILL)


def attend_forward(queries, keys_all, values_all, length):
    seq_count = queries.shape[0]
    block_rows = min(512, seq_count)
    outputs, maxima, totals = ([], [], [])
    for start_row in range(0, seq_count, block_rows):
        scores = masked_scores(
            queries[start_row : start_row + block_rows], keys_all, start_row, length
        )
        row_max = jnp.max(scores, axis=-1, keepdims=True)
        lifted = jnp.exp(scores - row_max)
        row_sum = jnp.sum(lifted, axis=-1, keepdims=True)
        weight_collection = (lifted / row_sum).astype(jnp.bfloat16)
        outputs.append(
            jnp.einsum(
                "hqk,khd->qhd", weight_collection, values_all, preferred_element_type=jnp.float32
            )
        )
        maxima.append(row_max)
        totals.append(row_sum)
    return (jnp.concatenate(outputs, 0), jnp.concatenate(maxima, 1), jnp.concatenate(totals, 1))


def attend_back(queries, keys_all, values_all, length, maxima, totals, upstream):
    seq_count = queries.shape[0]
    block_rows = min(512, seq_count)
    query_grads = []
    key_grad = jnp.zeros(keys_all.shape, jnp.float32)
    value_grad = jnp.zeros(values_all.shape, jnp.float32)
    for start_row in range(0, seq_count, block_rows):
        stop_row = start_row + block_rows
        query_rows = queries[start_row:stop_row]
        upstream_rows = upstream[start_row:stop_row]
        scores = masked_scores(query_rows, keys_all, start_row, length)
        probs_full = jnp.exp(scores - maxima[:, start_row:stop_row]) / totals[:, start_row:stop_row]
        prob_grad = jnp.einsum(
            "qhd,khd->hqk", upstream_rows, values_all, preferred_element_type=jnp.float32
        )
        centre = jnp.sum(prob_grad * probs_full, axis=-1, keepdims=True)
        score_grad = (probs_full * (prob_grad - centre) * HEAD_DIM ** (-0.5)).astype(jnp.bfloat16)
        query_grads.append(
            jnp.einsum("hqk,khd->qhd", score_grad, keys_all, preferred_element_type=jnp.float32)
        )
        key_grad = key_grad + jnp.einsum(
            "hqk,qhd->khd", score_grad, query_rows, preferred_element_type=jnp.float32
        )
        value_grad = value_grad + jnp.einsum(
            "hqk,qhd->khd",
            probs_full.astype(jnp.bfloat16),
            upstream_rows,
            preferred_element_type=jnp.float32,
        )
    return (jnp.concatenate(query_grads, 0), key_grad, value_grad)


def ffn_forward(normalized_rows, weight_collection):
    hidden_state_rows = jnp.einsum(
        "cbv,jv->cbj", normalized_rows, weight_collection[0], preferred_element_type=jnp.float32
    )
    relu_active_rows = jnp.square(jnp.maximum(hidden_state_rows, 0.0)).astype(jnp.bfloat16)
    return (
        hidden_state_rows,
        relu_active_rows,
        jnp.einsum(
            "gen,nc->gec",
            relu_active_rows,
            weight_collection[1],
            preferred_element_type=jnp.float32,
        ),
    )


def ffn_back(
    normalized_rows, weight_collection, hidden_state_rows, relu_active_rows, upstream_lower_rows
):
    grad_back_w = jnp.einsum(
        "vgq,vgh->qh", relu_active_rows, upstream_lower_rows, preferred_element_type=jnp.float32
    )
    grad_active = jnp.einsum(
        "cbv,jv->cbj", upstream_lower_rows, weight_collection[1], preferred_element_type=jnp.float32
    )
    hidden_state_gradient = (grad_active * 2.0 * jnp.maximum(hidden_state_rows, 0.0)).astype(
        jnp.bfloat16
    )
    input_weight_gradient = jnp.einsum(
        "vgq,vgh->qh", hidden_state_gradient, normalized_rows, preferred_element_type=jnp.float32
    )
    grad_normed = jnp.einsum(
        "gen,nc->gec",
        hidden_state_gradient,
        weight_collection[0],
        preferred_element_type=jnp.float32,
    )
    return (grad_normed, jnp.stack([input_weight_gradient, grad_back_w]))


SUB = 24
PAIR = 2 * SUB
BLK = 256
MESH_IDS = pl.DeviceIdType.MESH


def place():
    flat = lax.axis_index("dp")
    return flat // 8, lax.axis_index("head"), (flat // 2) % 4, flat % 2


def device(x, y, z, core):
    return (y % 4, ((x % 4) * 4 + z % 4) * 2 + core)


def greet(others):
    barrier = pltpu.get_barrier_semaphore()
    for other in others:
        pl.semaphore_signal(barrier, inc=1, device_id=other, device_id_type=MESH_IDS)
    pl.semaphore_wait(barrier, len(others))


def send(source, target, sems, index, other):
    copy = pltpu.make_async_remote_copy(
        src_ref=source,
        dst_ref=target,
        send_sem=sems[0].at[index],
        recv_sem=sems[1].at[index],
        device_id=other,
        device_id_type=MESH_IDS,
    )
    copy.start()
    return copy


def rows(start, count):
    return pl.ds(pl.multiple_of(start, 8), count)


def split(values):
    high = values.astype(jnp.bfloat16)
    return high, (values - high.astype(jnp.float32)).astype(jnp.bfloat16)


def product(left, right, dims=(((1,), (0,)), ((), ()))):
    lh, ll = left
    rh, rl = right

    def dot(a, b):
        return lax.dot_general(a, b, dims, preferred_element_type=jnp.float32)

    return dot(lh, rh) + (dot(lh, rl) + dot(ll, rh))


UPPER = ((0, 0), (0, 1), (0, 2), (1, 1), (1, 2), (2, 2))


def sum_kernel(
    g_ffn, g_heads, m_ffn, m_heads, small,
    small_out, gram_out, hgram_out, x_out, xh_out,
    gin, min_, ghin, mhin, s_core, s_x, s_z, s_y, part, r_one, r_two, r_three, hpart, hr_one, hr_two,
    send_sem, recv_sem,
):
    x, y, z, core = place()
    sems = (send_sem, recv_sem)
    sibling = device(x, y, z, 1 - core)
    along = {
        "x": [device(x + k, y, z, core) for k in (1, 2, 3)],
        "z": [device(x, y, z + k, core) for k in (1, 2, 3)],
        "y": [device(x, y + k, z, core) for k in (1, 2, 3)],
    }
    greet([sibling] + along["x"] + along["z"] + along["y"])
    swaps = [
        send(g_ffn.at[1 - core], gin, sems, 0, sibling),
        send(m_ffn.at[1 - core], min_, sems, 1, sibling),
        send(g_heads.at[pl.ds(2 - 2 * core, 2)], ghin, sems, 2, sibling),
        send(m_heads.at[pl.ds(2 - 2 * core, 2)], mhin, sems, 3, sibling),
    ]
    lanes_ffn = jnp.sum(g_ffn[...] * g_ffn[...], axis=(0, 1))
    lanes_heads = jnp.sum(g_heads[...] * g_heads[...], axis=(0, 1))
    own = small[...]
    row_ids = lax.broadcasted_iota(jnp.int32, own.shape, 0)
    wide = jnp.concatenate([lanes_heads, jnp.zeros((D - lanes_heads.shape[0],), jnp.float32)])
    own = own + jnp.where(row_ids == 11, lanes_ffn[None, :] + wide[None, :], 0.0)
    number = 4
    s_core[core] = own
    copy = send(s_core.at[core], s_core.at[core], sems, number, sibling)
    copy.wait()
    total = s_core[0] + s_core[1]
    number = 5
    for slots, axis, here in ((s_x, "x", x), (s_z, "z", z), (s_y, "y", y)):
        slots[here] = total
        copies = [
            send(slots.at[here], slots.at[here], sems, number + k, along[axis][k]) for k in range(3)
        ]
        for copy in copies:
            copy.wait()
        total = (slots[0] + slots[1]) + (slots[2] + slots[3])
        number += 3
    small_out[...] = total
    squared = jnp.sum(jnp.where(row_ids < 11, total * total, total), axis=(0, 1), keepdims=True)
    factor = CLIP_NORM / jnp.maximum(jnp.sqrt(squared), CLIP_NORM)
    for copy in swaps:
        copy.wait()
    here_rows = MOMENTUM * m_ffn[core] + factor * g_ffn[core]
    there_rows = MOMENTUM * min_[...] + factor * gin[...]
    x_out[rows(core * SUB, SUB), :] = here_rows
    x_out[rows((1 - core) * SUB, SUB), :] = there_rows
    for kind in range(2):
        xh_out[kind, rows(core * SUB, SUB), :] = (
            MOMENTUM * m_heads[2 * core + kind] + factor * g_heads[2 * core + kind]
        )
        xh_out[kind, rows((1 - core) * SUB, SUB), :] = MOMENTUM * mhin[kind] + factor * ghin[kind]
    transposed = (((0,), (0,)), ((), ()))
    for number_of, (i, j) in enumerate(UPPER):
        part[number_of * BLK : (number_of + 1) * BLK, :] = product(
            split(x_out[:, i * BLK : (i + 1) * BLK]),
            split(x_out[:, j * BLK : (j + 1) * BLK]),
            transposed,
        )
    columns = xh_out.shape[2]
    r_ids = lax.broadcasted_iota(jnp.int32, (columns, columns), 0) // HEAD_DIM
    c_ids = lax.broadcasted_iota(jnp.int32, (columns, columns), 1) // HEAD_DIM
    packed = []
    for kind in range(2):
        pieces = split(xh_out[kind])
        gram = jnp.where(r_ids == c_ids, product(pieces, pieces, transposed), 0.0)
        folded = gram[:, :HEAD_DIM]
        for head in range(1, columns // HEAD_DIM):
            folded = folded + gram[:, head * HEAD_DIM : (head + 1) * HEAD_DIM]
        packed.append(folded)
    hpart[columns:, :] = jnp.zeros((hpart.shape[0] - columns, 2 * HEAD_DIM), jnp.float32)
    hpart[:columns, :] = jnp.concatenate(packed, axis=1)
    one = x + core * (z - x)
    two = z + core * (x - z)
    first = [device(x + k * (1 - core), y, z + k * core, core) for k in (1, 2, 3)]
    second = [device(x + k * core, y, z + k * (1 - core), core) for k in (1, 2, 3)]
    n_one, n_two, n_three = part.shape[0] // 4, part.shape[0] // 16, part.shape[0] // 64
    h_one, h_two = hpart.shape[0] // 4, hpart.shape[0] // 16

    copies = []
    for k in range(3):
        to = (one + k + 1) % 4
        copies.append(send(part.at[rows(to * n_one, n_one)], r_one.at[k], sems, 14 + k, first[k]))
        copies.append(send(hpart.at[rows(to * h_one, h_one)], hr_one.at[k], sems, 17 + k, first[k]))
    for copy in copies:
        copy.wait()
    base = one * n_one
    hbase = one * h_one
    part[rows(base, n_one), :] += (r_one[0] + r_one[1]) + r_one[2]
    hpart[rows(hbase, h_one), :] += (hr_one[0] + hr_one[1]) + hr_one[2]
    copies = []
    for k in range(3):
        to = (two + k + 1) % 4
        copies.append(
            send(part.at[rows(base + to * n_two, n_two)], r_two.at[k], sems, 20 + k, second[k])
        )
        copies.append(
            send(hpart.at[rows(hbase + to * h_two, h_two)], hr_two.at[k], sems, 23 + k, second[k])
        )
    for copy in copies:
        copy.wait()
    base2 = base + two * n_two
    hbase2 = hbase + two * h_two
    part[rows(base2, n_two), :] += (r_two[0] + r_two[1]) + r_two[2]
    hgram_out[rows(hbase2, h_two), :] = (
        hpart[rows(hbase2, h_two), :] + (hr_two[0] + hr_two[1]) + hr_two[2]
    )
    copies = []
    for k in range(3):
        to = (y + k + 1) % 4
        copies.append(
            send(part.at[rows(base2 + to * n_three, n_three)], r_three.at[k], sems, 26 + k, along["y"][k])
        )
    for copy in copies:
        copy.wait()
    base3 = base2 + y * n_three
    gram_out[rows(base3, n_three), :] = (
        part[rows(base3, n_three), :] + (r_three[0] + r_three[1]) + r_three[2]
    )
    number = 29
    for others, start, count, hstart, hcount in (
        (along["y"], base3, n_three, None, None),
        (second, base2, n_two, hbase2, h_two),
        (first, base, n_one, hbase, h_one),
    ):
        copies = []
        for k in range(3):
            region = gram_out.at[rows(start, count)]
            copies.append(send(region, region, sems, number + k, others[k]))
            if hstart is not None:
                region = hgram_out.at[rows(hstart, hcount)]
                copies.append(send(region, region, sems, number + 3 + k, others[k]))
        for copy in copies:
            copy.wait()
        number += 3 if hstart is None else 6


def sum_over_devices(g_ffn, g_heads, m_ffn, m_heads, small):
    f32 = jnp.float32
    cols = g_heads.shape[2]
    vmem = pl.BlockSpec(memory_space=pltpu.VMEM)
    return pl.pallas_call(
        sum_kernel,
        out_shape=[
            jax.ShapeDtypeStruct((16, D), f32),
            jax.ShapeDtypeStruct((6 * BLK, BLK), f32),
            jax.ShapeDtypeStruct((BLK, 2 * HEAD_DIM), f32),
            jax.ShapeDtypeStruct((PAIR, D), f32),
            jax.ShapeDtypeStruct((2, PAIR, cols), f32),
        ],
        in_specs=[vmem] * 5,
        out_specs=[vmem] * 5,
        scratch_shapes=[
            pltpu.VMEM((SUB, D), f32),
            pltpu.VMEM((SUB, D), f32),
            pltpu.VMEM((2, SUB, cols), f32),
            pltpu.VMEM((2, SUB, cols), f32),
            pltpu.VMEM((2, 16, D), f32),
            pltpu.VMEM((4, 16, D), f32),
            pltpu.VMEM((4, 16, D), f32),
            pltpu.VMEM((4, 16, D), f32),
            pltpu.VMEM((6 * BLK, BLK), f32),
            pltpu.VMEM((3, 6 * BLK // 4, BLK), f32),
            pltpu.VMEM((3, 6 * BLK // 16, BLK), f32),
            pltpu.VMEM((3, 6 * BLK // 64, BLK), f32),
            pltpu.VMEM((BLK, 2 * HEAD_DIM), f32),
            pltpu.VMEM((3, BLK // 4, 2 * HEAD_DIM), f32),
            pltpu.VMEM((3, BLK // 16, 2 * HEAD_DIM), f32),
            pltpu.SemaphoreType.DMA((48,)),
            pltpu.SemaphoreType.DMA((48,)),
        ],
        name="sum_grams",
        compiler_params=pltpu.CompilerParams(
            collective_id=0, has_side_effects=True, vmem_limit_bytes=48 * 2**20
        ),
    )(g_ffn, g_heads, m_ffn, m_heads, small)


def chain_kernel(gram_in, hgram_in, x_in, xh_in, x_out, xh_out, gram, high, low, next_high, next_low, iterate, hgram):
    def tile(i):
        return slice(i * BLK, (i + 1) * BLK)

    eye = (
        lax.broadcasted_iota(jnp.int32, (BLK, BLK), 0)
        == lax.broadcasted_iota(jnp.int32, (BLK, BLK), 1)
    ).astype(jnp.float32)
    trace = jnp.zeros((1, 1), jnp.float32)
    for number, (i, j) in enumerate(UPPER):
        block = gram_in[tile(number), :]
        gram[tile(i), tile(j)] = block
        if i == j:
            trace = trace + jnp.sum(block * eye, axis=(0, 1), keepdims=True)
        else:
            gram[tile(j), tile(i)] = block.T
    scale = 1.0 / (jnp.sqrt(trace) + NS_EPS)
    gram[...] = gram[...] * (scale * scale)
    iterate[...] = x_in[...] * scale
    cols = xh_in.shape[2]
    h_rows = lax.broadcasted_iota(jnp.int32, (cols, cols), 0)
    h_cols = lax.broadcasted_iota(jnp.int32, (cols, cols), 1)
    same = h_rows // HEAD_DIM == h_cols // HEAD_DIM
    h_eye = (h_rows == h_cols).astype(jnp.float32)
    for kind in range(2):
        folded = hgram_in[:cols, kind * HEAD_DIM : (kind + 1) * HEAD_DIM]
        full = jnp.where(same, jnp.concatenate([folded] * (cols // HEAD_DIM), axis=1), 0.0)
        on_diagonal = full * h_eye
        by_column = jnp.sum(on_diagonal, axis=0, keepdims=True)
        by_row = jnp.sum(on_diagonal, axis=1, keepdims=True)
        trace_row = jnp.sum(jnp.where(same, by_column, 0.0), axis=1, keepdims=True)
        trace_column = jnp.sum(jnp.where(same, by_row, 0.0), axis=0, keepdims=True)
        scale_column = 1.0 / (jnp.sqrt(trace_column) + NS_EPS)
        scale_row = 1.0 / (jnp.sqrt(trace_row) + NS_EPS)
        hgram[kind] = full * scale_row * scale_column
        xh_out[kind] = xh_in[kind] * scale_column

    def sweep_heads(last):
        for kind in range(2):
            current = hgram[kind]
            pieces = split(current)
            poly = COEF_A * h_eye + COEF_B * current + COEF_C * product(pieces, pieces)
            poly_pieces = split(poly)
            xh_out[kind] = product(split(xh_out[kind]), poly_pieces)
            if not last:
                hgram[kind] = product(split(product(pieces, poly_pieces)), poly_pieces)

    def sweep(last):
        current = gram[...]
        high[...], low[...] = split(current)
        for i in range(3):
            squared = product((high[tile(i), :], low[tile(i), :]), (high[...], low[...]))
            poly = COEF_B * gram[tile(i), :] + COEF_C * squared
            next_high[tile(i), :], next_low[tile(i), :] = split(
                poly
                + COEF_A
                * jnp.concatenate(
                    [eye if k == i else jnp.zeros((BLK, BLK), jnp.float32) for k in range(3)], axis=1
                )
            )
        factor = (next_high[...], next_low[...])
        iterate[...] = product(split(iterate[...]), factor)
        if not last:
            for i in range(3):
                half = product((high[tile(i), :], low[tile(i), :]), factor)
                gram[tile(i), :] = product(split(half), factor)
        sweep_heads(last)

    def body(_, carry):
        sweep(False)
        return carry

    lax.fori_loop(0, NS_ITERS - 1, body, 0)
    sweep(True)
    x_out[...] = iterate[...]


def chain(gram, hgram, iterate, head_iterate):
    f32, b16 = jnp.float32, jnp.bfloat16
    cols = head_iterate.shape[2]
    vmem = pl.BlockSpec(memory_space=pltpu.VMEM)
    return pl.pallas_call(
        chain_kernel,
        out_shape=[
            jax.ShapeDtypeStruct(iterate.shape, f32),
            jax.ShapeDtypeStruct(head_iterate.shape, f32),
        ],
        in_specs=[vmem] * 4,
        out_specs=[vmem] * 2,
        scratch_shapes=[
            pltpu.VMEM((D, D), f32),
            pltpu.VMEM((D, D), b16),
            pltpu.VMEM((D, D), b16),
            pltpu.VMEM((D, D), b16),
            pltpu.VMEM((D, D), b16),
            pltpu.VMEM(iterate.shape, f32),
            pltpu.VMEM((2, cols, cols), f32),
        ],
        name="chain",
        compiler_params=pltpu.CompilerParams(vmem_limit_bytes=48 * 2**20),
    )(gram, hgram, iterate, head_iterate)


def swap_kernel(o_ffn, o_heads, ffn_out, heads_out, send_sem, recv_sem):
    x, y, z, core = place()
    sems = (send_sem, recv_sem)
    sibling = device(x, y, z, 1 - core)
    greet([sibling])
    copies = [
        send(o_ffn.at[rows((1 - core) * SUB, SUB)], ffn_out.at[core], sems, 0, sibling)
    ]
    for kind in range(2):
        copies.append(
            send(
                o_heads.at[kind, rows((1 - core) * SUB, SUB)],
                heads_out.at[2 * core + kind],
                sems,
                1 + kind,
                sibling,
            )
        )
    ffn_out[core] = o_ffn[rows(core * SUB, SUB), :]
    for kind in range(2):
        heads_out[2 * core + kind] = o_heads[kind, rows(core * SUB, SUB), :]
    for copy in copies:
        copy.wait()


def swap(o_ffn, o_heads):
    vmem = pl.BlockSpec(memory_space=pltpu.VMEM)
    cols = o_heads.shape[2]
    return pl.pallas_call(
        swap_kernel,
        out_shape=[
            jax.ShapeDtypeStruct((2, SUB, D), jnp.float32),
            jax.ShapeDtypeStruct((4, SUB, cols), jnp.float32),
        ],
        in_specs=[vmem] * 2,
        out_specs=[vmem] * 2,
        scratch_shapes=[pltpu.SemaphoreType.DMA((3,)), pltpu.SemaphoreType.DMA((3,))],
        name="swap",
        compiler_params=pltpu.CompilerParams(collective_id=1, has_side_effects=True),
    )(o_ffn, o_heads)


def adam_step(weight, gradient, moment_one, moment_two):
    first_new = BETA_ONE * moment_one + (1.0 - BETA_ONE) * gradient
    second_new = BETA_TWO * moment_two + (1.0 - BETA_TWO) * gradient * gradient
    stepped = (
        first_new
        / (1.0 - BETA_ONE**STEP)
        / (jnp.sqrt(second_new / (1.0 - BETA_TWO**STEP)) + ADAM_EPS)
    )
    return (first_new, second_new, weight - ADAM_RATE * stepped)


def per_device(
    tokens,
    lengths,
    cotangent,
    gains,
    conv,
    w_qkv,
    w_out,
    ffn_weights,
    mom_qkv,
    mom_out,
    mom_ffn,
    gain_first,
    gain_second,
    conv_first,
    conv_second,
):
    heads_axis = lax.axis_size("head")
    head_at = lax.axis_index("head")
    seq_here, rows_here, width = tokens.shape
    seq_length = rows_here * heads_axis
    cols_here = w_qkv.shape[2]
    heads_local = cols_here // HEAD_DIM
    positions = head_at * rows_here + jnp.arange(rows_here)
    real_rows = (positions[None, :] < lengths[:, None]).astype(jnp.float32)[:, :, None]
    kernel = lax.dynamic_slice_in_dim(conv, head_at * cols_here, cols_here, 2)
    query_key_value_lower, output_lower_rows, ffn_low = (
        lax.all_gather(w_qkv.astype(jnp.bfloat16), "dp", axis=1, tiled=True),
        lax.all_gather(w_out.astype(jnp.bfloat16), "dp", axis=1, tiled=True),
        lax.all_gather(ffn_weights.astype(jnp.bfloat16), "dp", axis=1, tiled=True),
    )
    resid_in = tokens.astype(jnp.float32)
    unit_one, inverse_one, normed_one = norm_parts(resid_in, gains[0])
    normalized_every_row = lax.all_gather(normed_one, "head", axis=1, tiled=True)
    projected_rows = jnp.einsum(
        "vru,jua->jvra",
        normalized_every_row,
        query_key_value_lower,
        preferred_element_type=jnp.float32,
    )
    streams = conv_forward(projected_rows, kernel).astype(jnp.bfloat16)
    shaped = streams.reshape(3, seq_here, seq_length, heads_local, HEAD_DIM)

    def forward_one(bundle):
        return attend_forward(bundle[0], bundle[1], bundle[2], bundle[3])

    attended, maxima, totals = lax.map(forward_one, (shaped[0], shaped[1], shaped[2], lengths))
    attended_lower_rows = attended.reshape(seq_here, seq_length, cols_here).astype(jnp.bfloat16)
    projection_portion = jnp.einsum(
        "azp,pm->azm", attended_lower_rows, output_lower_rows, preferred_element_type=jnp.float32
    )
    attn_rows = lax.psum_scatter(projection_portion, "head", scatter_dimension=1, tiled=True)
    middle = resid_in + attn_rows
    unit_two, inverse_two, normed_two = norm_parts(middle, gains[1])
    upstream = cotangent.astype(jnp.float32) * real_rows
    upstream_lower_rows = upstream.astype(jnp.bfloat16)
    normed_wide = lax.all_gather(normed_two, "head", axis=1, tiled=True)
    hidden_state_rows, relu_active_rows, ffn_part = ffn_forward(normed_wide, ffn_low)
    ffn_rows_out = lax.psum_scatter(
        ffn_part.astype(jnp.bfloat16), "head", scatter_dimension=1, tiled=True
    ).astype(jnp.float32)
    output = middle + ffn_rows_out
    upstream_wide = lax.all_gather(upstream_lower_rows, "head", axis=1, tiled=True)
    grad_normed_part, ffn_grad = ffn_back(
        normed_wide, ffn_low, hidden_state_rows, relu_active_rows, upstream_wide
    )
    grad_normed_two = lax.psum_scatter(grad_normed_part, "head", scatter_dimension=1, tiled=True)
    grad_norm_two, gain_two_grad = norm_back(grad_normed_two, unit_two, inverse_two, gains[1])
    grad_middle = upstream + grad_norm_two
    attention_wide_gradient = lax.all_gather(
        grad_middle.astype(jnp.bfloat16), "head", axis=1, tiled=True
    )
    out_grad = jnp.einsum(
        "tzu,tzx->ux",
        attended_lower_rows,
        attention_wide_gradient,
        preferred_element_type=jnp.float32,
    )
    grad_attended = jnp.einsum(
        "kmh,uh->kmu",
        attention_wide_gradient,
        output_lower_rows,
        preferred_element_type=jnp.float32,
    ).astype(jnp.bfloat16)
    grad_shaped = grad_attended.reshape(seq_here, seq_length, heads_local, HEAD_DIM)

    def back_one(bundle):
        return attend_back(
            bundle[0], bundle[1], bundle[2], bundle[3], bundle[4], bundle[5], bundle[6]
        )

    query_grad, key_grad, value_grad = lax.map(
        back_one, (shaped[0], shaped[1], shaped[2], lengths, maxima, totals, grad_shaped)
    )
    grad_streams = (
        jnp.stack([query_grad, key_grad, value_grad])
        .reshape(3, seq_here, seq_length, cols_here)
        .astype(jnp.bfloat16)
    )
    grad_projected, kernel_grad = conv_back(grad_streams, projected_rows, kernel)
    projected_lower_gradient = grad_projected.astype(jnp.bfloat16)
    qkv_grad = jnp.einsum(
        "uvm,buvh->bmh",
        normalized_every_row,
        projected_lower_gradient,
        preferred_element_type=jnp.float32,
    )
    grad_normed_part_one = jnp.einsum(
        "rptv,rov->pto",
        projected_lower_gradient,
        query_key_value_lower,
        preferred_element_type=jnp.float32,
    )
    grad_normed_one = lax.psum_scatter(
        grad_normed_part_one.astype(jnp.bfloat16), "head", scatter_dimension=1, tiled=True
    ).astype(jnp.float32)
    grad_norm_one, gain_one_grad = norm_back(grad_normed_one, unit_one, inverse_one, gains[0])
    input_grad = grad_middle + grad_norm_one
    qkv_part, out_part, ffn_part_grad = (
        lax.psum_scatter(
            qkv_grad.astype(jnp.bfloat16), "dp", scatter_dimension=1, tiled=True
        ).astype(jnp.float32),
        lax.psum_scatter(
            out_grad.astype(jnp.bfloat16), "dp", scatter_dimension=1, tiled=True
        ).astype(jnp.float32),
        lax.psum_scatter(
            ffn_grad.astype(jnp.bfloat16), "dp", scatter_dimension=1, tiled=True
        ).astype(jnp.float32),
    )
    conv_placed = lax.dynamic_update_slice_in_dim(
        jnp.zeros(conv.shape, jnp.float32), kernel_grad, head_at * cols_here, 2
    )
    small = jnp.concatenate(
        [
            jnp.stack([gain_one_grad, gain_two_grad]),
            conv_placed.reshape(KW * 3, D),
            jnp.zeros((5, D), jnp.float32),
        ]
    )
    heads_grad = jnp.concatenate([qkv_part, out_part.T[None]])
    heads_mom = jnp.concatenate([mom_qkv, mom_out.T[None]])
    small_sum, gram, hgram, iterate, head_iterate = sum_over_devices(
        ffn_part_grad, heads_grad, mom_ffn, heads_mom, small
    )
    gain_sum = small_sum[:2]
    conv_sum = small_sum[2:11].reshape(conv.shape)
    grad_norm = jnp.sqrt(jnp.sum(small_sum[:11] * small_sum[:11]) + jnp.sum(small_sum[11]))
    factor = CLIP_NORM / jnp.maximum(grad_norm, CLIP_NORM)
    grad_gains = gain_sum * factor
    grad_conv = conv_sum * factor
    grad_qkv = qkv_part * factor
    grad_out = out_part * factor
    grad_ffn = ffn_part_grad * factor
    new_mom_qkv = MOMENTUM * mom_qkv + grad_qkv
    new_mom_out = MOMENTUM * mom_out + grad_out
    new_mom_ffn = MOMENTUM * mom_ffn + grad_ffn
    ffn_orth, heads_orth = swap(*chain(gram, hgram, iterate, head_iterate))
    new_qkv = w_qkv - RATE_IN * math.sqrt(D) * heads_orth[:3]
    new_out = w_out - RATE_OUT * math.sqrt(D) * heads_orth[3].T
    new_ffn = ffn_weights - RATE_IN * math.sqrt(max(FF, D)) * ffn_orth
    new_gain_first, new_gain_second, new_gains = adam_step(
        gains, grad_gains, gain_first, gain_second
    )
    new_conv_first, new_conv_second, new_conv = adam_step(conv, grad_conv, conv_first, conv_second)
    return (
        output,
        input_grad,
        grad_gains,
        grad_conv,
        grad_qkv,
        grad_out,
        grad_ffn,
        grad_norm,
        new_mom_qkv,
        new_mom_out,
        new_mom_ffn,
        new_gain_first,
        new_gain_second,
        new_conv_first,
        new_conv_second,
        new_gains,
        new_conv,
        new_qkv,
        new_out,
        new_ffn,
    )


def solution(mesh):
    placed = (
        P("dp", "head", None),
        P("dp"),
        P("dp", "head", None),
        P(),
        P(),
        P(None, "dp", "head"),
        P("head", "dp"),
        P(None, ("head", "dp"), None),
        P(None, "dp", "head"),
        P("head", "dp"),
        P(None, ("head", "dp"), None),
        P(),
        P(),
        P(),
        P(),
    )
    return jax.shard_map(
        per_device,
        mesh=mesh,
        in_specs=placed,
        out_specs=(
            P("dp", "head", None),
            P("dp", "head", None),
            P(),
            P(),
            P(None, "dp", "head"),
            P("head", "dp"),
            P(None, ("head", "dp"), None),
            P(),
            P(None, "dp", "head"),
            P("head", "dp"),
            P(None, ("head", "dp"), None),
            P(),
            P(),
            P(),
            P(),
            P(),
            P(),
            P(None, "dp", "head"),
            P("head", "dp"),
            P(None, ("head", "dp"), None),
        ),
        check_vma=False,
    )
```

```python
import math

import jax
import jax.numpy as jnp
from jax import lax
from jax.experimental import pallas as pl
from jax.experimental.pallas import tpu as pltpu
from jax.sharding import PartitionSpec as P

D = 768
HEADS = 12
HEAD_DIM = 64
FF = 3072
KW = 3
NS_ITERS = 5
STEP = 10


NORM_EPS = 1e-06
NEG_FILL = -1e30
CLIP_NORM = 1.0
MOMENTUM = 0.95
RATE_IN = 0.02
RATE_OUT = 0.15
ADAM_RATE = 0.5
BETA_ONE = 0.9
BETA_TWO = 0.999
ADAM_EPS = 1e-08
NS_EPS = 1e-07
COEF_A = 3.4445
COEF_B = -4.775
COEF_C = 2.0315
PRECISE = lax.Precision.HIGHEST


SUB = 24
PAIR = 2 * SUB
BLK = 256
MESH_IDS = pl.DeviceIdType.MESH


def place():
    flat = lax.axis_index("dp")
    return flat // 8, lax.axis_index("head"), (flat // 2) % 4, flat % 2


def device(x, y, z, core):
    return (y % 4, ((x % 4) * 4 + z % 4) * 2 + core)


def greet(others):
    barrier = pltpu.get_barrier_semaphore()
    for other in others:
        pl.semaphore_signal(barrier, inc=1, device_id=other, device_id_type=MESH_IDS)
    pl.semaphore_wait(barrier, len(others))


def send(source, target, sems, index, other):
    copy = pltpu.make_async_remote_copy(
        src_ref=source,
        dst_ref=target,
        send_sem=sems[0].at[index],
        recv_sem=sems[1].at[index],
        device_id=other,
        device_id_type=MESH_IDS,
    )
    copy.start()
    return copy


def rows(start, count):
    return pl.ds(pl.multiple_of(start, 8), count)


def split(values):
    high = values.astype(jnp.bfloat16)
    return high, (values - high.astype(jnp.float32)).astype(jnp.bfloat16)


def product(left, right, dims=(((1,), (0,)), ((), ()))):
    lh, ll = left
    rh, rl = right

    def dot(a, b):
        return lax.dot_general(a, b, dims, preferred_element_type=jnp.float32)

    return dot(lh, rh) + (dot(lh, rl) + dot(ll, rh))


UPPER = ((0, 0), (0, 1), (0, 2), (1, 1), (1, 2), (2, 2))


def sum_kernel(
    g_pair, g_heads, m_ffn, m_heads, small,
    small_out, gram_out, hgram_out, x_out, xh_out, g_out,
    min_, mhin, s_core, s_x, s_z, s_y, part, r_one, r_two, r_three, hpart, hr_one, hr_two,
    send_sem, recv_sem,
):
    x, y, z, core = place()
    sems = (send_sem, recv_sem)
    sibling = device(x, y, z, 1 - core)
    along = {
        "x": [device(x + k, y, z, core) for k in (1, 2, 3)],
        "z": [device(x, y, z + k, core) for k in (1, 2, 3)],
        "y": [device(x, y + k, z, core) for k in (1, 2, 3)],
    }
    greet([sibling] + along["x"] + along["z"] + along["y"])
    swaps = [
        send(g_pair.at[rows((1 - core) * SUB, SUB)], g_out.at[core], sems, 0, sibling),
        send(m_ffn.at[1 - core], min_, sems, 1, sibling),
        send(m_heads.at[pl.ds(2 - 2 * core, 2)], mhin, sems, 3, sibling),
    ]
    g_out[core] = g_pair[rows(core * SUB, SUB), :]
    mine = g_heads[pl.ds(2 * core, 2)]
    lanes_ffn = jnp.sum(g_pair[...] * g_pair[...], axis=0)
    lanes_heads = jnp.sum(mine * mine, axis=(0, 1))
    own = small[...]
    row_ids = lax.broadcasted_iota(jnp.int32, own.shape, 0)
    wide = jnp.concatenate([lanes_heads, jnp.zeros((D - lanes_heads.shape[0],), jnp.float32)])
    own = own + jnp.where(row_ids == 11, lanes_ffn[None, :] + wide[None, :], 0.0)
    number = 4
    s_core[core] = own
    copy = send(s_core.at[core], s_core.at[core], sems, number, sibling)
    copy.wait()
    total = s_core[0] + s_core[1]
    number = 5
    for slots, axis, here in ((s_x, "x", x), (s_z, "z", z), (s_y, "y", y)):
        slots[here] = total
        copies = [
            send(slots.at[here], slots.at[here], sems, number + k, along[axis][k]) for k in range(3)
        ]
        for copy in copies:
            copy.wait()
        total = (slots[0] + slots[1]) + (slots[2] + slots[3])
        number += 3
    small_out[...] = total
    squared = jnp.sum(jnp.where(row_ids < 11, total * total, total), axis=(0, 1), keepdims=True)
    factor = CLIP_NORM / jnp.maximum(jnp.sqrt(squared), CLIP_NORM)
    for copy in swaps:
        copy.wait()
    for place_of, momentum in ((core, m_ffn[core]), (1 - core, min_[...])):
        at = rows(place_of * SUB, SUB)
        x_out[at, :] = MOMENTUM * momentum + factor * g_pair[at, :]
    for kind in range(2):
        for place_of, momentum in ((core, m_heads[2 * core + kind]), (1 - core, mhin[kind])):
            at = rows(place_of * SUB, SUB)
            xh_out[kind, at, :] = MOMENTUM * momentum + factor * g_heads[2 * core + kind, at, :]
    transposed = (((0,), (0,)), ((), ()))
    for number_of, (i, j) in enumerate(UPPER):
        part[number_of * BLK : (number_of + 1) * BLK, :] = product(
            split(x_out[:, i * BLK : (i + 1) * BLK]),
            split(x_out[:, j * BLK : (j + 1) * BLK]),
            transposed,
        )
    columns = xh_out.shape[2]
    r_ids = lax.broadcasted_iota(jnp.int32, (columns, columns), 0) // HEAD_DIM
    c_ids = lax.broadcasted_iota(jnp.int32, (columns, columns), 1) // HEAD_DIM
    packed = []
    for kind in range(2):
        pieces = split(xh_out[kind])
        gram = jnp.where(r_ids == c_ids, product(pieces, pieces, transposed), 0.0)
        folded = gram[:, :HEAD_DIM]
        for head in range(1, columns // HEAD_DIM):
            folded = folded + gram[:, head * HEAD_DIM : (head + 1) * HEAD_DIM]
        packed.append(folded)
    hpart[columns:, :] = jnp.zeros((hpart.shape[0] - columns, 2 * HEAD_DIM), jnp.float32)
    hpart[:columns, :] = jnp.concatenate(packed, axis=1)
    one = x + core * (z - x)
    two = z + core * (x - z)
    first = [device(x + k * (1 - core), y, z + k * core, core) for k in (1, 2, 3)]
    second = [device(x + k * core, y, z + k * (1 - core), core) for k in (1, 2, 3)]
    n_one, n_two, n_three = part.shape[0] // 4, part.shape[0] // 16, part.shape[0] // 64
    h_one, h_two = hpart.shape[0] // 4, hpart.shape[0] // 16

    copies = []
    for k in range(3):
        to = (one + k + 1) % 4
        copies.append(send(part.at[rows(to * n_one, n_one)], r_one.at[k], sems, 14 + k, first[k]))
        copies.append(send(hpart.at[rows(to * h_one, h_one)], hr_one.at[k], sems, 17 + k, first[k]))
    for copy in copies:
        copy.wait()
    base = one * n_one
    hbase = one * h_one
    part[rows(base, n_one), :] += (r_one[0] + r_one[1]) + r_one[2]
    hpart[rows(hbase, h_one), :] += (hr_one[0] + hr_one[1]) + hr_one[2]
    copies = []
    for k in range(3):
        to = (two + k + 1) % 4
        copies.append(
            send(part.at[rows(base + to * n_two, n_two)], r_two.at[k], sems, 20 + k, second[k])
        )
        copies.append(
            send(hpart.at[rows(hbase + to * h_two, h_two)], hr_two.at[k], sems, 23 + k, second[k])
        )
    for copy in copies:
        copy.wait()
    base2 = base + two * n_two
    hbase2 = hbase + two * h_two
    part[rows(base2, n_two), :] += (r_two[0] + r_two[1]) + r_two[2]
    hgram_out[rows(hbase2, h_two), :] = (
        hpart[rows(hbase2, h_two), :] + (hr_two[0] + hr_two[1]) + hr_two[2]
    )
    copies = []
    for k in range(3):
        to = (y + k + 1) % 4
        copies.append(
            send(part.at[rows(base2 + to * n_three, n_three)], r_three.at[k], sems, 26 + k, along["y"][k])
        )
    for copy in copies:
        copy.wait()
    base3 = base2 + y * n_three
    gram_out[rows(base3, n_three), :] = (
        part[rows(base3, n_three), :] + (r_three[0] + r_three[1]) + r_three[2]
    )
    number = 29
    for others, start, count, hstart, hcount in (
        (along["y"], base3, n_three, None, None),
        (second, base2, n_two, hbase2, h_two),
        (first, base, n_one, hbase, h_one),
    ):
        copies = []
        for k in range(3):
            region = gram_out.at[rows(start, count)]
            copies.append(send(region, region, sems, number + k, others[k]))
            if hstart is not None:
                region = hgram_out.at[rows(hstart, hcount)]
                copies.append(send(region, region, sems, number + 3 + k, others[k]))
        for copy in copies:
            copy.wait()
        number += 3 if hstart is None else 6


def sum_over_devices(g_pair, g_heads, m_ffn, m_heads, small):
    f32 = jnp.float32
    cols = g_heads.shape[2]
    vmem = pl.BlockSpec(memory_space=pltpu.VMEM)
    return pl.pallas_call(
        sum_kernel,
        out_shape=[
            jax.ShapeDtypeStruct((16, D), f32),
            jax.ShapeDtypeStruct((6 * BLK, BLK), f32),
            jax.ShapeDtypeStruct((BLK, 2 * HEAD_DIM), f32),
            jax.ShapeDtypeStruct((PAIR, D), f32),
            jax.ShapeDtypeStruct((2, PAIR, cols), f32),
            jax.ShapeDtypeStruct((2, SUB, D), f32),
        ],
        in_specs=[vmem] * 5,
        out_specs=[vmem] * 6,
        scratch_shapes=[
            pltpu.VMEM((SUB, D), f32),
            pltpu.VMEM((2, SUB, cols), f32),
            pltpu.VMEM((2, 16, D), f32),
            pltpu.VMEM((4, 16, D), f32),
            pltpu.VMEM((4, 16, D), f32),
            pltpu.VMEM((4, 16, D), f32),
            pltpu.VMEM((6 * BLK, BLK), f32),
            pltpu.VMEM((3, 6 * BLK // 4, BLK), f32),
            pltpu.VMEM((3, 6 * BLK // 16, BLK), f32),
            pltpu.VMEM((3, 6 * BLK // 64, BLK), f32),
            pltpu.VMEM((BLK, 2 * HEAD_DIM), f32),
            pltpu.VMEM((3, BLK // 4, 2 * HEAD_DIM), f32),
            pltpu.VMEM((3, BLK // 16, 2 * HEAD_DIM), f32),
            pltpu.SemaphoreType.DMA((48,)),
            pltpu.SemaphoreType.DMA((48,)),
        ],
        name="sum_grams",
        compiler_params=pltpu.CompilerParams(
            collective_id=0, has_side_effects=True, vmem_limit_bytes=48 * 2**20
        ),
    )(g_pair, g_heads, m_ffn, m_heads, small)


def chain_kernel(gram_in, hgram_in, x_in, xh_in, x_out, xh_out, gram, high, low, next_high, next_low, iterate, hgram):
    def tile(i):
        return slice(i * BLK, (i + 1) * BLK)

    eye = (
        lax.broadcasted_iota(jnp.int32, (BLK, BLK), 0)
        == lax.broadcasted_iota(jnp.int32, (BLK, BLK), 1)
    ).astype(jnp.float32)
    trace = jnp.zeros((1, 1), jnp.float32)
    for number, (i, j) in enumerate(UPPER):
        block = gram_in[tile(number), :]
        gram[tile(i), tile(j)] = block
        if i == j:
            trace = trace + jnp.sum(block * eye, axis=(0, 1), keepdims=True)
        else:
            gram[tile(j), tile(i)] = block.T
    scale = 1.0 / (jnp.sqrt(trace) + NS_EPS)
    gram[...] = gram[...] * (scale * scale)
    iterate[...] = x_in[...] * scale
    cols = xh_in.shape[2]
    h_rows = lax.broadcasted_iota(jnp.int32, (cols, cols), 0)
    h_cols = lax.broadcasted_iota(jnp.int32, (cols, cols), 1)
    same = h_rows // HEAD_DIM == h_cols // HEAD_DIM
    h_eye = (h_rows == h_cols).astype(jnp.float32)
    for kind in range(2):
        folded = hgram_in[:cols, kind * HEAD_DIM : (kind + 1) * HEAD_DIM]
        full = jnp.where(same, jnp.concatenate([folded] * (cols // HEAD_DIM), axis=1), 0.0)
        on_diagonal = full * h_eye
        by_column = jnp.sum(on_diagonal, axis=0, keepdims=True)
        by_row = jnp.sum(on_diagonal, axis=1, keepdims=True)
        trace_row = jnp.sum(jnp.where(same, by_column, 0.0), axis=1, keepdims=True)
        trace_column = jnp.sum(jnp.where(same, by_row, 0.0), axis=0, keepdims=True)
        scale_column = 1.0 / (jnp.sqrt(trace_column) + NS_EPS)
        scale_row = 1.0 / (jnp.sqrt(trace_row) + NS_EPS)
        hgram[kind] = full * scale_row * scale_column
        xh_out[kind] = xh_in[kind] * scale_column

    def sweep_heads(last):
        for kind in range(2):
            current = hgram[kind]
            pieces = split(current)
            poly = COEF_A * h_eye + COEF_B * current + COEF_C * product(pieces, pieces)
            poly_pieces = split(poly)
            xh_out[kind] = product(split(xh_out[kind]), poly_pieces)
            if not last:
                hgram[kind] = product(split(product(pieces, poly_pieces)), poly_pieces)

    def sweep(last):
        current = gram[...]
        high[...], low[...] = split(current)
        for i in range(3):
            squared = product((high[tile(i), :], low[tile(i), :]), (high[...], low[...]))
            poly = COEF_B * gram[tile(i), :] + COEF_C * squared
            next_high[tile(i), :], next_low[tile(i), :] = split(
                poly
                + COEF_A
                * jnp.concatenate(
                    [eye if k == i else jnp.zeros((BLK, BLK), jnp.float32) for k in range(3)], axis=1
                )
            )
        factor = (next_high[...], next_low[...])
        iterate[...] = product(split(iterate[...]), factor)
        if not last:
            for i in range(3):
                half = product((high[tile(i), :], low[tile(i), :]), factor)
                gram[tile(i), :] = product(split(half), factor)
        sweep_heads(last)

    def body(_, carry):
        sweep(False)
        return carry

    lax.fori_loop(0, NS_ITERS - 1, body, 0)
    sweep(True)
    x_out[...] = iterate[...]


def chain(gram, hgram, iterate, head_iterate):
    f32, b16 = jnp.float32, jnp.bfloat16
    cols = head_iterate.shape[2]
    vmem = pl.BlockSpec(memory_space=pltpu.VMEM)
    return pl.pallas_call(
        chain_kernel,
        out_shape=[
            jax.ShapeDtypeStruct(iterate.shape, f32),
            jax.ShapeDtypeStruct(head_iterate.shape, f32),
        ],
        in_specs=[vmem] * 4,
        out_specs=[vmem] * 2,
        scratch_shapes=[
            pltpu.VMEM((D, D), f32),
            pltpu.VMEM((D, D), b16),
            pltpu.VMEM((D, D), b16),
            pltpu.VMEM((D, D), b16),
            pltpu.VMEM((D, D), b16),
            pltpu.VMEM(iterate.shape, f32),
            pltpu.VMEM((2, cols, cols), f32),
        ],
        name="chain",
        compiler_params=pltpu.CompilerParams(vmem_limit_bytes=48 * 2**20),
    )(gram, hgram, iterate, head_iterate)


def swap_kernel(o_ffn, o_heads, ffn_out, heads_out, send_sem, recv_sem):
    x, y, z, core = place()
    sems = (send_sem, recv_sem)
    sibling = device(x, y, z, 1 - core)
    greet([sibling])
    copies = [
        send(o_ffn.at[rows((1 - core) * SUB, SUB)], ffn_out.at[core], sems, 0, sibling)
    ]
    for kind in range(2):
        copies.append(
            send(
                o_heads.at[kind, rows((1 - core) * SUB, SUB)],
                heads_out.at[2 * core + kind],
                sems,
                1 + kind,
                sibling,
            )
        )
    ffn_out[core] = o_ffn[rows(core * SUB, SUB), :]
    for kind in range(2):
        heads_out[2 * core + kind] = o_heads[kind, rows(core * SUB, SUB), :]
    for copy in copies:
        copy.wait()


def swap(o_ffn, o_heads):
    vmem = pl.BlockSpec(memory_space=pltpu.VMEM)
    cols = o_heads.shape[2]
    return pl.pallas_call(
        swap_kernel,
        out_shape=[
            jax.ShapeDtypeStruct((2, SUB, D), jnp.float32),
            jax.ShapeDtypeStruct((4, SUB, cols), jnp.float32),
        ],
        in_specs=[vmem] * 2,
        out_specs=[vmem] * 2,
        scratch_shapes=[pltpu.SemaphoreType.DMA((3,)), pltpu.SemaphoreType.DMA((3,))],
        name="swap",
        compiler_params=pltpu.CompilerParams(collective_id=1, has_side_effects=True),
    )(o_ffn, o_heads)


SEQ = 1024
QUARTER = SEQ // 4
GROUP = D // 4
GROUP_HEADS = GROUP // HEAD_DIM
SCALE = HEAD_DIM ** (-0.5)
NT = (((1,), (1,)), ((), ()))
TN = (((0,), (0,)), ((), ()))
NN = (((1,), (0,)), ((), ()))
PARTS = (("yzx", 0, 256), ("xyz", 256, 256), ("zxy", 512, 256))


def mul(a, b, dims=NN):
    return lax.dot_general(a, b, dims, preferred_element_type=jnp.float32)


def neighbours(x, y, z, core):
    return {
        "x": [device(x + k, y, z, core) for k in (1, 2, 3)],
        "y": [device(x, y + k, z, core) for k in (1, 2, 3)],
        "z": [device(x, y, z + k, core) for k in (1, 2, 3)],
    }


def cell(here, free, moved=None):
    moved = moved or {}
    return tuple(slice(None) if a in free else moved.get(a, here[a]) for a in "yxz")


class Counter:
    def __init__(self):
        self.count = 0

    def take(self):
        self.count += 1
        return self.count - 1


def wait_all(copies):
    for copy in copies:
        copy.wait()


def in_core_order(core, own, other):
    return jnp.concatenate(
        [jnp.where(core == 0, own, other), jnp.where(core == 0, other, own)], axis=-2
    )


def forward_kernel(
    length, tokens, gains, taps, w_heads, w_ffn,
    normed, streams, projected, lse, attended, w_all, wo_all, ffn_all,
    swap_heads, swap_ffn, ffn_own, att_send, send_sem, recv_sem, local_sem,
):
    x, y, z, core = place()
    here = {"x": x, "y": y, "z": z}
    sems = (send_sem, recv_sem)
    sibling = device(x, y, z, 1 - core)
    along = neighbours(x, y, z, core)
    count = Counter()

    def go(source, target, other):
        return send(source, target, sems, count.take(), other)

    greet([sibling] + along["x"] + along["y"] + along["z"])
    swaps = [
        go(w_heads, swap_heads, sibling),
        go(w_ffn.at[1 - core], swap_ffn, sibling),
    ]
    values = tokens[...].astype(jnp.float32)
    inverse = lax.rsqrt(jnp.mean(values * values, axis=-1, keepdims=True) + NORM_EPS)
    normed[y] = (values * inverse * gains[0:1]).astype(jnp.bfloat16)
    spread = [go(normed.at[y], normed.at[y], other) for other in along["y"]]
    wait_all(swaps)
    at_xz = x * 4 + z
    w_all[:, x, z] = in_core_order(core, w_heads[...], swap_heads[...]).astype(jnp.bfloat16)
    ffn_own[...] = in_core_order(core, w_ffn[core], swap_ffn[...]).astype(jnp.bfloat16)
    one = [device(x + k * (1 - core), y, z + k * core, core) for k in (1, 2, 3)]
    two = [device(x + k * core, y, z + k * (1 - core), core) for k in (1, 2, 3)]
    heads_one = [go(w_all.at[:, x, z], w_all.at[:, x, z], other) for other in one]
    kept = pltpu.make_async_copy(ffn_own, ffn_all.at[core, y, x, z], local_sem.at[0])
    kept.start()
    ffn_one = [
        go(ffn_own.at[:, c : c + w], ffn_all.at[core, y, x, z, :, c : c + w], other)
        for order, c, w in PARTS
        for other in along[order[0]]
    ]
    wait_all(heads_one)

    @pl.when(core == 0)
    def _():
        for k in range(3):
            pltpu.make_async_remote_copy(
                src_ref=w_all.at[:, :, z], dst_ref=w_all.at[:, :, z],
                send_sem=send_sem.at[60 + k], recv_sem=recv_sem.at[60 + k],
                device_id=along["z"][k], device_id_type=MESH_IDS,
            ).start()

    @pl.when(core == 1)
    def _():
        for k in range(3):
            pltpu.make_async_remote_copy(
                src_ref=w_all.at[:, x], dst_ref=w_all.at[:, x],
                send_sem=send_sem.at[60 + k], recv_sem=recv_sem.at[60 + k],
                device_id=along["x"][k], device_id_type=MESH_IDS,
            ).start()

    kept.wait()
    wait_all(ffn_one)
    ffn_two = []
    for order, c, w in PARTS:
        region = ffn_all.at[(core,) + cell(here, order[0]) + (slice(None), slice(c, c + w))]
        ffn_two += [go(region, region, other) for other in along[order[1]]]

    @pl.when(core == 0)
    def _():
        for k in range(3):
            pltpu.make_async_remote_copy(
                src_ref=w_all.at[:, :, z], dst_ref=w_all.at[:, :, z],
                send_sem=send_sem.at[60 + k], recv_sem=recv_sem.at[60 + k],
                device_id=along["z"][k], device_id_type=MESH_IDS,
            ).wait()

    @pl.when(core == 1)
    def _():
        for k in range(3):
            pltpu.make_async_remote_copy(
                src_ref=w_all.at[:, x], dst_ref=w_all.at[:, x],
                send_sem=send_sem.at[60 + k], recv_sem=recv_sem.at[60 + k],
                device_id=along["x"][k], device_id_type=MESH_IDS,
            ).wait()

    half = pl.ds(2 * core, 2)
    wo_y = [go(w_all.at[3, half], wo_all.at[y, half], other) for other in along["y"]]
    wo_all[y] = w_all[3]
    wait_all(spread)
    projected[:, 0:8, :] = jnp.zeros((3, 8, GROUP), jnp.float32)
    key_ids = lax.broadcasted_iota(jnp.int32, (SEQ, 1), 0)
    bias = jnp.where(key_ids < length[0], 0.0, NEG_FILL)
    upper = (
        lax.broadcasted_iota(jnp.int32, (QUARTER, QUARTER), 0)
        <= lax.broadcasted_iota(jnp.int32, (QUARTER, QUARTER), 1)
    )

    def project(i):
        rows_i = slice(i * QUARTER, (i + 1) * QUARTER)
        for kind in range(3):
            base = 8 + i * QUARTER
            projected[kind, base : base + QUARTER, :] = mul(
                normed[i], w_all[kind].reshape(D, GROUP)
            )
            summed = taps[0, kind : kind + 1] * projected[kind, base : base + QUARTER, :]
            for t in range(1, KW):
                summed = summed + taps[t, kind : kind + 1] * projected[
                    kind, base - t : base - t + QUARTER, :
                ]
            stream = summed.astype(jnp.bfloat16)
            if kind == 0:
                stream = stream * jnp.bfloat16(SCALE)
            for head in range(GROUP_HEADS):
                streams[kind * GROUP_HEADS + head, rows_i, :] = stream[
                    :, head * HEAD_DIM : (head + 1) * HEAD_DIM
                ]

    def attend(i):
        rows_i = slice(i * QUARTER, (i + 1) * QUARTER)
        keys = (i + 1) * QUARTER
        pieces = []
        for head in range(GROUP_HEADS):
            scores = mul(
                streams[GROUP_HEADS + head, :keys, :], streams[head, rows_i, :], NT
            ) + bias[:keys]
            corner = jnp.where(upper, scores[keys - QUARTER :], NEG_FILL)
            scores = corner if i == 0 else jnp.concatenate([scores[: keys - QUARTER], corner], 0)
            top = jnp.max(scores, axis=0, keepdims=True)
            lifted = jnp.exp(scores - top)
            total = jnp.sum(lifted, axis=0, keepdims=True)
            probs = (lifted * (1.0 / total)).astype(jnp.bfloat16)
            lse[head, :, rows_i] = top + jnp.log(total)
            pieces.append(mul(streams[2 * GROUP_HEADS + head, :keys, :], probs, TN).T)
        att_send[i] = jnp.concatenate(pieces, axis=1).astype(jnp.bfloat16)

    for i in range(4):
        project(i)
    attend(0)
    attend(1)
    wait_all(ffn_two)
    ffn_three = []
    for order, c, w in PARTS:
        region = ffn_all.at[(core,) + cell(here, order[:2]) + (slice(None), slice(c, c + w))]
        ffn_three += [go(region, region, other) for other in along[order[2]]]
    wait_all(wo_y)
    wo_pair = [
        go(wo_all.at[(y + k) % 4, half], wo_all.at[(y + k) % 4, half], sibling) for k in (1, 2, 3)
    ]
    attend(2)
    attend(3)
    heads_out = [
        go(att_send.at[(y + k) % 4], attended.at[y], along["y"][k - 1]) for k in (1, 2, 3)
    ]
    attended[y] = att_send[y]
    wait_all(ffn_three)
    ffn_pair = [
        go(ffn_all.at[core, quarter], ffn_all.at[core, quarter], sibling) for quarter in range(4)
    ]
    wait_all(wo_pair)
    wait_all(heads_out)
    wait_all(ffn_pair)


def forward(length, tokens, gains, taps, w_heads, w_ffn):
    f32, b16 = jnp.float32, jnp.bfloat16
    vmem = pl.BlockSpec(memory_space=pltpu.VMEM)
    return pl.pallas_call(
        forward_kernel,
        out_shape=[
            jax.ShapeDtypeStruct((4, QUARTER, D), b16),
            jax.ShapeDtypeStruct((3 * GROUP_HEADS, SEQ, HEAD_DIM), b16),
            jax.ShapeDtypeStruct((3, SEQ + 8, GROUP), f32),
            jax.ShapeDtypeStruct((GROUP_HEADS, 1, SEQ), f32),
            jax.ShapeDtypeStruct((4, QUARTER, GROUP), b16),
            jax.ShapeDtypeStruct((4, 4, 4, PAIR, GROUP), b16),
            jax.ShapeDtypeStruct((4, 4, 4, PAIR, GROUP), b16),
            jax.ShapeDtypeStruct((2, 4, 4, 4, PAIR, D), b16),
        ],
        in_specs=[pl.BlockSpec(memory_space=pltpu.SMEM)] + [vmem] * 5,
        out_specs=[vmem] * 7 + [pl.BlockSpec(memory_space=pl.ANY)],
        scratch_shapes=[
            pltpu.VMEM((4, SUB, GROUP), f32),
            pltpu.VMEM((SUB, D), f32),
            pltpu.VMEM((PAIR, D), b16),
            pltpu.VMEM((4, QUARTER, GROUP), b16),
            pltpu.SemaphoreType.DMA((64,)),
            pltpu.SemaphoreType.DMA((64,)),
            pltpu.SemaphoreType.DMA((1,)),
        ],
        name="attend_and_gather",
        compiler_params=pltpu.CompilerParams(
            collective_id=2, has_side_effects=True, vmem_limit_bytes=56 * 2**20
        ),
    )(length, tokens, gains, taps, w_heads, w_ffn)


def ffn_kernel(
    limit, tokens, cotangent, gains, attended, wo, weights,
    output, grad_middle, gain_two, grad_attended, raw_out, raw_ffn,
    middle, normed, upstream, out_sum, grad_sum,
):
    step = pl.program_id(0)

    @pl.when(step == 0)
    def _():
        mixed = mul(attended[0], wo[0], NT)
        for group in range(1, 4):
            mixed = mixed + mul(attended[group], wo[group], NT)
        rows_here = tokens[...].astype(jnp.float32) + mixed
        middle[...] = rows_here
        inverse = lax.rsqrt(jnp.mean(rows_here * rows_here, axis=-1, keepdims=True) + NORM_EPS)
        normed[...] = (rows_here * inverse * gains[1:2]).astype(jnp.bfloat16)
        real = lax.broadcasted_iota(jnp.int32, (QUARTER, 1), 0) < limit[0]
        upstream[...] = jnp.where(real, cotangent[...].astype(jnp.float32), 0.0).astype(jnp.bfloat16)
        out_sum[...] = jnp.zeros_like(out_sum)
        grad_sum[...] = jnp.zeros_like(grad_sum)

    into, back = weights[0], weights[1]
    positive = jnp.maximum(mul(normed[...], into, NT), 0.0)
    active = (positive * positive).astype(jnp.bfloat16)
    grad_hidden = (mul(upstream[...], back, NT) * (2.0 * positive)).astype(jnp.bfloat16)
    out_sum[...] += mul(active, back)
    grad_sum[...] += mul(grad_hidden, into)
    raw_ffn[0] = mul(grad_hidden, normed[...], TN).astype(jnp.bfloat16)
    raw_ffn[1] = mul(active, upstream[...], TN).astype(jnp.bfloat16)

    @pl.when(step == pl.num_programs(0) - 1)
    def _():
        rows_here = middle[...]
        output[...] = rows_here + out_sum[...]
        inverse = lax.rsqrt(jnp.mean(rows_here * rows_here, axis=-1, keepdims=True) + NORM_EPS)
        unit = rows_here * inverse
        grad = grad_sum[...]
        gain_two[...] = jnp.sum(grad * unit, axis=0, keepdims=True)
        scaled = grad * gains[1:2]
        inner = jnp.mean(scaled * unit, axis=-1, keepdims=True)
        real = lax.broadcasted_iota(jnp.int32, (QUARTER, 1), 0) < limit[0]
        grad_rows = jnp.where(real, cotangent[...].astype(jnp.float32), 0.0) + inverse * (
            scaled - unit * inner
        )
        grad_middle[...] = grad_rows
        lower = grad_rows.astype(jnp.bfloat16)
        for group in range(4):
            grad_attended[group] = mul(lower, wo[group]).astype(jnp.bfloat16)
            raw_out[group] = mul(lower, attended[group], TN).astype(jnp.bfloat16)


def feed_forward(limit, tokens, cotangent, gains, attended, wo, weights):
    f32, b16 = jnp.float32, jnp.bfloat16
    units = 512

    def whole(*shape):
        return pl.BlockSpec(shape, lambda i: (0,) * len(shape))

    return pl.pallas_call(
        ffn_kernel,
        grid=(FF // units,),
        out_shape=[
            jax.ShapeDtypeStruct((QUARTER, D), f32),
            jax.ShapeDtypeStruct((QUARTER, D), f32),
            jax.ShapeDtypeStruct((1, D), f32),
            jax.ShapeDtypeStruct((4, QUARTER, GROUP), b16),
            jax.ShapeDtypeStruct((4, D, GROUP), b16),
            jax.ShapeDtypeStruct((2, FF, D), b16),
        ],
        in_specs=[
            pl.BlockSpec(memory_space=pltpu.SMEM),
            whole(QUARTER, D),
            whole(QUARTER, D),
            whole(2, D),
            whole(4, QUARTER, GROUP),
            whole(4, D, GROUP),
            pl.BlockSpec((2, units, D), lambda i: (0, i, 0)),
        ],
        out_specs=[
            whole(QUARTER, D),
            whole(QUARTER, D),
            whole(1, D),
            whole(4, QUARTER, GROUP),
            whole(4, D, GROUP),
            pl.BlockSpec((2, units, D), lambda i: (0, i, 0)),
        ],
        scratch_shapes=[
            pltpu.VMEM((QUARTER, D), f32),
            pltpu.VMEM((QUARTER, D), b16),
            pltpu.VMEM((QUARTER, D), b16),
            pltpu.VMEM((QUARTER, D), f32),
            pltpu.VMEM((QUARTER, D), f32),
        ],
        name="feed_forward",
        compiler_params=pltpu.CompilerParams(vmem_limit_bytes=56 * 2**20),
    )(limit, tokens, cotangent, gains, attended, wo, weights)


def backward_kernel(
    length, tokens, gains, taps, normed, streams, projected, lse, w_all, grad_rows, grad_middle,
    gain_two, raw_out, raw_ffn,
    input_grad, small, ffn_pair, heads_pair,
    grad_heads, ffn_sum, ffn_in, f_one_a, f_one_b, f_one_c, f_two_a, f_two_b, f_two_c,
    f_three_a, f_three_b, f_three_c, o_one, o_two, o_three, out_part,
    key_grad, value_grad, key_turned, grad_stream, raw_conv, raw_qkv, qkv_low, q_one, q_two, normed_part, normed_in,
    pair_out, pair_in, send_sem, recv_sem, local_sem,
):
    x, y, z, core = place()
    here = {"x": x, "y": y, "z": z}
    sems = (send_sem, recv_sem)
    sibling = device(x, y, z, 1 - core)
    along = neighbours(x, y, z, core)
    count = Counter()
    f_one, f_two, f_three = (f_one_a, f_one_b, f_one_c), (f_two_a, f_two_b, f_two_c), (f_three_a, f_three_b, f_three_c)

    def go(source, target, other):
        return send(source, target, sems, count.take(), other)

    def to(axis, k):
        return (here[axis] + k) % 4

    greet([sibling] + along["x"] + along["y"] + along["z"])
    turned = [go(grad_rows.at[to("y", k)], grad_heads.at[y], along["y"][k - 1]) for k in (1, 2, 3)]
    ffn_zero = [
        go(raw_ffn.at[1 - core, quarter], ffn_in.at[quarter], sibling) for quarter in range(4)
    ]
    kept = pltpu.make_async_copy(raw_ffn.at[core], ffn_sum, local_sem.at[0])
    kept.start()
    out_one = [go(raw_out.at[to("y", k)], o_one.at[k - 1], along["y"][k - 1]) for k in (1, 2, 3)]
    grad_heads[y] = grad_rows[y]
    key_grad[...] = jnp.zeros_like(key_grad)
    value_grad[...] = jnp.zeros_like(value_grad)
    raw_conv[...] = jnp.zeros_like(raw_conv)
    raw_qkv[...] = jnp.zeros_like(raw_qkv)
    grad_stream[:, SEQ : SEQ + 8, :] = jnp.zeros((3, 8, GROUP), jnp.float32)
    for head in range(GROUP_HEADS):
        key_turned[head] = streams[GROUP_HEADS + head].T
    key_ids = lax.broadcasted_iota(jnp.int32, (SEQ, 1), 0)
    bias = jnp.where(key_ids < length[0], 0.0, NEG_FILL)
    upper = (
        lax.broadcasted_iota(jnp.int32, (QUARTER, QUARTER), 0)
        <= lax.broadcasted_iota(jnp.int32, (QUARTER, QUARTER), 1)
    )
    wait_all(turned)

    def attend_back(i):
        rows_i = slice(i * QUARTER, (i + 1) * QUARTER)
        keys = (i + 1) * QUARTER
        grads = grad_heads[i]
        query_pieces = []
        for head in range(GROUP_HEADS):
            query = streams[head, rows_i, :]
            upstream = grads[:, head * HEAD_DIM : (head + 1) * HEAD_DIM]
            scores = mul(streams[GROUP_HEADS + head, :keys, :], query, NT) + (
                bias[:keys] - lse[head, :, rows_i]
            )
            corner = jnp.where(upper, scores[keys - QUARTER :], NEG_FILL)
            scores = corner if i == 0 else jnp.concatenate([scores[: keys - QUARTER], corner], 0)
            probs = jnp.exp(scores)
            prob_grad = mul(streams[2 * GROUP_HEADS + head, :keys, :], upstream, NT)
            centre = jnp.sum(prob_grad * probs, axis=0, keepdims=True)
            score_grad = (probs * (prob_grad - centre)).astype(jnp.bfloat16)
            query_pieces.append((mul(key_turned[head, :, :keys], score_grad) * SCALE).T)
            key_grad[head, :keys, :] += mul(score_grad, query)
            value_grad[head, :keys, :] += mul(probs.astype(jnp.bfloat16), upstream)
        for kind, pieces in (
            (0, query_pieces),
            (1, [key_grad[head, rows_i, :] for head in range(GROUP_HEADS)]),
            (2, [value_grad[head, rows_i, :] for head in range(GROUP_HEADS)]),
        ):
            grad_stream[kind, rows_i, :] = (
                jnp.concatenate(pieces, axis=1).astype(jnp.bfloat16).astype(jnp.float32)
            )
        normed_turned = normed[i].T
        total = None
        for kind in range(3):
            block = projected[kind, 8 + i * QUARTER : 8 + (i + 1) * QUARTER, :]
            summed = None
            for t in range(KW):
                shifted = grad_stream[kind, i * QUARTER + t : (i + 1) * QUARTER + t, :]
                term = taps[t, kind : kind + 1] * shifted
                summed = term if summed is None else summed + term
                raw_conv[t, kind : kind + 1, :] += jnp.sum(shifted * block, axis=0, keepdims=True)
            lower = summed.astype(jnp.bfloat16)
            raw_qkv[kind] += mul(normed_turned, lower)
            term = mul(lower, w_all[kind].reshape(D, GROUP), NT)
            total = term if total is None else total + term
        normed_part[i] = total.astype(jnp.bfloat16)

    def part_cell(order, fixed, moved):
        free = [a for a in "yxz" if a not in fixed]
        return cell(here, free, moved)

    attend_back(3)
    kept.wait()
    wait_all(ffn_zero)

    def add_zero(index, carry):
        a, b = index // 4, index % 4
        ffn_sum[a, b] = (
            ffn_sum[a, b].astype(jnp.float32) + ffn_in[a, b].astype(jnp.float32)
        ).astype(jnp.bfloat16)
        return carry

    lax.fori_loop(0, 16, add_zero, 0)
    stage_one = []
    for number, (order, c, w) in enumerate(RS_PARTS):
        for k in (1, 2, 3):
            index = cell(here, order[1:], {order[0]: to(order[0], k)})
            stage_one.append(
                go(
                    ffn_sum.at[index + (slice(None), slice(c, c + w))],
                    f_one[number].at[k - 1],
                    along[order[0]][k - 1],
                )
            )
    attend_back(2)
    wait_all(stage_one)
    stage_two = []
    for number, (order, c, w) in enumerate(RS_PARTS):
        for step in range(4):
            free = [a for a in "yxz" if a in order[1:]]
            index = cell(here, free[1:], {free[0]: step}) + (slice(None), slice(c, c + w))
            ffn_sum[index] = (
                ffn_sum[index].astype(jnp.float32)
                + f_one[number][0, step].astype(jnp.float32)
                + f_one[number][1, step].astype(jnp.float32)
                + f_one[number][2, step].astype(jnp.float32)
            ).astype(jnp.bfloat16)
        for k in (1, 2, 3):
            index = cell(here, order[2], {order[1]: to(order[1], k)})
            stage_two.append(
                go(
                    ffn_sum.at[index + (slice(None), slice(c, c + w))],
                    f_two[number].at[k - 1],
                    along[order[1]][k - 1],
                )
            )
    wait_all(out_one)
    out_part[...] = (
        raw_out[y].astype(jnp.float32)
        + o_one[0].astype(jnp.float32)
        + o_one[1].astype(jnp.float32)
        + o_one[2].astype(jnp.float32)
    ).astype(jnp.bfloat16)
    out_two = [go(out_part.at[to("x", k)], o_two.at[k - 1], along["x"][k - 1]) for k in (1, 2, 3)]
    attend_back(1)
    wait_all(stage_two)
    stage_three = []
    for number, (order, c, w) in enumerate(RS_PARTS):
        index = cell(here, order[2]) + (slice(None), slice(c, c + w))
        ffn_sum[index] = (
            ffn_sum[index].astype(jnp.float32)
            + f_two[number][0].astype(jnp.float32)
            + f_two[number][1].astype(jnp.float32)
            + f_two[number][2].astype(jnp.float32)
        ).astype(jnp.bfloat16)
        for k in (1, 2, 3):
            index = cell(here, "", {order[2]: to(order[2], k)})
            stage_three.append(
                go(
                    ffn_sum.at[index + (slice(None), slice(c, c + w))],
                    f_three[number].at[k - 1],
                    along[order[2]][k - 1],
                )
            )
    wait_all(out_two)
    out_part[x] = (
        out_part[x].astype(jnp.float32)
        + o_two[0].astype(jnp.float32)
        + o_two[1].astype(jnp.float32)
        + o_two[2].astype(jnp.float32)
    ).astype(jnp.bfloat16)
    out_three = [
        go(out_part.at[x, to("z", k)], o_three.at[k - 1], along["z"][k - 1]) for k in (1, 2, 3)
    ]
    attend_back(0)
    rows_out = [
        go(normed_part.at[to("y", k)], normed_in.at[k - 1], along["y"][k - 1]) for k in (1, 2, 3)
    ]
    qkv_low[...] = raw_qkv[...].reshape(3, 4, 4, PAIR, GROUP).astype(jnp.bfloat16)
    qkv_one = [go(qkv_low.at[:, to("x", k)], q_one.at[k - 1], along["x"][k - 1]) for k in (1, 2, 3)]
    wait_all(stage_three)
    for number, (order, c, w) in enumerate(RS_PARTS):
        index = cell(here, "") + (slice(None), slice(c, c + w))
        ffn_pair[:, c : c + w] = (
            ffn_sum[index].astype(jnp.float32)
            + f_three[number][0].astype(jnp.float32)
            + f_three[number][1].astype(jnp.float32)
            + f_three[number][2].astype(jnp.float32)
        )
    wait_all(out_three)
    pair_out[3] = (
        out_part[x, z].astype(jnp.float32)
        + o_three[0].astype(jnp.float32)
        + o_three[1].astype(jnp.float32)
        + o_three[2].astype(jnp.float32)
    )
    wait_all(qkv_one)
    qkv_low[:, x] = (
        qkv_low[:, x].astype(jnp.float32)
        + q_one[0].astype(jnp.float32)
        + q_one[1].astype(jnp.float32)
        + q_one[2].astype(jnp.float32)
    ).astype(jnp.bfloat16)
    qkv_two = [go(qkv_low.at[:, x, to("z", k)], q_two.at[k - 1], along["z"][k - 1]) for k in (1, 2, 3)]
    wait_all(qkv_two)
    pair_out[0:3] = (
        qkv_low[:, x, z].astype(jnp.float32)
        + q_two[0].astype(jnp.float32)
        + q_two[1].astype(jnp.float32)
        + q_two[2].astype(jnp.float32)
    )
    pair = go(pair_out, pair_in, sibling)
    wait_all(rows_out)
    grad = (
        normed_part[y].astype(jnp.float32)
        + normed_in[0].astype(jnp.float32)
        + normed_in[1].astype(jnp.float32)
        + normed_in[2].astype(jnp.float32)
    )
    values = tokens[...].astype(jnp.float32)
    inverse = lax.rsqrt(jnp.mean(values * values, axis=-1, keepdims=True) + NORM_EPS)
    unit = values * inverse
    scaled = grad * gains[0:1]
    inner = jnp.mean(scaled * unit, axis=-1, keepdims=True)
    input_grad[...] = grad_middle[...] + inverse * (scaled - unit * inner)
    small[...] = jnp.zeros_like(small)
    small[0:1, :] = jnp.sum(grad * unit, axis=0, keepdims=True)
    small[1:2, :] = gain_two[...]
    mine = lax.broadcasted_iota(jnp.int32, (1, D), 1) // GROUP == y
    for t in range(KW):
        for kind in range(3):
            row = raw_conv[t, kind : kind + 1, :]
            small[2 + 3 * t + kind : 3 + 3 * t + kind, :] = jnp.where(
                mine, jnp.concatenate([row] * 4, axis=1), 0.0
            )
    pair.wait()
    heads_pair[...] = pair_out[...] + pair_in[...]


RS_PARTS = (("xzy", 0, 256), ("zyx", 256, 256), ("yxz", 512, 256))


def backward(length, tokens, gains, taps, normed, streams, projected, lse, w_all, grad_rows, grad_middle, gain_two, raw_out, raw_ffn):
    f32, b16 = jnp.float32, jnp.bfloat16
    vmem = pl.BlockSpec(memory_space=pltpu.VMEM)
    scratch = [
        pltpu.VMEM((4, QUARTER, GROUP), b16),
        pltpu.VMEM((4, 4, 4, PAIR, D), b16),
        pltpu.VMEM((4, 4, 4, PAIR, D), b16),
    ]
    scratch += [pltpu.VMEM((3, 4, 4, PAIR, w), b16) for _, _, w in RS_PARTS]
    scratch += [pltpu.VMEM((3, 4, PAIR, w), b16) for _, _, w in RS_PARTS]
    scratch += [pltpu.VMEM((3, PAIR, w), b16) for _, _, w in RS_PARTS]
    scratch += [
        pltpu.VMEM((3, 4, 4, PAIR, GROUP), b16),
        pltpu.VMEM((3, 4, PAIR, GROUP), b16),
        pltpu.VMEM((3, PAIR, GROUP), b16),
        pltpu.VMEM((4, 4, PAIR, GROUP), b16),
        pltpu.VMEM((GROUP_HEADS, SEQ, HEAD_DIM), f32),
        pltpu.VMEM((GROUP_HEADS, SEQ, HEAD_DIM), f32),
        pltpu.VMEM((GROUP_HEADS, HEAD_DIM, SEQ), b16),
        pltpu.VMEM((3, SEQ + 8, GROUP), f32),
        pltpu.VMEM((KW, 8, GROUP), f32),
        pltpu.VMEM((3, D, GROUP), f32),
        pltpu.VMEM((3, 4, 4, PAIR, GROUP), b16),
        pltpu.VMEM((3, 3, 4, PAIR, GROUP), b16),
        pltpu.VMEM((3, 3, PAIR, GROUP), b16),
        pltpu.VMEM((4, QUARTER, D), b16),
        pltpu.VMEM((3, QUARTER, D), b16),
        pltpu.VMEM((4, PAIR, GROUP), f32),
        pltpu.VMEM((4, PAIR, GROUP), f32),
        pltpu.SemaphoreType.DMA((64,)),
        pltpu.SemaphoreType.DMA((64,)),
        pltpu.SemaphoreType.DMA((1,)),
    ]
    return pl.pallas_call(
        backward_kernel,
        out_shape=[
            jax.ShapeDtypeStruct((QUARTER, D), f32),
            jax.ShapeDtypeStruct((16, D), f32),
            jax.ShapeDtypeStruct((PAIR, D), f32),
            jax.ShapeDtypeStruct((4, PAIR, GROUP), f32),
        ],
        in_specs=[pl.BlockSpec(memory_space=pltpu.SMEM)]
        + [vmem] * 12
        + [pl.BlockSpec(memory_space=pl.ANY)],
        out_specs=[vmem] * 4,
        scratch_shapes=scratch,
        name="attend_back_and_scatter",
        compiler_params=pltpu.CompilerParams(
            collective_id=3, has_side_effects=True, vmem_limit_bytes=60 * 2**20
        ),
    )(length, tokens, gains, taps, normed, streams, projected, lse, w_all, grad_rows, grad_middle, gain_two, raw_out, raw_ffn)


def adam_step(weight, gradient, moment_one, moment_two):
    first_new = BETA_ONE * moment_one + (1.0 - BETA_ONE) * gradient
    second_new = BETA_TWO * moment_two + (1.0 - BETA_TWO) * gradient * gradient
    stepped = (
        first_new
        / (1.0 - BETA_ONE**STEP)
        / (jnp.sqrt(second_new / (1.0 - BETA_TWO**STEP)) + ADAM_EPS)
    )
    return (first_new, second_new, weight - ADAM_RATE * stepped)


def per_device(
    tokens,
    lengths,
    cotangent,
    gains,
    conv,
    w_qkv,
    w_out,
    ffn_weights,
    mom_qkv,
    mom_out,
    mom_ffn,
    gain_first,
    gain_second,
    conv_first,
    conv_second,
):
    head_at = lax.axis_index("head")
    taps = lax.dynamic_slice_in_dim(conv, head_at * GROUP, GROUP, 2)
    w_heads = jnp.concatenate([w_qkv, w_out.T[None]])
    mom_heads = jnp.concatenate([mom_qkv, mom_out.T[None]])
    rows_in = tokens[0]
    normed, streams, projected, lse, attended, w_all, wo_all, ffn_all = forward(
        lengths, rows_in, gains, taps, w_heads, ffn_weights
    )
    output, grad_middle, gain_two, grad_rows, raw_out, raw_ffn = feed_forward(
        lengths - head_at * QUARTER,
        rows_in,
        cotangent[0],
        gains,
        attended,
        wo_all.reshape(4, D, GROUP),
        ffn_all.reshape(2, FF, D),
    )
    input_grad, small, ffn_pair, heads_pair = backward(
        lengths,
        rows_in,
        gains,
        taps,
        normed,
        streams,
        projected,
        lse,
        w_all,
        grad_rows,
        grad_middle,
        gain_two,
        raw_out.reshape(4, 4, 4, PAIR, GROUP),
        raw_ffn.reshape(2, 4, 4, 4, PAIR, D),
    )
    small_sum, gram, hgram, iterate, head_iterate, ffn_part = sum_over_devices(
        ffn_pair, heads_pair, mom_ffn, mom_heads, small
    )
    gain_sum = small_sum[:2]
    conv_sum = small_sum[2:11].reshape(conv.shape)
    grad_norm = jnp.sqrt(jnp.sum(small_sum[:11] * small_sum[:11]) + jnp.sum(small_sum[11]))
    factor = CLIP_NORM / jnp.maximum(grad_norm, CLIP_NORM)
    heads_part = lax.dynamic_slice_in_dim(heads_pair, (lax.axis_index("dp") % 2) * SUB, SUB, 1)
    grad_gains = gain_sum * factor
    grad_conv = conv_sum * factor
    grad_qkv = heads_part[:3] * factor
    grad_out = heads_part[3].T * factor
    grad_ffn = ffn_part * factor
    new_mom_qkv = MOMENTUM * mom_qkv + grad_qkv
    new_mom_out = MOMENTUM * mom_out + grad_out
    new_mom_ffn = MOMENTUM * mom_ffn + grad_ffn
    ffn_orth, heads_orth = swap(*chain(gram, hgram, iterate, head_iterate))
    new_qkv = w_qkv - RATE_IN * math.sqrt(D) * heads_orth[:3]
    new_out = w_out - RATE_OUT * math.sqrt(D) * heads_orth[3].T
    new_ffn = ffn_weights - RATE_IN * math.sqrt(max(FF, D)) * ffn_orth
    new_gain_first, new_gain_second, new_gains = adam_step(
        gains, grad_gains, gain_first, gain_second
    )
    new_conv_first, new_conv_second, new_conv = adam_step(conv, grad_conv, conv_first, conv_second)
    return (
        output[None],
        input_grad[None],
        grad_gains,
        grad_conv,
        grad_qkv,
        grad_out,
        grad_ffn,
        grad_norm,
        new_mom_qkv,
        new_mom_out,
        new_mom_ffn,
        new_gain_first,
        new_gain_second,
        new_conv_first,
        new_conv_second,
        new_gains,
        new_conv,
        new_qkv,
        new_out,
        new_ffn,
    )


def solution(mesh):
    placed = (
        P("dp", "head", None),
        P("dp"),
        P("dp", "head", None),
        P(),
        P(),
        P(None, "dp", "head"),
        P("head", "dp"),
        P(None, ("head", "dp"), None),
        P(None, "dp", "head"),
        P("head", "dp"),
        P(None, ("head", "dp"), None),
        P(),
        P(),
        P(),
        P(),
    )
    return jax.shard_map(
        per_device,
        mesh=mesh,
        in_specs=placed,
        out_specs=(
            P("dp", "head", None),
            P("dp", "head", None),
            P(),
            P(),
            P(None, "dp", "head"),
            P("head", "dp"),
            P(None, ("head", "dp"), None),
            P(),
            P(None, "dp", "head"),
            P("head", "dp"),
            P(None, ("head", "dp"), None),
            P(),
            P(),
            P(),
            P(),
            P(),
            P(),
            P(None, "dp", "head"),
            P("head", "dp"),
            P(None, ("head", "dp"), None),
        ),
        check_vma=False,
    )
```

```python
import math

import jax
import jax.numpy as jnp
from jax import lax
from jax.experimental import pallas as pl
from jax.experimental.pallas import tpu as pltpu
from jax.sharding import PartitionSpec as P

D = 768
HEADS = 12
HEAD_DIM = 64
FF = 3072
KW = 3
NS_ITERS = 5
STEP = 10


NORM_EPS = 1e-06
NEG_FILL = -1e30
CLIP_NORM = 1.0
MOMENTUM = 0.95
RATE_IN = 0.02
RATE_OUT = 0.15
ADAM_RATE = 0.5
BETA_ONE = 0.9
BETA_TWO = 0.999
ADAM_EPS = 1e-08
NS_EPS = 1e-07
COEF_A = 3.4445
COEF_B = -4.775
COEF_C = 2.0315


SUB = 24
PAIR = 2 * SUB
BLK = 256
MESH_IDS = pl.DeviceIdType.MESH


def place():
    flat = lax.axis_index("dp")
    return flat // 8, lax.axis_index("head"), (flat // 2) % 4, flat % 2


def device(x, y, z, core):
    return (y % 4, ((x % 4) * 4 + z % 4) * 2 + core)


def greet(others):
    barrier = pltpu.get_barrier_semaphore()
    for other in others:
        pl.semaphore_signal(barrier, inc=1, device_id=other, device_id_type=MESH_IDS)
    pl.semaphore_wait(barrier, len(others))


def send(source, target, sems, index, other):
    copy = pltpu.make_async_remote_copy(
        src_ref=source,
        dst_ref=target,
        send_sem=sems[0].at[index],
        recv_sem=sems[1].at[index],
        device_id=other,
        device_id_type=MESH_IDS,
    )
    copy.start()
    return copy


def rows(start, count):
    return pl.ds(pl.multiple_of(start, 8), count)


def split(values):
    high = values.astype(jnp.bfloat16)
    return high, (values - high.astype(jnp.float32)).astype(jnp.bfloat16)


def product(left, right, dims=(((1,), (0,)), ((), ()))):
    lh, ll = left
    rh, rl = right

    def dot(a, b):
        return lax.dot_general(a, b, dims, preferred_element_type=jnp.float32)

    return dot(lh, rh) + (dot(lh, rl) + dot(ll, rh))


SEQ = 1024
QUARTER = SEQ // 4
GROUP = D // 4
GROUP_HEADS = GROUP // HEAD_DIM
SCALE = HEAD_DIM ** (-0.5)
NT = (((1,), (1,)), ((), ()))
TN = (((0,), (0,)), ((), ()))
NN = (((1,), (0,)), ((), ()))
PARTS = (("yzx", 0, 384), ("yxz", 384, 384))


def mul(a, b, dims=NN):
    return lax.dot_general(a, b, dims, preferred_element_type=jnp.float32)


def neighbours(x, y, z, core):
    return {
        "x": [device(x + k, y, z, core) for k in (1, 2, 3)],
        "y": [device(x, y + k, z, core) for k in (1, 2, 3)],
        "z": [device(x, y, z + k, core) for k in (1, 2, 3)],
    }


def cell(here, free, moved=None):
    moved = moved or {}
    return tuple(slice(None) if a in free else moved.get(a, here[a]) for a in "yxz")


class Counter:
    def __init__(self):
        self.count = 0

    def take(self):
        self.count += 1
        return self.count - 1


def wait_all(copies):
    for copy in copies:
        copy.wait()


def in_core_order(core, own, other):
    return jnp.concatenate(
        [jnp.where(core == 0, own, other), jnp.where(core == 0, other, own)], axis=-2
    )


def unit_rows(values):
    values = values.astype(jnp.float32)
    inverse = lax.rsqrt(jnp.mean(values * values, axis=-1, keepdims=True) + NORM_EPS)
    return values * inverse, inverse


def forward_kernel(
    length, tokens, gains, conv, w_qkv, w_out, w_ffn,
    all_tokens, normed, streams, projected, lse, attended, w_all, wo_all, taps, ffn_all,
    w_heads, swap_heads, swap_ffn, ffn_own, att_send, send_sem, recv_sem, local_sem,
):
    x, y, z, core = place()
    here = {"x": x, "y": y, "z": z}
    sems = (send_sem, recv_sem)
    sibling = device(x, y, z, 1 - core)
    along = neighbours(x, y, z, core)
    count = Counter()

    def go(source, target, other):
        return send(source, target, sems, count.take(), other)

    all_tokens[y] = tokens[...]
    w_heads[0:3] = w_qkv[...]
    w_heads[3] = w_out[...].T
    greet([sibling] + along["x"] + along["y"] + along["z"])
    swaps = [
        go(w_heads, swap_heads, sibling),
        go(w_ffn.at[1 - core], swap_ffn, sibling),
    ]
    for t in range(KW):
        taps[t] = sum(
            jnp.where(y == group, conv[t, :, group * GROUP : (group + 1) * GROUP], 0.0)
            for group in range(4)
        )
    wait_all(swaps)
    at_xz = x * 4 + z
    ffn_own[...] = in_core_order(core, w_ffn[core], swap_ffn[...]).astype(jnp.bfloat16)
    w_all[:, x, z] = in_core_order(core, w_heads[...], swap_heads[...]).astype(jnp.bfloat16)
    one = [device(x + k * (1 - core), y, z + k * core, core) for k in (1, 2, 3)]
    ffn_one = [
        go(ffn_own.at[:, c : c + w], ffn_all.at[y, x, z, :, c : c + w], other)
        for order, c, w in PARTS
        for other in along[order[0]]
    ]
    spread = [go(all_tokens.at[y], all_tokens.at[y], other) for other in along["y"]]
    heads_one = [go(w_all.at[:, x, z], w_all.at[:, x, z], other) for other in one]
    kept = pltpu.make_async_copy(ffn_own, ffn_all.at[y, x, z], local_sem.at[0])
    kept.start()
    wait_all(heads_one)

    @pl.when(core == 0)
    def _():
        for k in range(3):
            pltpu.make_async_remote_copy(
                src_ref=w_all.at[:, :, z], dst_ref=w_all.at[:, :, z],
                send_sem=send_sem.at[60 + k], recv_sem=recv_sem.at[60 + k],
                device_id=along["z"][k], device_id_type=MESH_IDS,
            ).start()

    @pl.when(core == 1)
    def _():
        for k in range(3):
            pltpu.make_async_remote_copy(
                src_ref=w_all.at[:, x], dst_ref=w_all.at[:, x],
                send_sem=send_sem.at[60 + k], recv_sem=recv_sem.at[60 + k],
                device_id=along["x"][k], device_id_type=MESH_IDS,
            ).start()

    kept.wait()
    wait_all(ffn_one)
    ffn_two = []
    for order, c, w in PARTS:
        region = ffn_all.at[cell(here, order[0]) + (slice(None), slice(c, c + w))]
        ffn_two += [go(region, region, other) for other in along[order[1]]]

    @pl.when(core == 0)
    def _():
        for k in range(3):
            pltpu.make_async_remote_copy(
                src_ref=w_all.at[:, :, z], dst_ref=w_all.at[:, :, z],
                send_sem=send_sem.at[60 + k], recv_sem=recv_sem.at[60 + k],
                device_id=along["z"][k], device_id_type=MESH_IDS,
            ).wait()

    @pl.when(core == 1)
    def _():
        for k in range(3):
            pltpu.make_async_remote_copy(
                src_ref=w_all.at[:, x], dst_ref=w_all.at[:, x],
                send_sem=send_sem.at[60 + k], recv_sem=recv_sem.at[60 + k],
                device_id=along["x"][k], device_id_type=MESH_IDS,
            ).wait()

    half = pl.ds(2 * core, 2)
    wo_y = [go(w_all.at[3, half], wo_all.at[y, half], other) for other in along["y"]]
    wo_all[y] = w_all[3]
    wait_all(spread)
    projected[:, 0:8, :] = jnp.zeros((3, 8, GROUP), jnp.float32)
    key_ids = lax.broadcasted_iota(jnp.int32, (SEQ, 1), 0)
    bias = jnp.where(key_ids < length[0], 0.0, NEG_FILL)
    upper = (
        lax.broadcasted_iota(jnp.int32, (QUARTER, QUARTER), 0)
        <= lax.broadcasted_iota(jnp.int32, (QUARTER, QUARTER), 1)
    )

    def project(i):
        unit, _ = unit_rows(all_tokens[i])
        normed[i] = (unit * gains[0:1]).astype(jnp.bfloat16)
        rows_i = slice(i * QUARTER, (i + 1) * QUARTER)
        for kind in range(3):
            base = 8 + i * QUARTER
            projected[kind, base : base + QUARTER, :] = mul(
                normed[i], w_all[kind].reshape(D, GROUP)
            )
            summed = taps[0, kind : kind + 1] * projected[kind, base : base + QUARTER, :]
            for t in range(1, KW):
                summed = summed + taps[t, kind : kind + 1] * projected[
                    kind, base - t : base - t + QUARTER, :
                ]
            stream = summed.astype(jnp.bfloat16)
            if kind == 0:
                stream = stream * jnp.bfloat16(SCALE)
            for head in range(GROUP_HEADS):
                streams[kind * GROUP_HEADS + head, rows_i, :] = stream[
                    :, head * HEAD_DIM : (head + 1) * HEAD_DIM
                ]

    def attend(i):
        rows_i = slice(i * QUARTER, (i + 1) * QUARTER)
        keys = (i + 1) * QUARTER
        pieces = []
        for head in range(GROUP_HEADS):
            scores = mul(
                streams[GROUP_HEADS + head, :keys, :], streams[head, rows_i, :], NT
            ) + bias[:keys]
            corner = jnp.where(upper, scores[keys - QUARTER :], NEG_FILL)
            scores = corner if i == 0 else jnp.concatenate([scores[: keys - QUARTER], corner], 0)
            top = jnp.max(scores, axis=0, keepdims=True)
            lifted = jnp.exp(scores - top)
            total = jnp.sum(lifted, axis=0, keepdims=True)
            probs = (lifted * (1.0 / total)).astype(jnp.bfloat16)
            lse[head, :, rows_i] = top + jnp.log(total)
            pieces.append(mul(streams[2 * GROUP_HEADS + head, :keys, :], probs, TN).T)
        att_send[i] = jnp.concatenate(pieces, axis=1).astype(jnp.bfloat16)

    wait_all(ffn_two)
    ffn_three = []
    for order, c, w in PARTS:
        region = ffn_all.at[cell(here, order[:2]) + (slice(None), slice(c, c + w))]
        ffn_three += [go(region, region, other) for other in along[order[2]]]
    for i in range(4):
        project(i)
    attend(0)
    attend(1)
    wait_all(wo_y)
    wo_pair = [
        go(wo_all.at[(y + k) % 4, half], wo_all.at[(y + k) % 4, half], sibling) for k in (1, 2, 3)
    ]
    attend(2)
    attend(3)
    heads_out = [
        go(att_send.at[(y + k) % 4], attended.at[y], along["y"][k - 1]) for k in (1, 2, 3)
    ]
    attended[y] = att_send[y]
    wait_all(wo_pair)
    wait_all(ffn_three)
    wait_all(heads_out)


def forward(length, tokens, gains, conv, w_qkv, w_out, w_ffn):
    f32, b16 = jnp.float32, jnp.bfloat16
    vmem = pl.BlockSpec(memory_space=pltpu.VMEM)
    return pl.pallas_call(
        forward_kernel,
        out_shape=[
            jax.ShapeDtypeStruct((4, QUARTER, D), b16),
            jax.ShapeDtypeStruct((4, QUARTER, D), b16),
            jax.ShapeDtypeStruct((3 * GROUP_HEADS, SEQ, HEAD_DIM), b16),
            jax.ShapeDtypeStruct((3, SEQ + 8, GROUP), f32),
            jax.ShapeDtypeStruct((GROUP_HEADS, 1, SEQ), f32),
            jax.ShapeDtypeStruct((4, QUARTER, GROUP), b16),
            jax.ShapeDtypeStruct((4, 4, 4, PAIR, GROUP), b16),
            jax.ShapeDtypeStruct((4, 4, 4, PAIR, GROUP), b16),
            jax.ShapeDtypeStruct((KW, 3, GROUP), f32),
            jax.ShapeDtypeStruct((4, 4, 4, PAIR, D), b16),
        ],
        in_specs=[pl.BlockSpec(memory_space=pltpu.SMEM)] + [vmem] * 6,
        out_specs=[vmem] * 9 + [pl.BlockSpec(memory_space=pl.ANY)],
        scratch_shapes=[
            pltpu.VMEM((4, SUB, GROUP), f32),
            pltpu.VMEM((4, SUB, GROUP), f32),
            pltpu.VMEM((SUB, D), f32),
            pltpu.VMEM((PAIR, D), b16),
            pltpu.VMEM((4, QUARTER, GROUP), b16),
            pltpu.SemaphoreType.DMA((64,)),
            pltpu.SemaphoreType.DMA((64,)),
            pltpu.SemaphoreType.DMA((1,)),
        ],
        name="attend_and_gather",
        compiler_params=pltpu.CompilerParams(
            collective_id=2, has_side_effects=True, vmem_limit_bytes=56 * 2**20
        ),
    )(length, tokens, gains, conv, w_qkv, w_out, w_ffn)


UNITS = (256, 512, 768, 768, 512, 256)


def ffn_kernel(
    limit, tokens, cotangent, gains, attended, wo, own_weights,
    output, grad_middle, gain_two, grad_attended, raw_out, ffn_sum,
    weights, raw, raw_in, middle, normed, upstream, out_sum, grad_sum, send_sem, recv_sem, local_sem,
):
    x, y, z, core = place()
    sems = (send_sem, recv_sem)
    sibling = device(x, y, z, 1 - core)
    parts = []
    for units in UNITS:
        start = parts[-1][0].stop if parts else 0
        parts.append((slice(start, start + units),))
    greet([sibling])
    arriving = [
        send(own_weights.at[at], weights.at[(core,) + at], sems, number, sibling)
        for number, at in enumerate(parts)
    ]
    loading = []
    for number, at in enumerate(parts):
        copy = pltpu.make_async_copy(
            own_weights.at[at], weights.at[(core,) + at], local_sem.at[number]
        )
        copy.start()
        loading.append(copy)
    mixed = mul(attended[0], wo[0], NT)
    for group in range(1, 4):
        mixed = mixed + mul(attended[group], wo[group], NT)
    rows_here = tokens[...].astype(jnp.float32) + mixed
    middle[...] = rows_here
    inverse = lax.rsqrt(jnp.mean(rows_here * rows_here, axis=-1, keepdims=True) + NORM_EPS)
    normed[...] = (rows_here * inverse * gains[1:2]).astype(jnp.bfloat16)
    real = lax.broadcasted_iota(jnp.int32, (QUARTER, 1), 0) < limit[0]
    upstream[...] = jnp.where(real, cotangent[...].astype(jnp.float32), 0.0).astype(jnp.bfloat16)
    leaving = []

    def settle(number):
        at = parts[number]
        leaving[number].wait()
        ffn_sum[at] = (
            raw[(core,) + at].astype(jnp.float32) + raw_in[at].astype(jnp.float32)
        ).astype(jnp.bfloat16)

    for number, at in enumerate(parts):
        loading[number].wait()
        arriving[number].wait()
        into, back = weights[(0,) + at], weights[(1,) + at]
        positive = jnp.maximum(mul(normed[...], into, NT), 0.0)
        active = (positive * positive).astype(jnp.bfloat16)
        grad_hidden = (mul(upstream[...], back, NT) * (2.0 * positive)).astype(jnp.bfloat16)
        out_term = mul(active, back)
        grad_term = mul(grad_hidden, into)
        out_sum[...] = out_term if number == 0 else out_sum[...] + out_term
        grad_sum[...] = grad_term if number == 0 else grad_sum[...] + grad_term
        raw[(0,) + at] = mul(grad_hidden, normed[...], TN).astype(jnp.bfloat16)
        raw[(1,) + at] = mul(active, upstream[...], TN).astype(jnp.bfloat16)
        leaving.append(
            send(raw.at[(1 - core,) + at], raw_in.at[at], sems, len(parts) + number, sibling)
        )
        if number >= 2:
            settle(number - 2)
    rows_here = middle[...]
    output[...] = rows_here + out_sum[...]
    inverse = lax.rsqrt(jnp.mean(rows_here * rows_here, axis=-1, keepdims=True) + NORM_EPS)
    unit = rows_here * inverse
    grad = grad_sum[...]
    gain_two[...] = jnp.sum(grad * unit, axis=0, keepdims=True)
    scaled = grad * gains[1:2]
    inner = jnp.mean(scaled * unit, axis=-1, keepdims=True)
    grad_rows = jnp.where(real, cotangent[...].astype(jnp.float32), 0.0) + inverse * (
        scaled - unit * inner
    )
    grad_middle[...] = grad_rows
    lower = grad_rows.astype(jnp.bfloat16)
    for group in range(4):
        grad_attended[group] = mul(lower, wo[group]).astype(jnp.bfloat16)
        raw_out[group] = mul(lower, attended[group], TN).astype(jnp.bfloat16)
    settle(len(parts) - 2)
    settle(len(parts) - 1)


def feed_forward(limit, tokens, cotangent, gains, attended, wo, weights):
    f32, b16 = jnp.float32, jnp.bfloat16
    vmem = pl.BlockSpec(memory_space=pltpu.VMEM)
    anywhere = pl.BlockSpec(memory_space=pl.ANY)
    return pl.pallas_call(
        ffn_kernel,
        out_shape=[
            jax.ShapeDtypeStruct((QUARTER, D), f32),
            jax.ShapeDtypeStruct((QUARTER, D), f32),
            jax.ShapeDtypeStruct((1, D), f32),
            jax.ShapeDtypeStruct((4, QUARTER, GROUP), b16),
            jax.ShapeDtypeStruct((4, D, GROUP), b16),
            jax.ShapeDtypeStruct((FF, D), b16),
        ],
        in_specs=[pl.BlockSpec(memory_space=pltpu.SMEM)] + [vmem] * 5 + [anywhere],
        out_specs=[vmem] * 6,
        scratch_shapes=[
            pltpu.VMEM((2, FF, D), b16),
            pltpu.VMEM((2, FF, D), b16),
            pltpu.VMEM((FF, D), b16),
            pltpu.VMEM((QUARTER, D), f32),
            pltpu.VMEM((QUARTER, D), b16),
            pltpu.VMEM((QUARTER, D), b16),
            pltpu.VMEM((QUARTER, D), f32),
            pltpu.VMEM((QUARTER, D), f32),
            pltpu.SemaphoreType.DMA((16,)),
            pltpu.SemaphoreType.DMA((16,)),
            pltpu.SemaphoreType.DMA((8,)),
        ],
        name="feed_forward",
        compiler_params=pltpu.CompilerParams(
            collective_id=1, has_side_effects=True, vmem_limit_bytes=60 * 2**20
        ),
    )(limit, tokens, cotangent, gains, attended, wo, weights)


def backward_kernel(
    length, taps, lse, grad_rows, gain_two,
    streams_far, all_tokens_far, normed_far, projected_far, w_all_far, raw_out, ffn_part,
    normed_part, small, ffn_pair, heads_pair,
    streams, all_tokens, normed, projected, w_all, out_own, grad_heads, ffn_sum, f_one_a, f_one_b, f_two_a, f_two_b, f_three_a, f_three_b, o_one, o_two, o_three, out_part,
    key_grad, value_grad, key_turned, grad_stream, raw_conv, raw_qkv, qkv_low, qkv_half, q_one, q_two, gain_one,
    pair_out, pair_in, send_sem, recv_sem, local_sem,
):
    x, y, z, core = place()
    here = {"x": x, "y": y, "z": z}
    sems = (send_sem, recv_sem)
    sibling = device(x, y, z, 1 - core)
    along = neighbours(x, y, z, core)
    count = Counter()
    f_one, f_two, f_three = (f_one_a, f_one_b), (f_two_a, f_two_b), (f_three_a, f_three_b)

    def go(source, target, other):
        return send(source, target, sems, count.take(), other)

    def to(axis, k):
        return (here[axis] + k) % 4

    loads = [
        pltpu.make_async_copy(far, near, local_sem.at[number])
        for number, (far, near) in enumerate(
            (
                (streams_far, streams),
                (all_tokens_far, all_tokens),
                (normed_far, normed),
                (projected_far, projected),
                (w_all_far, w_all),
                (raw_out.at[y], out_own),
            )
        )
    ]
    for load in loads:
        load.start()
    greet([sibling] + along["x"] + along["y"] + along["z"])
    turned = [go(grad_rows.at[to("y", k)], grad_heads.at[y], along["y"][k - 1]) for k in (1, 2, 3)]
    stage_one = []
    for number, (order, c, w) in enumerate(RS_PARTS):
        for k in (1, 2, 3):
            index = cell(here, order[1:], {order[0]: to(order[0], k)})
            stage_one.append(
                go(
                    ffn_part.at[index + (slice(None), slice(c, c + w))],
                    f_one[number].at[k - 1],
                    along[order[0]][k - 1],
                )
            )
    kept = pltpu.make_async_copy(ffn_part, ffn_sum, local_sem.at[6])
    kept.start()
    grad_heads[y] = grad_rows[y]
    key_grad[...] = jnp.zeros_like(key_grad)
    value_grad[...] = jnp.zeros_like(value_grad)
    raw_conv[...] = jnp.zeros_like(raw_conv)
    raw_qkv[...] = jnp.zeros_like(raw_qkv)
    grad_stream[:, SEQ : SEQ + 8, :] = jnp.zeros((3, 8, GROUP), jnp.float32)
    loads[0].wait()
    for head in range(GROUP_HEADS):
        key_turned[head] = streams[GROUP_HEADS + head].T
    key_ids = lax.broadcasted_iota(jnp.int32, (SEQ, 1), 0)
    bias = jnp.where(key_ids < length[0], 0.0, NEG_FILL)
    upper = (
        lax.broadcasted_iota(jnp.int32, (QUARTER, QUARTER), 0)
        <= lax.broadcasted_iota(jnp.int32, (QUARTER, QUARTER), 1)
    )
    wait_all(loads[1:])
    wait_all(turned)
    out_one = [go(raw_out.at[to("y", k)], o_one.at[k - 1], along["y"][k - 1]) for k in (1, 2, 3)]

    def attend_back(i):
        rows_i = slice(i * QUARTER, (i + 1) * QUARTER)
        keys = (i + 1) * QUARTER
        grads = grad_heads[i]
        query_pieces = []
        for head in range(GROUP_HEADS):
            query = streams[head, rows_i, :]
            upstream = grads[:, head * HEAD_DIM : (head + 1) * HEAD_DIM]
            scores = mul(streams[GROUP_HEADS + head, :keys, :], query, NT) + (
                bias[:keys] - lse[head, :, rows_i]
            )
            corner = jnp.where(upper, scores[keys - QUARTER :], NEG_FILL)
            scores = corner if i == 0 else jnp.concatenate([scores[: keys - QUARTER], corner], 0)
            probs = jnp.exp(scores)
            prob_grad = mul(streams[2 * GROUP_HEADS + head, :keys, :], upstream, NT)
            centre = jnp.sum(prob_grad * probs, axis=0, keepdims=True)
            score_grad = (probs * (prob_grad - centre)).astype(jnp.bfloat16)
            query_pieces.append((mul(key_turned[head, :, :keys], score_grad) * SCALE).T)
            key_grad[head, :keys, :] += mul(score_grad, query)
            value_grad[head, :keys, :] += mul(probs.astype(jnp.bfloat16), upstream)
        for kind, pieces in (
            (0, query_pieces),
            (1, [key_grad[head, rows_i, :] for head in range(GROUP_HEADS)]),
            (2, [value_grad[head, rows_i, :] for head in range(GROUP_HEADS)]),
        ):
            grad_stream[kind, rows_i, :] = (
                jnp.concatenate(pieces, axis=1).astype(jnp.bfloat16).astype(jnp.float32)
            )
        normed_turned = normed[i].T
        total = None
        for kind in range(3):
            block = projected[kind, 8 + i * QUARTER : 8 + (i + 1) * QUARTER, :]
            summed = None
            for t in range(KW):
                shifted = grad_stream[kind, i * QUARTER + t : (i + 1) * QUARTER + t, :]
                term = taps[t, kind : kind + 1] * shifted
                summed = term if summed is None else summed + term
                raw_conv[t, kind : kind + 1, :] += jnp.sum(shifted * block, axis=0, keepdims=True)
            lower = summed.astype(jnp.bfloat16)
            raw_qkv[kind] += mul(normed_turned, lower)
            term = mul(lower, w_all[kind].reshape(D, GROUP), NT)
            total = term if total is None else total + term
        normed_part[i] = total.astype(jnp.bfloat16)
        term = jnp.sum(total * unit_rows(all_tokens[i])[0], axis=0, keepdims=True)
        gain_one[...] = term if i == 3 else gain_one[...] + term

    def part_cell(order, fixed, moved):
        free = [a for a in "yxz" if a not in fixed]
        return cell(here, free, moved)

    attend_back(3)
    kept.wait()
    wait_all(stage_one)
    stage_two = []
    for number, (order, c, w) in enumerate(RS_PARTS):
        for step in range(4):
            free = [a for a in "yxz" if a in order[1:]]
            index = cell(here, free[1:], {free[0]: step}) + (slice(None), slice(c, c + w))
            ffn_sum[index] = (
                ffn_sum[index].astype(jnp.float32)
                + f_one[number][0, step].astype(jnp.float32)
                + f_one[number][1, step].astype(jnp.float32)
                + f_one[number][2, step].astype(jnp.float32)
            ).astype(jnp.bfloat16)
        for k in (1, 2, 3):
            index = cell(here, order[2], {order[1]: to(order[1], k)})
            stage_two.append(
                go(
                    ffn_sum.at[index + (slice(None), slice(c, c + w))],
                    f_two[number].at[k - 1],
                    along[order[1]][k - 1],
                )
            )
    attend_back(2)
    wait_all(stage_two)
    stage_three = []
    for number, (order, c, w) in enumerate(RS_PARTS):
        index = cell(here, order[2]) + (slice(None), slice(c, c + w))
        ffn_sum[index] = (
            ffn_sum[index].astype(jnp.float32)
            + f_two[number][0].astype(jnp.float32)
            + f_two[number][1].astype(jnp.float32)
            + f_two[number][2].astype(jnp.float32)
        ).astype(jnp.bfloat16)
        for k in (1, 2, 3):
            index = cell(here, "", {order[2]: to(order[2], k)})
            stage_three.append(
                go(
                    ffn_sum.at[index + (slice(None), slice(c, c + w))],
                    f_three[number].at[k - 1],
                    along[order[2]][k - 1],
                )
            )
    attend_back(1)
    wait_all(out_one)
    out_part[...] = (
        out_own[...].astype(jnp.float32)
        + o_one[0].astype(jnp.float32)
        + o_one[1].astype(jnp.float32)
        + o_one[2].astype(jnp.float32)
    ).astype(jnp.bfloat16)
    out_two = [go(out_part.at[to("x", k)], o_two.at[k - 1], along["x"][k - 1]) for k in (1, 2, 3)]
    attend_back(0)
    qkv_low[...] = raw_qkv[...].reshape(3, 4, 4, PAIR, GROUP).astype(jnp.bfloat16)

    def qkv_copies(axis):
        copies = []
        for k in (1, 2, 3):
            place_of = (slice(None), to("x", k)) if axis == "x" else (slice(None), slice(None), to("z", k))
            copies.append(
                pltpu.make_async_remote_copy(
                    src_ref=qkv_low.at[place_of], dst_ref=q_one.at[k - 1],
                    send_sem=send_sem.at[70 + k], recv_sem=recv_sem.at[70 + k],
                    device_id=along[axis][k - 1], device_id_type=MESH_IDS,
                )
            )
        return copies

    for number, axis in enumerate("xz"):

        @pl.when(core == number)
        def _():
            for copy in qkv_copies(axis):
                copy.start()

    wait_all(out_two)
    out_part[x] = (
        out_part[x].astype(jnp.float32)
        + o_two[0].astype(jnp.float32)
        + o_two[1].astype(jnp.float32)
        + o_two[2].astype(jnp.float32)
    ).astype(jnp.bfloat16)
    out_three = [
        go(out_part.at[x, to("z", k)], o_three.at[k - 1], along["z"][k - 1]) for k in (1, 2, 3)
    ]
    wait_all(stage_three)
    for number, (order, c, w) in enumerate(RS_PARTS):
        index = cell(here, "") + (slice(None), slice(c, c + w))
        ffn_pair[:, c : c + w] = (
            ffn_sum[index].astype(jnp.float32)
            + f_three[number][0].astype(jnp.float32)
            + f_three[number][1].astype(jnp.float32)
            + f_three[number][2].astype(jnp.float32)
        )
    wait_all(out_three)
    pair_out[3] = (
        out_part[x, z].astype(jnp.float32)
        + o_three[0].astype(jnp.float32)
        + o_three[1].astype(jnp.float32)
        + o_three[2].astype(jnp.float32)
    )
    for number, axis in enumerate("xz"):
        other_axis = "zx"[number]

        @pl.when(core == number)
        def _():
            wait_all(qkv_copies(axis))
            at = (slice(None), x) if axis == "x" else (slice(None), slice(None), z)
            qkv_half[...] = (
                qkv_low[at].astype(jnp.float32)
                + q_one[0].astype(jnp.float32)
                + q_one[1].astype(jnp.float32)
                + q_one[2].astype(jnp.float32)
            ).astype(jnp.bfloat16)
            copies = [
                pltpu.make_async_remote_copy(
                    src_ref=qkv_half.at[:, to(other_axis, k)], dst_ref=q_two.at[k - 1],
                    send_sem=send_sem.at[74 + k], recv_sem=recv_sem.at[74 + k],
                    device_id=along[other_axis][k - 1], device_id_type=MESH_IDS,
                )
                for k in (1, 2, 3)
            ]
            for copy in copies:
                copy.start()
            wait_all(copies)
            pair_out[0:3] = (
                qkv_half[:, here[other_axis]].astype(jnp.float32)
                + q_two[0].astype(jnp.float32)
                + q_two[1].astype(jnp.float32)
                + q_two[2].astype(jnp.float32)
            )

    pair = go(pair_out, pair_in, sibling)
    small[...] = jnp.zeros_like(small)
    for row, gain in enumerate((gain_one[...], gain_two[...])):
        for group in range(4):
            small[4 * row + group : 4 * row + group + 1, :] = gain[
                :, group * GROUP : (group + 1) * GROUP
            ]
    for t in range(KW):
        small[8 + 3 * t : 11 + 3 * t, :] = raw_conv[t, 0:3, :]
    pair.wait()
    heads_pair[...] = pair_out[...] + pair_in[...]


RS_PARTS = (("xzy", 0, 384), ("zxy", 384, 384))


def backward(length, taps, lse, grad_rows, gain_two, streams, all_tokens, normed, projected, w_all, raw_out, ffn_part):
    f32, b16 = jnp.float32, jnp.bfloat16
    vmem = pl.BlockSpec(memory_space=pltpu.VMEM)
    scratch = [
        pltpu.VMEM((3 * GROUP_HEADS, SEQ, HEAD_DIM), b16),
        pltpu.VMEM((4, QUARTER, D), b16),
        pltpu.VMEM((4, QUARTER, D), b16),
        pltpu.VMEM((3, SEQ + 8, GROUP), f32),
        pltpu.VMEM((4, 4, 4, PAIR, GROUP), b16),
        pltpu.VMEM((4, 4, PAIR, GROUP), b16),
        pltpu.VMEM((4, QUARTER, GROUP), b16),
        pltpu.VMEM((4, 4, 4, PAIR, D), b16),
    ]
    scratch += [pltpu.VMEM((3, 4, 4, PAIR, w), b16) for _, _, w in RS_PARTS]
    scratch += [pltpu.VMEM((3, 4, PAIR, w), b16) for _, _, w in RS_PARTS]
    scratch += [pltpu.VMEM((3, PAIR, w), b16) for _, _, w in RS_PARTS]
    scratch += [
        pltpu.VMEM((3, 4, 4, PAIR, GROUP), b16),
        pltpu.VMEM((3, 4, PAIR, GROUP), b16),
        pltpu.VMEM((3, PAIR, GROUP), b16),
        pltpu.VMEM((4, 4, PAIR, GROUP), b16),
        pltpu.VMEM((GROUP_HEADS, SEQ, HEAD_DIM), f32),
        pltpu.VMEM((GROUP_HEADS, SEQ, HEAD_DIM), f32),
        pltpu.VMEM((GROUP_HEADS, HEAD_DIM, SEQ), b16),
        pltpu.VMEM((3, SEQ + 8, GROUP), f32),
        pltpu.VMEM((KW, 8, GROUP), f32),
        pltpu.VMEM((3, D, GROUP), f32),
        pltpu.VMEM((3, 4, 4, PAIR, GROUP), b16),
        pltpu.VMEM((3, 4, PAIR, GROUP), b16),
        pltpu.VMEM((3, 3, 4, PAIR, GROUP), b16),
        pltpu.VMEM((3, 3, PAIR, GROUP), b16),
        pltpu.VMEM((1, D), f32),
        pltpu.VMEM((4, PAIR, GROUP), f32),
        pltpu.VMEM((4, PAIR, GROUP), f32),
        pltpu.SemaphoreType.DMA((88,)),
        pltpu.SemaphoreType.DMA((88,)),
        pltpu.SemaphoreType.DMA((8,)),
    ]
    return pl.pallas_call(
        backward_kernel,
        out_shape=[
            jax.ShapeDtypeStruct((4, QUARTER, D), b16),
            jax.ShapeDtypeStruct((SMALL, GROUP), f32),
            jax.ShapeDtypeStruct((PAIR, D), f32),
            jax.ShapeDtypeStruct((4, PAIR, GROUP), f32),
        ],
        in_specs=[pl.BlockSpec(memory_space=pltpu.SMEM)]
        + [vmem] * 4
        + [pl.BlockSpec(memory_space=pl.ANY)] * 7,
        out_specs=[vmem] * 4,
        scratch_shapes=scratch,
        name="attend_back_and_scatter",
        compiler_params=pltpu.CompilerParams(
            collective_id=3, has_side_effects=True, vmem_limit_bytes=60 * 2**20
        ),
    )(length, taps, lse, grad_rows, gain_two, streams, all_tokens, normed, projected, w_all, raw_out, ffn_part)


UPPER = ((0, 0), (0, 1), (0, 2), (1, 1), (1, 2), (2, 2))
SUM_PARTS = ("xzy", "zyx", "yxz")
SMALL = 24


def adam(weight, gradient, moment_one, moment_two):
    first_new = BETA_ONE * moment_one + (1.0 - BETA_ONE) * gradient
    second_new = BETA_TWO * moment_two + (1.0 - BETA_TWO) * gradient * gradient
    stepped = (
        first_new
        / (1.0 - BETA_ONE**STEP)
        / (jnp.sqrt(second_new / (1.0 - BETA_TWO**STEP)) + ADAM_EPS)
    )
    return first_new, second_new, weight - ADAM_RATE * stepped


def tile(i):
    return slice(i * BLK, (i + 1) * BLK)


def optimizer_kernel(
    g_pair, g_heads, small, normed_part, m_ffn, m_qkv, m_out,
    wide, g_mine, o_ffn, o_heads, normed_in,
    m_heads, m_in, mh_in, s_core, s_x, s_z, s_y, iterate, head_iterate,
    part, gathered, r_one, r_two, r_three, hpart, hsum, hr_one, hr_two,
    g_high, g_low, z_high, z_low, t_high, t_low, gram, hgram,
    send_sem, recv_sem,
):
    x, y, z, core = place()
    here = {"x": x, "y": y, "z": z}
    sems = (send_sem, recv_sem)
    sibling = device(x, y, z, 1 - core)
    along = neighbours(x, y, z, core)
    count = Counter()

    def go(source, target, other):
        return send(source, target, sems, count.take(), other)

    def to(axis, k):
        return (here[axis] + k) % 4

    own_rows = rows(core * SUB, SUB)
    their_rows = rows((1 - core) * SUB, SUB)
    m_heads[0:3] = m_qkv[...]
    m_heads[3] = m_out[...].T
    mine = g_heads[pl.ds(2 * core, 2)]
    lanes = jnp.sum(g_pair[...] * g_pair[...], axis=0, keepdims=True)
    squares = jnp.sum(jnp.sum(mine * mine, axis=0), axis=0, keepdims=True)
    for group in range(4):
        squares = squares + lanes[:, group * GROUP : (group + 1) * GROUP]
    row_ids = lax.broadcasted_iota(jnp.int32, (SMALL, GROUP), 0)
    s_core[core] = small[...] + jnp.where(row_ids == 17, squares, 0.0)
    greet([sibling] + along["x"] + along["y"] + along["z"])
    chip = go(s_core.at[core], s_core.at[core], sibling)
    swaps = [
        go(g_pair.at[their_rows], g_mine.at[core], sibling),
        go(m_ffn.at[1 - core], m_in, sibling),
        go(m_heads.at[pl.ds(2 - 2 * core, 2)], mh_in, sibling),
    ]
    g_mine[core] = g_pair[own_rows, :]
    chip.wait()
    total = s_core[0] + s_core[1]
    for slots, axis in ((s_x, "x"), (s_z, "z")):
        at = here[axis]
        slots[at] = total
        wait_all([go(slots.at[at], slots.at[at], other) for other in along[axis]])
        total = (slots[0] + slots[1]) + (slots[2] + slots[3])
    s_y[y] = total
    wait_all([go(s_y.at[y], s_y.at[y], other) for other in along["y"]])
    total = (s_y[0] + s_y[1]) + (s_y[2] + s_y[3])
    for group in range(4):
        lanes_of = slice(group * GROUP, (group + 1) * GROUP)
        for row in range(2):
            wide[row : row + 1, lanes_of] = total[4 * row + group : 4 * row + group + 1, :]
        wide[2:11, lanes_of] = s_y[group, 8:17, :]
    gain_sum = wide[0:2, :]
    conv_sum = wide[2:11, :]
    squared = (
        jnp.sum(gain_sum * gain_sum, axis=(0, 1), keepdims=True)
        + jnp.sum(conv_sum * conv_sum, axis=(0, 1), keepdims=True)
        + jnp.sum(total[17:18, :], axis=(0, 1), keepdims=True)
    )
    norm = jnp.sqrt(squared)
    wide[11:16, :] = jnp.broadcast_to(norm, (5, D))
    factor = CLIP_NORM / jnp.maximum(norm, CLIP_NORM)
    wait_all(swaps)
    for at, momentum in ((own_rows, m_ffn[core]), (their_rows, m_in[...])):
        iterate[at, :] = MOMENTUM * momentum + factor * g_pair[at, :]
    for kind in range(2):
        for at, momentum in ((own_rows, m_heads[2 * core + kind]), (their_rows, mh_in[kind])):
            head_iterate[kind, at, :] = MOMENTUM * momentum + factor * g_heads[2 * core + kind, at, :]
    transposed = (((0,), (0,)), ((), ()))
    for number, (i, j) in enumerate(UPPER):
        part[tile(number), :] = product(
            split(iterate[:, tile(i)]), split(iterate[:, tile(j)]), transposed
        )
    h_rows = lax.broadcasted_iota(jnp.int32, (GROUP, GROUP), 0)
    h_cols = lax.broadcasted_iota(jnp.int32, (GROUP, GROUP), 1)
    same = h_rows // HEAD_DIM == h_cols // HEAD_DIM
    h_eye = (h_rows == h_cols).astype(jnp.float32)
    packed = []
    for kind in range(2):
        pieces = split(head_iterate[kind])
        full = jnp.where(same, product(pieces, pieces, transposed), 0.0)
        folded = full[:, :HEAD_DIM]
        for head in range(1, GROUP_HEADS):
            folded = folded + full[:, head * HEAD_DIM : (head + 1) * HEAD_DIM]
        packed.append(folded)
    hpart[GROUP:, :] = jnp.zeros((BLK - GROUP, 2 * HEAD_DIM), jnp.float32)
    hpart[:GROUP, :] = jnp.concatenate(packed, axis=1)
    one = x + core * (z - x)
    two = z + core * (x - z)
    h_first = [device(x + k * (1 - core), y, z + k * core, core) for k in (1, 2, 3)]
    h_second = [device(x + k * core, y, z + k * (1 - core), core) for k in (1, 2, 3)]
    third = 6 * BLK // 3
    sizes = (third // 4, third // 16, third // 64)
    h_sizes = (BLK // 4, BLK // 16)
    bases = [number * third for number in range(3)]
    h_base = 0
    for stage, slots in enumerate((r_one, r_two, r_three)):
        size = sizes[stage]
        copies = [
            go(
                part.at[rows(bases[number] + to(order[stage], k) * size, size)],
                slots.at[number, k - 1],
                along[order[stage]][k - 1],
            )
            for number, order in enumerate(SUM_PARTS)
            for k in (1, 2, 3)
        ]
        if stage < 2:
            h_size, h_here = h_sizes[stage], (one, two)[stage]
            h_slots, h_others = ((hr_one, h_first), (hr_two, h_second))[stage]
            copies += [
                go(
                    hpart.at[rows(h_base + (h_here + k) % 4 * h_size, h_size)],
                    h_slots.at[k - 1],
                    h_others[k - 1],
                )
                for k in (1, 2, 3)
            ]
        wait_all(copies)
        target = gathered if stage == 2 else part
        for number, order in enumerate(SUM_PARTS):
            bases[number] = bases[number] + here[order[stage]] * size
            at = rows(bases[number], size)
            target[at, :] = part[at, :] + (
                (slots[number, 0] + slots[number, 1]) + slots[number, 2]
            )
        if stage < 2:
            h_base = h_base + h_here * h_size
            at = rows(h_base, h_size)
            (hsum if stage == 1 else hpart)[at, :] = hpart[at, :] + (
                (h_slots[0] + h_slots[1]) + h_slots[2]
            )
    for stage in (2, 1, 0):
        size = sizes[stage]
        copies = []
        for number, order in enumerate(SUM_PARTS):
            region = gathered.at[rows(bases[number], size)]
            copies += [go(region, region, other) for other in along[order[stage]]]
            bases[number] = bases[number] - here[order[stage]] * size
        if stage < 2:
            region = hsum.at[rows(h_base, h_sizes[stage])]
            copies += [go(region, region, other) for other in (h_first, h_second)[stage]]
            h_base = h_base - (one, two)[stage] * h_sizes[stage]
        wait_all(copies)
    rows_out = [
        go(normed_part.at[to("y", k)], normed_in.at[k - 1], along["y"][k - 1]) for k in (1, 2, 3)
    ]
    normed_in[3] = normed_part[y]
    eye = (
        lax.broadcasted_iota(jnp.int32, (BLK, BLK), 0)
        == lax.broadcasted_iota(jnp.int32, (BLK, BLK), 1)
    ).astype(jnp.float32)
    trace = jnp.zeros((1, 1), jnp.float32)
    for number, (i, j) in enumerate(UPPER):
        if i == j:
            trace = trace + jnp.sum(gathered[tile(number), :] * eye, axis=(0, 1), keepdims=True)
    scale = 1.0 / (jnp.sqrt(trace) + NS_EPS)

    def keep(high, low, i, j, block):
        upper_pieces = split(block)
        for kept, piece in zip((high, low), upper_pieces):
            kept[tile(i), tile(j)] = piece
            if i != j:
                kept[tile(j), tile(i)] = piece.T

    def symmetric(left, right, use):
        number = 0
        for i in range(3):
            across = slice(i * BLK, D)
            row = product(
                (left[0][tile(i), :], left[1][tile(i), :]),
                (right[0][:, across], right[1][:, across]),
            )
            for j in range(i, 3):
                use(number, i, j, row[:, (j - i) * BLK : (j - i + 1) * BLK])
                number += 1

    for number, (i, j) in enumerate(UPPER):
        block = gathered[tile(number), :] * (scale * scale)
        gram[number] = block
        keep(g_high, g_low, i, j, block)
    iterate[...] = iterate[...] * scale
    for kind in range(2):
        folded = hsum[:GROUP, kind * HEAD_DIM : (kind + 1) * HEAD_DIM]
        full = jnp.where(same, jnp.concatenate([folded] * GROUP_HEADS, axis=1), 0.0)
        on_diagonal = full * h_eye
        by_column = jnp.sum(on_diagonal, axis=0, keepdims=True)
        by_row = jnp.sum(on_diagonal, axis=1, keepdims=True)
        trace_row = jnp.sum(jnp.where(same, by_column, 0.0), axis=1, keepdims=True)
        trace_column = jnp.sum(jnp.where(same, by_row, 0.0), axis=0, keepdims=True)
        scale_column = 1.0 / (jnp.sqrt(trace_column) + NS_EPS)
        scale_row = 1.0 / (jnp.sqrt(trace_row) + NS_EPS)
        hgram[kind] = full * scale_row * scale_column
        head_iterate[kind] = head_iterate[kind] * scale_column

    def sweep_heads(last):
        for kind in range(2):
            current = hgram[kind]
            pieces = split(current)
            poly = COEF_A * h_eye + COEF_B * current + COEF_C * product(pieces, pieces)
            poly_pieces = split(poly)
            head_iterate[kind] = product(split(head_iterate[kind]), poly_pieces)
            if not last:
                hgram[kind] = product(split(product(pieces, poly_pieces)), poly_pieces)

    def sweep(last):
        def use_square(number, i, j, block):
            poly = COEF_B * gram[number] + COEF_C * block
            keep(z_high, z_low, i, j, poly + COEF_A * eye if i == j else poly)

        def use_half(number, i, j, block):
            keep(t_high, t_low, i, j, block)

        def use_gram(number, i, j, block):
            gram[number] = block
            keep(g_high, g_low, i, j, block)

        symmetric((g_high, g_low), (g_high, g_low), use_square)
        sweep_heads(last)
        iterate[...] = product(split(iterate[...]), (z_high[...], z_low[...]))
        if not last:
            symmetric((g_high, g_low), (z_high, z_low), use_half)
            symmetric((t_high, t_low), (z_high, z_low), use_gram)

    def body(_, carry):
        sweep(False)
        return carry

    lax.fori_loop(0, NS_ITERS - 1, body, 0)
    sweep(True)
    copies = [go(iterate.at[their_rows], o_ffn.at[core], sibling)]
    for kind in range(2):
        copies.append(go(head_iterate.at[kind, their_rows], o_heads.at[2 * core + kind], sibling))
    o_ffn[core] = iterate[own_rows, :]
    for kind in range(2):
        o_heads[2 * core + kind] = head_iterate[kind, own_rows, :]
    wait_all(copies)
    wait_all(rows_out)


def optimizer(g_pair, g_heads, small, normed_part, *momenta):
    f32, b16 = jnp.float32, jnp.bfloat16
    vmem = pl.BlockSpec(memory_space=pltpu.VMEM)
    third = 6 * BLK // 3
    scratch = [
        pltpu.VMEM((4, SUB, GROUP), f32),
        pltpu.VMEM((SUB, D), f32),
        pltpu.VMEM((2, SUB, GROUP), f32),
        pltpu.VMEM((2, SMALL, GROUP), f32),
        pltpu.VMEM((4, SMALL, GROUP), f32),
        pltpu.VMEM((4, SMALL, GROUP), f32),
        pltpu.VMEM((4, SMALL, GROUP), f32),
        pltpu.VMEM((PAIR, D), f32),
        pltpu.VMEM((2, PAIR, GROUP), f32),
        pltpu.VMEM((6 * BLK, BLK), f32),
        pltpu.VMEM((6 * BLK, BLK), f32),
        pltpu.VMEM((3, 3, third // 4, BLK), f32),
        pltpu.VMEM((3, 3, third // 16, BLK), f32),
        pltpu.VMEM((3, 3, third // 64, BLK), f32),
        pltpu.VMEM((BLK, 2 * HEAD_DIM), f32),
        pltpu.VMEM((BLK, 2 * HEAD_DIM), f32),
        pltpu.VMEM((3, BLK // 4, 2 * HEAD_DIM), f32),
        pltpu.VMEM((3, BLK // 16, 2 * HEAD_DIM), f32),
    ]
    scratch += [pltpu.VMEM((D, D), b16)] * 6
    scratch += [
        pltpu.VMEM((6, BLK, BLK), f32),
        pltpu.VMEM((2, GROUP, GROUP), f32),
        pltpu.SemaphoreType.DMA((96,)),
        pltpu.SemaphoreType.DMA((96,)),
    ]
    return pl.pallas_call(
        optimizer_kernel,
        out_shape=[
            jax.ShapeDtypeStruct((16, D), f32),
            jax.ShapeDtypeStruct((2, SUB, D), f32),
            jax.ShapeDtypeStruct((2, SUB, D), f32),
            jax.ShapeDtypeStruct((4, SUB, GROUP), f32),
            jax.ShapeDtypeStruct((4, QUARTER, D), b16),
        ],
        in_specs=[vmem] * 7,
        out_specs=[vmem] * 5,
        scratch_shapes=scratch,
        name="optimizer",
        compiler_params=pltpu.CompilerParams(
            collective_id=0, has_side_effects=True, vmem_limit_bytes=48 * 2**20
        ),
    )(g_pair, g_heads, small, normed_part, *momenta)


def update_kernel(
    wide, g_ffn, g_heads, o_ffn, o_heads, normed_in, tokens, grad_middle, out_rows,
    m_ffn, m_qkv, m_out, w_ffn, w_qkv, w_out,
    gains, conv, gain_first, gain_second, conv_first, conv_second,
    output, input_grad, out_gains, out_conv, out_qkv, out_out, out_ffn, out_norm,
    new_m_qkv, new_m_out, new_m_ffn,
    new_gain_first, new_gain_second, new_conv_first, new_conv_second, new_gains, new_conv,
    new_qkv, new_out, new_ffn,
):
    core = lax.axis_index("dp") % 2
    output[...] = out_rows[...]
    grad = (
        normed_in[0].astype(jnp.float32)
        + normed_in[1].astype(jnp.float32)
        + normed_in[2].astype(jnp.float32)
        + normed_in[3].astype(jnp.float32)
    )
    unit, inverse = unit_rows(tokens[...])
    scaled = grad * gains[0:1]
    inner = jnp.mean(scaled * unit, axis=-1, keepdims=True)
    input_grad[...] = grad_middle[...] + inverse * (scaled - unit * inner)
    norm = wide[11:12, 0:1]
    out_norm[...] = norm
    factor = CLIP_NORM / jnp.maximum(norm, CLIP_NORM)
    grad = wide[0:2, :] * factor
    out_gains[...] = grad
    first, second, new = adam(gains[...], grad, gain_first[...], gain_second[...])
    new_gain_first[...], new_gain_second[...], new_gains[...] = first, second, new
    for t in range(KW):
        grad = wide[2 + 3 * t : 5 + 3 * t, :] * factor
        out_conv[t] = grad
        first, second, new = adam(conv[t], grad, conv_first[t], conv_second[t])
        new_conv_first[t], new_conv_second[t], new_conv[t] = first, second, new
    grad = g_ffn[...] * factor
    out_ffn[...] = grad
    new_m_ffn[...] = MOMENTUM * m_ffn[...] + grad
    new_ffn[...] = w_ffn[...] - RATE_IN * math.sqrt(max(FF, D)) * o_ffn[...]
    own_rows = rows(core * SUB, SUB)
    for kind in range(3):
        grad = g_heads[kind, own_rows, :] * factor
        out_qkv[kind] = grad
        new_m_qkv[kind] = MOMENTUM * m_qkv[kind] + grad
    new_qkv[...] = w_qkv[...] - RATE_IN * math.sqrt(D) * o_heads[0:3]
    grad = (g_heads[3, own_rows, :] * factor).T
    out_out[...] = grad
    new_m_out[...] = MOMENTUM * m_out[...] + grad
    new_out[...] = w_out[...] - RATE_OUT * math.sqrt(D) * o_heads[3].T


def update(*arrays):
    vmem = pl.BlockSpec(memory_space=pltpu.VMEM)
    m_ffn, m_qkv, m_out, _, _, _, gains, conv = arrays[9:17]
    rows_like = arrays[8]
    like = [rows_like, rows_like, gains, conv, m_qkv, m_out, m_ffn, None, m_qkv, m_out, m_ffn]
    like += [gains, gains, conv, conv, gains, conv, m_qkv, m_out, m_ffn]
    return pl.pallas_call(
        update_kernel,
        out_shape=[
            jax.ShapeDtypeStruct((1, 1) if entry is None else entry.shape, jnp.float32)
            for entry in like
        ],
        in_specs=[vmem] * len(arrays),
        out_specs=[vmem] * len(like),
        name="update",
        compiler_params=pltpu.CompilerParams(vmem_limit_bytes=48 * 2**20),
    )(*arrays)


def per_device(
    tokens,
    lengths,
    cotangent,
    gains,
    conv,
    w_qkv,
    w_out,
    ffn_weights,
    mom_qkv,
    mom_out,
    mom_ffn,
    gain_first,
    gain_second,
    conv_first,
    conv_second,
):
    head_at = lax.axis_index("head")
    rows_in = tokens[0]
    all_tokens, normed, streams, projected, lse, attended, w_all, wo_all, taps, ffn_all = forward(
        lengths, rows_in, gains, conv, w_qkv, w_out, ffn_weights
    )
    output, grad_middle, gain_two, grad_rows, raw_out, ffn_part = feed_forward(
        lengths - head_at * QUARTER,
        rows_in,
        cotangent[0],
        gains,
        attended,
        wo_all.reshape(4, D, GROUP),
        ffn_all.reshape(FF, D),
    )
    normed_part, small, ffn_pair, heads_pair = backward(
        lengths,
        taps,
        lse,
        grad_rows,
        gain_two,
        streams,
        all_tokens,
        normed,
        projected,
        w_all,
        raw_out.reshape(4, 4, 4, PAIR, GROUP),
        ffn_part.reshape(4, 4, 4, PAIR, D),
    )
    wide, g_ffn, o_ffn, o_heads, normed_in = optimizer(
        ffn_pair, heads_pair, small, normed_part, mom_ffn, mom_qkv, mom_out
    )
    updated = update(
        wide, g_ffn, heads_pair, o_ffn, o_heads, normed_in, rows_in, grad_middle, output,
        mom_ffn, mom_qkv, mom_out, ffn_weights, w_qkv, w_out,
        gains, conv, gain_first, gain_second, conv_first, conv_second,
    )
    return (updated[0][None], updated[1][None], *updated[2:7], updated[7][0, 0], *updated[8:])


def solution(mesh):
    placed = (
        P("dp", "head", None),
        P("dp"),
        P("dp", "head", None),
        P(),
        P(),
        P(None, "dp", "head"),
        P("head", "dp"),
        P(None, ("head", "dp"), None),
        P(None, "dp", "head"),
        P("head", "dp"),
        P(None, ("head", "dp"), None),
        P(),
        P(),
        P(),
        P(),
    )
    return jax.shard_map(
        per_device,
        mesh=mesh,
        in_specs=placed,
        out_specs=(
            P("dp", "head", None),
            P("dp", "head", None),
            P(),
            P(),
            P(None, "dp", "head"),
            P("head", "dp"),
            P(None, ("head", "dp"), None),
            P(),
            P(None, "dp", "head"),
            P("head", "dp"),
            P(None, ("head", "dp"), None),
            P(),
            P(),
            P(),
            P(),
            P(),
            P(),
            P(None, "dp", "head"),
            P("head", "dp"),
            P(None, ("head", "dp"), None),
        ),
        check_vma=False,
    )
```

```python
import math

import jax
import jax.numpy as jnp
from jax import lax
from jax.experimental import pallas as pl
from jax.experimental.pallas import tpu as pltpu
from jax.sharding import PartitionSpec as P

D = 768
HEADS = 12
HEAD_DIM = 64
FF = 3072
KW = 3
NS_ITERS = 5
STEP = 10


NORM_EPS = 1e-06
NEG_FILL = -1e30
CLIP_NORM = 1.0
MOMENTUM = 0.95
RATE_IN = 0.02
RATE_OUT = 0.15
ADAM_RATE = 0.5
BETA_ONE = 0.9
BETA_TWO = 0.999
ADAM_EPS = 1e-08
NS_EPS = 1e-07
COEF_A = 3.4445
COEF_B = -4.775
COEF_C = 2.0315


SUB = 24
PAIR = 2 * SUB
BLK = 256
MESH_IDS = pl.DeviceIdType.MESH


def place():
    flat = lax.axis_index("dp")
    return flat // 8, lax.axis_index("head"), (flat // 2) % 4, flat % 2


def device(x, y, z, core):
    return (y % 4, ((x % 4) * 4 + z % 4) * 2 + core)


def greet(others):
    barrier = pltpu.get_barrier_semaphore()
    for other in others:
        pl.semaphore_signal(barrier, inc=1, device_id=other, device_id_type=MESH_IDS)
    pl.semaphore_wait(barrier, len(others))


def send(source, target, sems, index, other):
    copy = pltpu.make_async_remote_copy(
        src_ref=source,
        dst_ref=target,
        send_sem=sems[0].at[index],
        recv_sem=sems[1].at[index],
        device_id=other,
        device_id_type=MESH_IDS,
    )
    copy.start()
    return copy


def rows(start, count):
    return pl.ds(pl.multiple_of(start, 8), count)


def split(values):
    high = values.astype(jnp.bfloat16)
    return high, (values - high.astype(jnp.float32)).astype(jnp.bfloat16)


def product(left, right, dims=(((1,), (0,)), ((), ()))):
    lh, ll = left
    rh, rl = right

    def dot(a, b):
        return lax.dot_general(a, b, dims, preferred_element_type=jnp.float32)

    return dot(lh, rh) + (dot(lh, rl) + dot(ll, rh))


SEQ = 1024
QUARTER = SEQ // 4
GROUP = D // 4
GROUP_HEADS = GROUP // HEAD_DIM
SCALE = HEAD_DIM ** (-0.5)
NT = (((1,), (1,)), ((), ()))
TN = (((0,), (0,)), ((), ()))
NN = (((1,), (0,)), ((), ()))
PARTS = (("yzx", 0, 384), ("yxz", 384, 384))
RS_PARTS = (("xzy", 0, 384), ("zxy", 384, 384))


def mul(a, b, dims=NN):
    return lax.dot_general(a, b, dims, preferred_element_type=jnp.float32)


def neighbours(x, y, z, core):
    return {
        "x": [device(x + k, y, z, core) for k in (1, 2, 3)],
        "y": [device(x, y + k, z, core) for k in (1, 2, 3)],
        "z": [device(x, y, z + k, core) for k in (1, 2, 3)],
    }


def cell(here, free, moved=None):
    moved = moved or {}
    return tuple(slice(None) if a in free else moved.get(a, here[a]) for a in "yxz")


class Counter:
    def __init__(self):
        self.count = 0

    def take(self, many=1):
        self.count += many
        return self.count - many


def wait_all(copies):
    for copy in copies:
        copy.wait()


def in_core_order(core, own, other):
    return jnp.concatenate(
        [jnp.where(core == 0, own, other), jnp.where(core == 0, other, own)], axis=-2
    )


def unit_rows(values):
    values = values.astype(jnp.float32)
    inverse = lax.rsqrt(jnp.mean(values * values, axis=-1, keepdims=True) + NORM_EPS)
    return values * inverse, inverse


def total_of(*pieces):
    total = pieces[0].astype(jnp.float32)
    for piece in pieces[1:]:
        total = total + piece.astype(jnp.float32)
    return total


def layer_kernel(
    length, tokens, cotangent_far, gains, conv, w_qkv, w_out, w_ffn_far,
    output_far, grad_middle_far, normed_part_far, small, ffn_pair, heads_pair,
    cotangent, w_ffn, output, grad_middle, normed_part, all_tokens, streams, projected, lse, taps, w_heads, swap_heads, swap_ffn, w_all, wo_all,
    attended, att_send, weights, raw_own, raw_send, raw_in, middle, normed_two, upstream,
    grad_rows, grad_heads, raw_out, f_one_a, f_one_b, f_two_a, f_two_b, f_three_a, f_three_b,
    o_one, o_two, o_three, out_part, key_grad, value_grad, key_turned, grad_stream, raw_conv,
    raw_qkv, qkv_low, qkv_half, q_one, q_two, gain_one, gain_two, pair_out, pair_in,
    send_sem, recv_sem, local_sem,
):
    x, y, z, core = place()
    here = {"x": x, "y": y, "z": z}
    sems = (send_sem, recv_sem)
    sibling = device(x, y, z, 1 - core)
    along = neighbours(x, y, z, core)
    count = Counter()
    f_one, f_two, f_three = (f_one_a, f_one_b), (f_two_a, f_two_b), (f_three_a, f_three_b)
    columns = [slice(c, c + w) for _, c, w in PARTS]

    def describe(source, target, number, other, number_there=None):
        return pltpu.make_async_remote_copy(
            src_ref=source,
            dst_ref=target,
            send_sem=send_sem.at[number],
            recv_sem=recv_sem.at[number if number_there is None else number_there],
            device_id=other,
            device_id_type=MESH_IDS,
        )

    def go(source, target, other):
        return send(source, target, sems, count.take(), other)

    def to(axis, k):
        return (here[axis] + k) % 4

    loads = [
        pltpu.make_async_copy(far, near, local_sem.at[6 + number])
        for number, (far, near) in enumerate(
            (
                (w_ffn_far, w_ffn),
                (w_qkv, w_heads.at[pl.ds(0, 3)]),
                (w_out, w_heads.at[3]),
                (tokens, all_tokens.at[y]),
                (cotangent_far, cotangent),
            )
        )
    ]
    for load in loads:
        load.start()
    greet([sibling] + along["x"] + along["y"] + along["z"])
    wait_all(loads)
    swaps = [
        go(w_ffn.at[1 - core], swap_ffn, sibling),
        go(w_heads.at[pl.ds(2 - 2 * core, 2)], swap_heads, sibling),
    ]
    for t in range(KW):
        taps[t] = sum(
            jnp.where(y == group, conv[t, :, group * GROUP : (group + 1) * GROUP], 0.0)
            for group in range(4)
        )
    wait_all(swaps)
    weights[core, y, x, z] = in_core_order(core, w_ffn[core], swap_ffn[...]).astype(jnp.bfloat16)
    kinds = pl.ds(2 * core, 2)
    w_all[kinds, x, z] = in_core_order(core, w_heads[kinds], swap_heads[...]).astype(jnp.bfloat16)
    ffn_one = []
    for (order, _, _), cols in zip(PARTS, columns):
        region = weights.at[core, y, x, z, :, cols]
        ffn_one += [go(region, region, other) for other in along[order[0]]]
    one = [device(x + k * (1 - core), y, z + k * core, core) for k in (1, 2, 3)]
    ahead, behind = along["y"][0], along["y"][2]
    spread = [go(all_tokens.at[y], all_tokens.at[y], other) for other in (ahead, behind)]
    heads_one = [go(w_all.at[kinds, x, z], w_all.at[kinds, x, z], other) for other in one]
    wait_all(heads_one)
    second = count.take(3)

    def heads_two(axis):
        at = (kinds, slice(None), z) if axis == "z" else (kinds, x)
        return [
            describe(w_all.at[at], w_all.at[at], second + k, along[axis][k]) for k in range(3)
        ]

    for number, axis in enumerate("zx"):

        @pl.when(core == number)
        def _():
            for copy in heads_two(axis):
                copy.start()

    wait_all(ffn_one)
    ffn_two = []
    for (order, _, _), cols in zip(PARTS, columns):
        region = weights.at[(core,) + cell(here, order[0]) + (slice(None), cols)]
        ffn_two += [go(region, region, other) for other in along[order[1]]]
    for number, axis in enumerate("zx"):

        @pl.when(core == number)
        def _():
            wait_all(heads_two(axis))

    heads_pair_copy = go(w_all.at[kinds], w_all.at[kinds], sibling)
    wait_all(ffn_two)
    ffn_three = []

    def last_hop():
        quarter = len(ffn_three)
        copies = []
        for (order, _, _), cols in zip(PARTS, columns):
            region = weights.at[
                (core,) + cell(here, order[1], {"y": quarter}) + (slice(None), cols)
            ]
            copies += [go(region, region, other) for other in along[order[2]]]
        ffn_three.append(copies)

    last_hop()
    last_hop()
    spread[0].wait()
    forwarded = [
        go(all_tokens.at[to("y", 3), pl.ds(0, 128)], all_tokens.at[to("y", 3), pl.ds(0, 128)], ahead)
    ]
    spread[1].wait()
    forwarded.append(
        go(all_tokens.at[to("y", 1), pl.ds(128, 128)], all_tokens.at[to("y", 1), pl.ds(128, 128)], behind)
    )
    heads_pair_copy.wait()
    half = pl.ds(2 * core, 2)
    wo_all[y] = w_all[3]
    projected[:, 0:8, :] = jnp.zeros((3, 8, GROUP), jnp.float32)
    key_ids = lax.broadcasted_iota(jnp.int32, (SEQ, 1), 0)
    bias = jnp.where(key_ids < length[0], 0.0, NEG_FILL)
    upper = (
        lax.broadcasted_iota(jnp.int32, (QUARTER, QUARTER), 0)
        <= lax.broadcasted_iota(jnp.int32, (QUARTER, QUARTER), 1)
    )

    def project(block):
        normed = (unit_rows(all_tokens[block])[0] * gains[0:1]).astype(jnp.bfloat16)
        for kind in range(3):
            projected[kind, rows(8 + block * QUARTER, QUARTER), :] = mul(
                normed, w_all[kind].reshape(D, GROUP)
            )

    def convolve(i):
        rows_i = slice(i * QUARTER, (i + 1) * QUARTER)
        for kind in range(3):
            base = 8 + i * QUARTER
            summed = taps[0, kind : kind + 1] * projected[kind, base : base + QUARTER, :]
            for t in range(1, KW):
                summed = summed + taps[t, kind : kind + 1] * projected[
                    kind, base - t : base - t + QUARTER, :
                ]
            stream = summed.astype(jnp.bfloat16)
            if kind == 0:
                stream = stream * jnp.bfloat16(SCALE)
            for head in range(GROUP_HEADS):
                streams[kind * GROUP_HEADS + head, rows_i, :] = stream[
                    :, head * HEAD_DIM : (head + 1) * HEAD_DIM
                ]

    for k in (0, 1, 3):
        project(to("y", k))
    wait_all(forwarded)
    wo_y = [go(w_all.at[3, half], wo_all.at[y, half], other) for other in along["y"]]
    project(to("y", 2))

    heads_send, heads_recv = count.take(4), count.take(4)

    def head_copy(i):
        return describe(
            att_send.at[i], attended.at[y], heads_send + i, device(x, i, z, core),
            heads_recv + (i - y + 3) % 4,
        )

    def attend(i):
        rows_i = slice(i * QUARTER, (i + 1) * QUARTER)
        keys = (i + 1) * QUARTER
        pieces = []
        for head in range(GROUP_HEADS):
            scores = mul(
                streams[GROUP_HEADS + head, :keys, :], streams[head, rows_i, :], NT
            ) + bias[:keys]
            corner = jnp.where(upper, scores[keys - QUARTER :], NEG_FILL)
            scores = corner if i == 0 else jnp.concatenate([scores[: keys - QUARTER], corner], 0)
            top = jnp.max(scores, axis=0, keepdims=True)
            lifted = jnp.exp(scores - top)
            total = jnp.sum(lifted, axis=0, keepdims=True)
            probs = (lifted * (1.0 / total)).astype(jnp.bfloat16)
            lse[head, :, rows_i] = top + jnp.log(total)
            pieces.append(mul(streams[2 * GROUP_HEADS + head, :keys, :], probs, TN).T)
        att_send[i] = jnp.concatenate(pieces, axis=1).astype(jnp.bfloat16)

        @pl.when(i != y)
        def _():
            head_copy(i).start()

    for i in range(4):
        convolve(i)
    attend(3)
    wait_all(wo_y)
    wo_pair = [
        go(wo_all.at[to("y", k), half], wo_all.at[to("y", k), half], sibling) for k in (1, 2, 3)
    ]
    pairing = []

    def pair_up(quarter):
        wait_all(ffn_three[quarter])
        pairing.append(go(weights.at[core, quarter], weights.at[core, quarter], sibling))

    pair_up(0)
    pair_up(1)
    last_hop()
    last_hop()
    attend(2)
    attend(1)
    attend(0)
    wait_all(wo_pair)
    attended[y] = att_send[y]
    for i in range(4):

        @pl.when(i != y)
        def _():
            head_copy(i).wait_send()

    for k in range(3):
        describe(
            att_send.at[0], attended.at[y], heads_send, along["y"][k], heads_recv + k
        ).wait_recv()

    mixed = all_tokens[y].astype(jnp.float32)
    for group in range(4):
        mixed = mixed + mul(attended[group], wo_all[group].reshape(D, GROUP), NT)
    middle[...] = mixed
    output[...] = mixed
    normed_two[...] = (unit_rows(mixed)[0] * gains[1:2]).astype(jnp.bfloat16)
    row_ids = lax.broadcasted_iota(jnp.int32, (QUARTER, 1), 0)
    real = row_ids + y * QUARTER < length[0]
    upstream[...] = jnp.where(real, cotangent[...].astype(jnp.float32), 0.0).astype(jnp.bfloat16)
    leaving = []
    stage_one = []
    right_own = jnp.where(core == 0, normed_two[...], upstream[...])
    right_other = jnp.where(core == 0, upstream[...], normed_two[...])

    def settle(quarter):
        leaving[quarter].wait()
        for step in range(4):
            raw_own[quarter, step] = total_of(
                raw_own[quarter, step], raw_in[quarter, step]
            ).astype(jnp.bfloat16)
        for number, ((order, _, _), cols) in enumerate(zip(RS_PARTS, columns)):
            for k in (1, 2, 3):
                index = cell(here, order[1], {"y": quarter, order[0]: to(order[0], k)})
                stage_one.append(
                    go(
                        raw_own.at[index + (slice(None), cols)],
                        f_one[number].at[k - 1, quarter],
                        along[order[0]][k - 1],
                    )
                )

    for quarter in range(4):
        pairing[quarter].wait()
        into = weights[0, quarter].reshape(D, D)
        back = weights[1, quarter].reshape(D, D)
        positive = jnp.maximum(mul(normed_two[...], into, NT), 0.0)
        active = (positive * positive).astype(jnp.bfloat16)
        grad_hidden = (mul(upstream[...], back, NT) * (2.0 * positive)).astype(jnp.bfloat16)
        output[...] += mul(active, back)
        grad_term = mul(grad_hidden, into)
        grad_middle[...] = grad_term if quarter == 0 else grad_middle[...] + grad_term
        left_own = jnp.where(core == 0, grad_hidden, active)
        left_other = jnp.where(core == 0, active, grad_hidden)
        shape = (4, 4, PAIR, D)
        raw_send[quarter % 2] = mul(left_other, right_other, TN).astype(jnp.bfloat16).reshape(shape)
        leaving.append(go(raw_send.at[quarter % 2], raw_in.at[quarter], sibling))
        raw_own[quarter] = mul(left_own, right_own, TN).astype(jnp.bfloat16).reshape(shape)
        if quarter < 2:
            pair_up(quarter + 2)
        if quarter >= 1:
            settle(quarter - 1)
    unit, inverse = unit_rows(middle[...])
    grad = grad_middle[...]
    gain_two[...] = jnp.sum(grad * unit, axis=0, keepdims=True)
    scaled = grad * gains[1:2]
    inner = jnp.mean(scaled * unit, axis=-1, keepdims=True)
    grad_all = jnp.where(real, cotangent[...].astype(jnp.float32), 0.0) + inverse * (
        scaled - unit * inner
    )
    grad_middle[...] = grad_all
    stores = []

    def store(near, far):
        copy = pltpu.make_async_copy(near, far, local_sem.at[len(stores)])
        copy.start()
        stores.append(copy)

    store(output, output_far)
    store(grad_middle, grad_middle_far)
    lower_rows = grad_all.astype(jnp.bfloat16)
    for group in range(4):
        grad_rows[group] = mul(lower_rows, wo_all[group].reshape(D, GROUP)).astype(jnp.bfloat16)

    turned = [go(grad_rows.at[to("y", k)], grad_heads.at[y], along["y"][k - 1]) for k in (1, 2, 3)]
    for group in range(4):
        raw_out[group] = (
            mul(lower_rows, attended[group], TN).astype(jnp.bfloat16).reshape(4, 4, PAIR, GROUP)
        )
    grad_heads[y] = grad_rows[y]
    key_grad[...] = jnp.zeros_like(key_grad)
    value_grad[...] = jnp.zeros_like(value_grad)
    raw_conv[...] = jnp.zeros_like(raw_conv)
    raw_qkv[...] = jnp.zeros_like(raw_qkv)
    grad_stream[:, 0:8, :] = jnp.zeros((3, 8, GROUP), jnp.float32)
    for head in range(GROUP_HEADS):
        key_turned[head] = streams[GROUP_HEADS + head].T
    settle(3)
    wait_all(turned)
    out_one = [go(raw_out.at[to("y", k)], o_one.at[k - 1], along["y"][k - 1]) for k in (1, 2, 3)]

    def attend_back(i):
        rows_i = slice(i * QUARTER, (i + 1) * QUARTER)
        keys = (i + 1) * QUARTER
        grads = grad_heads[i]
        query_pieces = []
        for head in range(GROUP_HEADS):
            query = streams[head, rows_i, :]
            upstream_rows = grads[:, head * HEAD_DIM : (head + 1) * HEAD_DIM]
            scores = mul(streams[GROUP_HEADS + head, :keys, :], query, NT) + (
                bias[:keys] - lse[head, :, rows_i]
            )
            corner = jnp.where(upper, scores[keys - QUARTER :], NEG_FILL)
            scores = corner if i == 0 else jnp.concatenate([scores[: keys - QUARTER], corner], 0)
            probs = jnp.exp(scores)
            prob_grad = mul(streams[2 * GROUP_HEADS + head, :keys, :], upstream_rows, NT)
            centre = jnp.sum(prob_grad * probs, axis=0, keepdims=True)
            score_grad = (probs * (prob_grad - centre)).astype(jnp.bfloat16)
            query_pieces.append((mul(key_turned[head, :, :keys], score_grad) * SCALE).T)
            key_grad[head, :keys, :] += mul(score_grad, query)
            value_grad[head, :keys, :] += mul(probs.astype(jnp.bfloat16), upstream_rows)
        grad_stream[:, QUARTER:, :] = grad_stream[:, 0:8, :]
        for kind, pieces in (
            (0, query_pieces),
            (1, [key_grad[head, rows_i, :] for head in range(GROUP_HEADS)]),
            (2, [value_grad[head, rows_i, :] for head in range(GROUP_HEADS)]),
        ):
            grad_stream[kind, 0:QUARTER, :] = (
                jnp.concatenate(pieces, axis=1).astype(jnp.bfloat16).astype(jnp.float32)
            )
        unit_i = unit_rows(all_tokens[i])[0]
        normed_turned = (unit_i * gains[0:1]).astype(jnp.bfloat16).T
        total = None
        for kind in range(3):
            block = projected[kind, 8 + i * QUARTER : 8 + (i + 1) * QUARTER, :]
            summed = None
            for t in range(KW):
                shifted = grad_stream[kind, t : QUARTER + t, :]
                term = taps[t, kind : kind + 1] * shifted
                summed = term if summed is None else summed + term
                raw_conv[t, kind : kind + 1, :] += jnp.sum(shifted * block, axis=0, keepdims=True)
            lower = summed.astype(jnp.bfloat16)
            raw_qkv[kind] += mul(normed_turned, lower)
            term = mul(lower, w_all[kind].reshape(D, GROUP), NT)
            total = term if total is None else total + term
        normed_part[i] = total.astype(jnp.bfloat16)
        store(normed_part.at[i], normed_part_far.at[i])
        term = jnp.sum(total * unit_i, axis=0, keepdims=True)
        gain_one[...] = term if i == 3 else gain_one[...] + term

    attend_back(3)
    wait_all(stage_one)
    stage_two = []
    for number, ((order, _, _), cols) in enumerate(zip(RS_PARTS, columns)):
        for quarter in range(4):
            index = cell(here, order[1], {"y": quarter}) + (slice(None), cols)
            raw_own[index] = total_of(
                raw_own[index], *(f_one[number][k, quarter] for k in range(3))
            ).astype(jnp.bfloat16)
        for k in (1, 2, 3):
            index = cell(here, order[2], {order[1]: to(order[1], k)})
            stage_two.append(
                go(
                    raw_own.at[index + (slice(None), cols)],
                    f_two[number].at[k - 1],
                    along[order[1]][k - 1],
                )
            )
    attend_back(2)
    wait_all(stage_two)
    stage_three = []
    for number, ((order, _, _), cols) in enumerate(zip(RS_PARTS, columns)):
        index = cell(here, order[2]) + (slice(None), cols)
        raw_own[index] = total_of(
            raw_own[index], *(f_two[number][k] for k in range(3))
        ).astype(jnp.bfloat16)
        for k in (1, 2, 3):
            index = cell(here, "", {order[2]: to(order[2], k)})
            stage_three.append(
                go(
                    raw_own.at[index + (slice(None), cols)],
                    f_three[number].at[k - 1],
                    along[order[2]][k - 1],
                )
            )
    wait_all(out_one)
    out_part[...] = total_of(raw_out[y], *(o_one[k] for k in range(3))).astype(jnp.bfloat16)
    out_two = [go(out_part.at[to("x", k)], o_two.at[k - 1], along["x"][k - 1]) for k in (1, 2, 3)]
    attend_back(1)
    wait_all(out_two)
    out_part[x] = total_of(out_part[x], *(o_two[k] for k in range(3))).astype(jnp.bfloat16)
    out_three = [
        go(out_part.at[x, to("z", k)], o_three.at[k - 1], along["z"][k - 1]) for k in (1, 2, 3)
    ]
    wait_all(stage_three)
    for number, cols in enumerate(columns):
        index = cell(here, "") + (slice(None), cols)
        ffn_pair[:, cols] = total_of(raw_own[index], *(f_three[number][k] for k in range(3)))
    attend_back(0)
    qkv_low[...] = raw_qkv[...].reshape(3, 4, 4, PAIR, GROUP).astype(jnp.bfloat16)
    first_hop, second_hop = count.take(3), count.take(3)

    def qkv_one(axis):
        copies = []
        for k in (1, 2, 3):
            at = (slice(None), to("x", k)) if axis == "x" else (slice(None), slice(None), to("z", k))
            copies.append(
                describe(qkv_low.at[at], q_one.at[k - 1], first_hop + k - 1, along[axis][k - 1])
            )
        return copies

    for number, axis in enumerate("xz"):

        @pl.when(core == number)
        def _():
            for copy in qkv_one(axis):
                copy.start()

    wait_all(out_three)
    pair_out[3] = total_of(out_part[x, z], *(o_three[k] for k in range(3)))
    small[...] = jnp.zeros_like(small)
    for row, gain in enumerate((gain_one[...], gain_two[...])):
        for group in range(4):
            small[4 * row + group : 4 * row + group + 1, :] = gain[
                :, group * GROUP : (group + 1) * GROUP
            ]
    for t in range(KW):
        small[8 + 3 * t : 11 + 3 * t, :] = raw_conv[t, 0:3, :]
    for number, axis in enumerate("xz"):
        other_axis = "zx"[number]

        @pl.when(core == number)
        def _():
            wait_all(qkv_one(axis))
            at = (slice(None), x) if axis == "x" else (slice(None), slice(None), z)
            qkv_half[...] = total_of(qkv_low[at], *(q_one[k] for k in range(3))).astype(jnp.bfloat16)
            copies = [
                describe(
                    qkv_half.at[:, to(other_axis, k)], q_two.at[k - 1], second_hop + k - 1,
                    along[other_axis][k - 1],
                )
                for k in (1, 2, 3)
            ]
            for copy in copies:
                copy.start()
            wait_all(copies)
            pair_out[0:3] = total_of(qkv_half[:, here[other_axis]], *(q_two[k] for k in range(3)))

    go(pair_out, pair_in, sibling).wait()
    heads_pair[...] = pair_out[...] + pair_in[...]
    wait_all(stores)


def layer(length, tokens, cotangent, gains, conv, w_qkv, w_out, w_ffn):
    f32, b16 = jnp.float32, jnp.bfloat16
    vmem = pl.BlockSpec(memory_space=pltpu.VMEM)
    far = pl.BlockSpec(memory_space=pl.ANY)
    blocks = (4, 4, PAIR)
    scratch = [
        pltpu.VMEM((QUARTER, D), b16),
        pltpu.VMEM((2, SUB, D), f32),
        pltpu.VMEM((QUARTER, D), f32),
        pltpu.VMEM((QUARTER, D), f32),
        pltpu.VMEM((4, QUARTER, D), b16),
        pltpu.VMEM((4, QUARTER, D), b16),
        pltpu.VMEM((3 * GROUP_HEADS, SEQ, HEAD_DIM), b16),
        pltpu.VMEM((3, SEQ + 8, GROUP), f32),
        pltpu.VMEM((GROUP_HEADS, 1, SEQ), f32),
        pltpu.VMEM((KW, 3, GROUP), f32),
        pltpu.VMEM((4, SUB, GROUP), f32),
        pltpu.VMEM((2, SUB, GROUP), f32),
        pltpu.VMEM((SUB, D), f32),
        pltpu.VMEM((4,) + blocks + (GROUP,), b16),
        pltpu.VMEM((4,) + blocks + (GROUP,), b16),
        pltpu.VMEM((4, QUARTER, GROUP), b16),
        pltpu.VMEM((4, QUARTER, GROUP), b16),
        pltpu.VMEM((2, 4) + blocks + (D,), b16),
        pltpu.VMEM((4,) + blocks + (D,), b16),
        pltpu.VMEM((2,) + blocks + (D,), b16),
        pltpu.VMEM((4,) + blocks + (D,), b16),
        pltpu.VMEM((QUARTER, D), f32),
        pltpu.VMEM((QUARTER, D), b16),
        pltpu.VMEM((QUARTER, D), b16),
        pltpu.VMEM((4, QUARTER, GROUP), b16),
        pltpu.VMEM((4, QUARTER, GROUP), b16),
        pltpu.VMEM((4,) + blocks + (GROUP,), b16),
    ]
    scratch += [pltpu.VMEM((3, 4, 4, PAIR, w), b16) for _, _, w in RS_PARTS]
    scratch += [pltpu.VMEM((3, 4, PAIR, w), b16) for _, _, w in RS_PARTS]
    scratch += [pltpu.VMEM((3, PAIR, w), b16) for _, _, w in RS_PARTS]
    scratch += [
        pltpu.VMEM((3,) + blocks + (GROUP,), b16),
        pltpu.VMEM((3, 4, PAIR, GROUP), b16),
        pltpu.VMEM((3, PAIR, GROUP), b16),
        pltpu.VMEM(blocks + (GROUP,), b16),
        pltpu.VMEM((GROUP_HEADS, SEQ, HEAD_DIM), f32),
        pltpu.VMEM((GROUP_HEADS, SEQ, HEAD_DIM), f32),
        pltpu.VMEM((GROUP_HEADS, HEAD_DIM, SEQ), b16),
        pltpu.VMEM((3, QUARTER + 8, GROUP), f32),
        pltpu.VMEM((KW, 8, GROUP), f32),
        pltpu.VMEM((3, D, GROUP), f32),
        pltpu.VMEM((3,) + blocks + (GROUP,), b16),
        pltpu.VMEM((3, 4, PAIR, GROUP), b16),
        pltpu.VMEM((3, 3, 4, PAIR, GROUP), b16),
        pltpu.VMEM((3, 3, PAIR, GROUP), b16),
        pltpu.VMEM((1, D), f32),
        pltpu.VMEM((1, D), f32),
        pltpu.VMEM((4, PAIR, GROUP), f32),
        pltpu.VMEM((4, PAIR, GROUP), f32),
        pltpu.SemaphoreType.DMA((160,)),
        pltpu.SemaphoreType.DMA((160,)),
        pltpu.SemaphoreType.DMA((11,)),
    ]
    return pl.pallas_call(
        layer_kernel,
        out_shape=[
            jax.ShapeDtypeStruct((QUARTER, D), f32),
            jax.ShapeDtypeStruct((QUARTER, D), f32),
            jax.ShapeDtypeStruct((4, QUARTER, D), b16),
            jax.ShapeDtypeStruct((SMALL, GROUP), f32),
            jax.ShapeDtypeStruct((PAIR, D), f32),
            jax.ShapeDtypeStruct((4, PAIR, GROUP), f32),
        ],
        in_specs=[pl.BlockSpec(memory_space=pltpu.SMEM)]
        + [far, far, vmem, vmem, far, far, far],
        out_specs=[pl.BlockSpec(memory_space=pl.ANY)] * 3 + [vmem] * 3,
        scratch_shapes=scratch,
        name="layer",
        compiler_params=pltpu.CompilerParams(
            collective_id=2, has_side_effects=True, vmem_limit_bytes=63 * 2**20
        ),
    )(length, tokens, cotangent, gains, conv, w_qkv, w_out, w_ffn)


UPPER = ((0, 0), (0, 1), (0, 2), (1, 1), (1, 2), (2, 2))
SUM_PARTS = ("xzy", "zyx", "yxz")
SMALL = 24


def adam(weight, gradient, moment_one, moment_two):
    first_new = BETA_ONE * moment_one + (1.0 - BETA_ONE) * gradient
    second_new = BETA_TWO * moment_two + (1.0 - BETA_TWO) * gradient * gradient
    stepped = (
        first_new
        / (1.0 - BETA_ONE**STEP)
        / (jnp.sqrt(second_new / (1.0 - BETA_TWO**STEP)) + ADAM_EPS)
    )
    return first_new, second_new, weight - ADAM_RATE * stepped


def tile(i):
    return slice(i * BLK, (i + 1) * BLK)


def optimizer_kernel(
    g_pair_far, g_heads_far, small_far, normed_part, m_ffn_far, m_qkv, m_out,
    wide, g_mine, o_ffn, o_heads, normed_in,
    g_pair, g_heads, small, m_ffn, m_heads, m_in, mh_in, s_core, s_x, s_z, s_y, iterate, head_iterate,
    part, gathered, r_one, r_two, r_three, hpart, hsum, hr_one, hr_two,
    g_high, g_low, z_high, z_low, t_high, t_low, gram, hgram,
    send_sem, recv_sem, local_sem,
):
    x, y, z, core = place()
    here = {"x": x, "y": y, "z": z}
    sems = (send_sem, recv_sem)
    sibling = device(x, y, z, 1 - core)
    along = neighbours(x, y, z, core)
    count = Counter()

    def go(source, target, other):
        return send(source, target, sems, count.take(), other)

    def to(axis, k):
        return (here[axis] + k) % 4

    own_rows = rows(core * SUB, SUB)
    their_rows = rows((1 - core) * SUB, SUB)
    loads = [
        pltpu.make_async_copy(far, near, local_sem.at[number])
        for number, (far, near) in enumerate(
            (
                (g_pair_far, g_pair),
                (g_heads_far, g_heads),
                (small_far, small),
                (m_ffn_far, m_ffn),
                (m_qkv, m_heads.at[pl.ds(0, 3)]),
                (m_out, m_heads.at[3]),
                (normed_part.at[y], normed_in.at[3]),
            )
        )
    ]
    for load in loads:
        load.start()
    greet([sibling] + along["x"] + along["y"] + along["z"])
    wait_all(loads)
    mine = g_heads[pl.ds(2 * core, 2)]
    lanes = jnp.sum(g_pair[...] * g_pair[...], axis=0, keepdims=True)
    squares = jnp.sum(jnp.sum(mine * mine, axis=0), axis=0, keepdims=True)
    for group in range(4):
        squares = squares + lanes[:, group * GROUP : (group + 1) * GROUP]
    row_ids = lax.broadcasted_iota(jnp.int32, (SMALL, GROUP), 0)
    s_core[core] = small[...] + jnp.where(row_ids == 17, squares, 0.0)
    chip = go(s_core.at[core], s_core.at[core], sibling)
    swaps = [
        go(g_pair.at[their_rows], g_mine.at[core], sibling),
        go(m_ffn.at[1 - core], m_in, sibling),
        go(m_heads.at[pl.ds(2 - 2 * core, 2)], mh_in, sibling),
    ]
    g_mine[core] = g_pair[own_rows, :]
    chip.wait()
    total = s_core[0] + s_core[1]
    for slots, axis in ((s_x, "x"), (s_z, "z")):
        at = here[axis]
        slots[at] = total
        wait_all([go(slots.at[at], slots.at[at], other) for other in along[axis]])
        total = (slots[0] + slots[1]) + (slots[2] + slots[3])
    s_y[y] = total
    wait_all([go(s_y.at[y], s_y.at[y], other) for other in along["y"]])
    total = (s_y[0] + s_y[1]) + (s_y[2] + s_y[3])
    for group in range(4):
        lanes_of = slice(group * GROUP, (group + 1) * GROUP)
        for row in range(2):
            wide[row : row + 1, lanes_of] = total[4 * row + group : 4 * row + group + 1, :]
        wide[2:11, lanes_of] = s_y[group, 8:17, :]
    gain_sum = wide[0:2, :]
    conv_sum = wide[2:11, :]
    squared = (
        jnp.sum(gain_sum * gain_sum, axis=(0, 1), keepdims=True)
        + jnp.sum(conv_sum * conv_sum, axis=(0, 1), keepdims=True)
        + jnp.sum(total[17:18, :], axis=(0, 1), keepdims=True)
    )
    norm = jnp.sqrt(squared)
    wide[11:16, :] = jnp.broadcast_to(norm, (5, D))
    factor = CLIP_NORM / jnp.maximum(norm, CLIP_NORM)
    wait_all(swaps)
    for at, momentum in ((own_rows, m_ffn[core]), (their_rows, m_in[...])):
        iterate[at, :] = MOMENTUM * momentum + factor * g_pair[at, :]
    for kind in range(2):
        for at, momentum in ((own_rows, m_heads[2 * core + kind]), (their_rows, mh_in[kind])):
            head_iterate[kind, at, :] = MOMENTUM * momentum + factor * g_heads[2 * core + kind, at, :]
    transposed = (((0,), (0,)), ((), ()))
    for number, (i, j) in enumerate(UPPER):
        part[tile(number), :] = product(
            split(iterate[:, tile(i)]), split(iterate[:, tile(j)]), transposed
        )
    h_rows = lax.broadcasted_iota(jnp.int32, (GROUP, GROUP), 0)
    h_cols = lax.broadcasted_iota(jnp.int32, (GROUP, GROUP), 1)
    same = h_rows // HEAD_DIM == h_cols // HEAD_DIM
    h_eye = (h_rows == h_cols).astype(jnp.float32)
    packed = []
    for kind in range(2):
        pieces = split(head_iterate[kind])
        full = jnp.where(same, product(pieces, pieces, transposed), 0.0)
        folded = full[:, :HEAD_DIM]
        for head in range(1, GROUP_HEADS):
            folded = folded + full[:, head * HEAD_DIM : (head + 1) * HEAD_DIM]
        packed.append(folded)
    hpart[GROUP:, :] = jnp.zeros((BLK - GROUP, 2 * HEAD_DIM), jnp.float32)
    hpart[:GROUP, :] = jnp.concatenate(packed, axis=1)
    one = x + core * (z - x)
    two = z + core * (x - z)
    h_first = [device(x + k * (1 - core), y, z + k * core, core) for k in (1, 2, 3)]
    h_second = [device(x + k * core, y, z + k * (1 - core), core) for k in (1, 2, 3)]
    third = 6 * BLK // 3
    sizes = (third // 4, third // 16, third // 64)
    h_sizes = (BLK // 4, BLK // 16)
    bases = [number * third for number in range(3)]
    h_base = 0
    for stage, slots in enumerate((r_one, r_two, r_three)):
        size = sizes[stage]
        copies = [
            go(
                part.at[rows(bases[number] + to(order[stage], k) * size, size)],
                slots.at[number, k - 1],
                along[order[stage]][k - 1],
            )
            for number, order in enumerate(SUM_PARTS)
            for k in (1, 2, 3)
        ]
        if stage < 2:
            h_size, h_here = h_sizes[stage], (one, two)[stage]
            h_slots, h_others = ((hr_one, h_first), (hr_two, h_second))[stage]
            copies += [
                go(
                    hpart.at[rows(h_base + (h_here + k) % 4 * h_size, h_size)],
                    h_slots.at[k - 1],
                    h_others[k - 1],
                )
                for k in (1, 2, 3)
            ]
        wait_all(copies)
        target = gathered if stage == 2 else part
        for number, order in enumerate(SUM_PARTS):
            bases[number] = bases[number] + here[order[stage]] * size
            at = rows(bases[number], size)
            target[at, :] = part[at, :] + (
                (slots[number, 0] + slots[number, 1]) + slots[number, 2]
            )
        if stage < 2:
            h_base = h_base + h_here * h_size
            at = rows(h_base, h_size)
            (hsum if stage == 1 else hpart)[at, :] = hpart[at, :] + (
                (h_slots[0] + h_slots[1]) + h_slots[2]
            )
    for stage in (2, 1, 0):
        size = sizes[stage]
        copies = []
        for number, order in enumerate(SUM_PARTS):
            region = gathered.at[rows(bases[number], size)]
            copies += [go(region, region, other) for other in along[order[stage]]]
            bases[number] = bases[number] - here[order[stage]] * size
        if stage < 2:
            region = hsum.at[rows(h_base, h_sizes[stage])]
            copies += [go(region, region, other) for other in (h_first, h_second)[stage]]
            h_base = h_base - (one, two)[stage] * h_sizes[stage]
        wait_all(copies)
    rows_out = [
        go(normed_part.at[to("y", k)], normed_in.at[k - 1], along["y"][k - 1]) for k in (1, 2, 3)
    ]
    eye = (
        lax.broadcasted_iota(jnp.int32, (BLK, BLK), 0)
        == lax.broadcasted_iota(jnp.int32, (BLK, BLK), 1)
    ).astype(jnp.float32)
    trace = jnp.zeros((1, 1), jnp.float32)
    for number, (i, j) in enumerate(UPPER):
        if i == j:
            trace = trace + jnp.sum(gathered[tile(number), :] * eye, axis=(0, 1), keepdims=True)
    scale = 1.0 / (jnp.sqrt(trace) + NS_EPS)

    def keep(high, low, i, j, block):
        upper_pieces = split(block)
        for kept, piece in zip((high, low), upper_pieces):
            kept[tile(i), tile(j)] = piece
            if i != j:
                kept[tile(j), tile(i)] = piece.T

    def symmetric(left, right, use):
        number = 0
        for i in range(3):
            across = slice(i * BLK, D)
            row = product(
                (left[0][tile(i), :], left[1][tile(i), :]),
                (right[0][:, across], right[1][:, across]),
            )
            for j in range(i, 3):
                use(number, i, j, row[:, (j - i) * BLK : (j - i + 1) * BLK])
                number += 1

    for number, (i, j) in enumerate(UPPER):
        block = gathered[tile(number), :] * (scale * scale)
        gram[number] = block
        keep(g_high, g_low, i, j, block)
    iterate[...] = iterate[...] * scale
    for kind in range(2):
        folded = hsum[:GROUP, kind * HEAD_DIM : (kind + 1) * HEAD_DIM]
        full = jnp.where(same, jnp.concatenate([folded] * GROUP_HEADS, axis=1), 0.0)
        on_diagonal = full * h_eye
        by_column = jnp.sum(on_diagonal, axis=0, keepdims=True)
        by_row = jnp.sum(on_diagonal, axis=1, keepdims=True)
        trace_row = jnp.sum(jnp.where(same, by_column, 0.0), axis=1, keepdims=True)
        trace_column = jnp.sum(jnp.where(same, by_row, 0.0), axis=0, keepdims=True)
        scale_column = 1.0 / (jnp.sqrt(trace_column) + NS_EPS)
        scale_row = 1.0 / (jnp.sqrt(trace_row) + NS_EPS)
        hgram[kind] = full * scale_row * scale_column
        head_iterate[kind] = head_iterate[kind] * scale_column

    def sweep_heads(last):
        for kind in range(2):
            current = hgram[kind]
            pieces = split(current)
            poly = COEF_A * h_eye + COEF_B * current + COEF_C * product(pieces, pieces)
            poly_pieces = split(poly)
            head_iterate[kind] = product(split(head_iterate[kind]), poly_pieces)
            if not last:
                hgram[kind] = product(split(product(pieces, poly_pieces)), poly_pieces)

    def sweep(last):
        def use_square(number, i, j, block):
            poly = COEF_B * gram[number] + COEF_C * block
            keep(z_high, z_low, i, j, poly + COEF_A * eye if i == j else poly)

        def use_half(number, i, j, block):
            keep(t_high, t_low, i, j, block)

        def use_gram(number, i, j, block):
            gram[number] = block
            keep(g_high, g_low, i, j, block)

        symmetric((g_high, g_low), (g_high, g_low), use_square)
        sweep_heads(last)
        iterate[...] = product(split(iterate[...]), (z_high[...], z_low[...]))
        if not last:
            symmetric((g_high, g_low), (z_high, z_low), use_half)
            symmetric((t_high, t_low), (z_high, z_low), use_gram)

    def body(_, carry):
        sweep(False)
        return carry

    lax.fori_loop(0, NS_ITERS - 1, body, 0)
    sweep(True)
    copies = [go(iterate.at[their_rows], o_ffn.at[core], sibling)]
    for kind in range(2):
        copies.append(go(head_iterate.at[kind, their_rows], o_heads.at[2 * core + kind], sibling))
    o_ffn[core] = iterate[own_rows, :]
    for kind in range(2):
        o_heads[2 * core + kind] = head_iterate[kind, own_rows, :]
    wait_all(copies)
    wait_all(rows_out)


def optimizer(g_pair, g_heads, small, normed_part, *momenta):
    f32, b16 = jnp.float32, jnp.bfloat16
    vmem = pl.BlockSpec(memory_space=pltpu.VMEM)
    third = 6 * BLK // 3
    scratch = [
        pltpu.VMEM((PAIR, D), f32),
        pltpu.VMEM((4, PAIR, GROUP), f32),
        pltpu.VMEM((SMALL, GROUP), f32),
        pltpu.VMEM((2, SUB, D), f32),
        pltpu.VMEM((4, SUB, GROUP), f32),
        pltpu.VMEM((SUB, D), f32),
        pltpu.VMEM((2, SUB, GROUP), f32),
        pltpu.VMEM((2, SMALL, GROUP), f32),
        pltpu.VMEM((4, SMALL, GROUP), f32),
        pltpu.VMEM((4, SMALL, GROUP), f32),
        pltpu.VMEM((4, SMALL, GROUP), f32),
        pltpu.VMEM((PAIR, D), f32),
        pltpu.VMEM((2, PAIR, GROUP), f32),
        pltpu.VMEM((6 * BLK, BLK), f32),
        pltpu.VMEM((6 * BLK, BLK), f32),
        pltpu.VMEM((3, 3, third // 4, BLK), f32),
        pltpu.VMEM((3, 3, third // 16, BLK), f32),
        pltpu.VMEM((3, 3, third // 64, BLK), f32),
        pltpu.VMEM((BLK, 2 * HEAD_DIM), f32),
        pltpu.VMEM((BLK, 2 * HEAD_DIM), f32),
        pltpu.VMEM((3, BLK // 4, 2 * HEAD_DIM), f32),
        pltpu.VMEM((3, BLK // 16, 2 * HEAD_DIM), f32),
    ]
    scratch += [pltpu.VMEM((D, D), b16)] * 6
    scratch += [
        pltpu.VMEM((6, BLK, BLK), f32),
        pltpu.VMEM((2, GROUP, GROUP), f32),
        pltpu.SemaphoreType.DMA((96,)),
        pltpu.SemaphoreType.DMA((96,)),
        pltpu.SemaphoreType.DMA((7,)),
    ]
    return pl.pallas_call(
        optimizer_kernel,
        out_shape=[
            jax.ShapeDtypeStruct((16, D), f32),
            jax.ShapeDtypeStruct((2, SUB, D), f32),
            jax.ShapeDtypeStruct((2, SUB, D), f32),
            jax.ShapeDtypeStruct((4, SUB, GROUP), f32),
            jax.ShapeDtypeStruct((4, QUARTER, D), b16),
        ],
        in_specs=[pl.BlockSpec(memory_space=pl.ANY)] * 7,
        out_specs=[vmem] * 5,
        scratch_shapes=scratch,
        name="optimizer",
        compiler_params=pltpu.CompilerParams(
            collective_id=0, has_side_effects=True, vmem_limit_bytes=63 * 2**20
        ),
    )(g_pair, g_heads, small, normed_part, *momenta)


def update_kernel(
    wide, g_ffn, g_heads, o_ffn, o_heads, normed_in, tokens, grad_middle, out_rows,
    m_ffn, m_qkv, m_out, w_ffn, w_qkv, w_out,
    gains, conv, gain_first, gain_second, conv_first, conv_second,
    output, input_grad, out_gains, out_conv, out_qkv, out_out, out_ffn, out_norm,
    new_m_qkv, new_m_out, new_m_ffn,
    new_gain_first, new_gain_second, new_conv_first, new_conv_second, new_gains, new_conv,
    new_qkv, new_out, new_ffn,
):
    core = lax.axis_index("dp") % 2
    output[...] = out_rows[...]
    grad = (
        normed_in[0].astype(jnp.float32)
        + normed_in[1].astype(jnp.float32)
        + normed_in[2].astype(jnp.float32)
        + normed_in[3].astype(jnp.float32)
    )
    unit, inverse = unit_rows(tokens[...])
    scaled = grad * gains[0:1]
    inner = jnp.mean(scaled * unit, axis=-1, keepdims=True)
    input_grad[...] = grad_middle[...] + inverse * (scaled - unit * inner)
    norm = wide[11:12, 0:1]
    out_norm[...] = norm
    factor = CLIP_NORM / jnp.maximum(norm, CLIP_NORM)
    grad = wide[0:2, :] * factor
    out_gains[...] = grad
    first, second, new = adam(gains[...], grad, gain_first[...], gain_second[...])
    new_gain_first[...], new_gain_second[...], new_gains[...] = first, second, new
    for t in range(KW):
        grad = wide[2 + 3 * t : 5 + 3 * t, :] * factor
        out_conv[t] = grad
        first, second, new = adam(conv[t], grad, conv_first[t], conv_second[t])
        new_conv_first[t], new_conv_second[t], new_conv[t] = first, second, new
    grad = g_ffn[...] * factor
    out_ffn[...] = grad
    new_m_ffn[...] = MOMENTUM * m_ffn[...] + grad
    new_ffn[...] = w_ffn[...] - RATE_IN * math.sqrt(max(FF, D)) * o_ffn[...]
    own_rows = rows(core * SUB, SUB)
    for kind in range(3):
        grad = g_heads[kind, own_rows, :] * factor
        out_qkv[kind] = grad
        new_m_qkv[kind] = MOMENTUM * m_qkv[kind] + grad
    new_qkv[...] = w_qkv[...] - RATE_IN * math.sqrt(D) * o_heads[0:3]
    grad = g_heads[3, own_rows, :] * factor
    out_out[...] = grad
    new_m_out[...] = MOMENTUM * m_out[...] + grad
    new_out[...] = w_out[...] - RATE_OUT * math.sqrt(D) * o_heads[3]


def update(*arrays):
    vmem = pl.BlockSpec(memory_space=pltpu.VMEM)
    m_ffn, m_qkv, m_out, _, _, _, gains, conv = arrays[9:17]
    rows_like = arrays[8]
    like = [rows_like, rows_like, gains, conv, m_qkv, m_out, m_ffn, None, m_qkv, m_out, m_ffn]
    like += [gains, gains, conv, conv, gains, conv, m_qkv, m_out, m_ffn]
    return pl.pallas_call(
        update_kernel,
        out_shape=[
            jax.ShapeDtypeStruct((1, 1) if entry is None else entry.shape, jnp.float32)
            for entry in like
        ],
        in_specs=[vmem] * len(arrays),
        out_specs=[vmem] * len(like),
        name="update",
        compiler_params=pltpu.CompilerParams(vmem_limit_bytes=63 * 2**20),
    )(*arrays)


def per_device(
    tokens,
    lengths,
    cotangent,
    gains,
    conv,
    w_qkv,
    w_out,
    ffn_weights,
    mom_qkv,
    mom_out,
    mom_ffn,
    gain_first,
    gain_second,
    conv_first,
    conv_second,
):
    rows_in = tokens[0]
    output, grad_middle, normed_part, small, ffn_pair, heads_pair = layer(
        lengths, rows_in, cotangent[0], gains, conv, w_qkv, w_out.T, ffn_weights
    )
    wide, g_ffn, o_ffn, o_heads, normed_in = optimizer(
        ffn_pair, heads_pair, small, normed_part, mom_ffn, mom_qkv, mom_out.T
    )
    updated = update(
        wide, g_ffn, heads_pair, o_ffn, o_heads, normed_in, rows_in, grad_middle, output,
        mom_ffn, mom_qkv, mom_out.T, ffn_weights, w_qkv, w_out.T,
        gains, conv, gain_first, gain_second, conv_first, conv_second,
    )
    updated = list(updated)
    for number in (5, 9, 18):
        updated[number] = updated[number].T
    return (updated[0][None], updated[1][None], *updated[2:7], updated[7][0, 0], *updated[8:])


def solution(mesh):
    placed = (
        P("dp", "head", None),
        P("dp"),
        P("dp", "head", None),
        P(),
        P(),
        P(None, "dp", "head"),
        P("head", "dp"),
        P(None, ("head", "dp"), None),
        P(None, "dp", "head"),
        P("head", "dp"),
        P(None, ("head", "dp"), None),
        P(),
        P(),
        P(),
        P(),
    )
    return jax.shard_map(
        per_device,
        mesh=mesh,
        in_specs=placed,
        out_specs=(
            P("dp", "head", None),
            P("dp", "head", None),
            P(),
            P(),
            P(None, "dp", "head"),
            P("head", "dp"),
            P(None, ("head", "dp"), None),
            P(),
            P(None, "dp", "head"),
            P("head", "dp"),
            P(None, ("head", "dp"), None),
            P(),
            P(),
            P(),
            P(),
            P(),
            P(),
            P(None, "dp", "head"),
            P("head", "dp"),
            P(None, ("head", "dp"), None),
        ),
        check_vma=False,
    )
```

```python
import math

import jax
import jax.numpy as jnp
from jax import lax
from jax.experimental import pallas as pl
from jax.experimental.pallas import tpu as pltpu
from jax.sharding import PartitionSpec as P

D = 768
HEADS = 12
HEAD_DIM = 64
FF = 3072
KW = 3
NS_ITERS = 5
STEP = 10


NORM_EPS = 1e-06
NEG_FILL = -1e30
CLIP_NORM = 1.0
MOMENTUM = 0.95
RATE_IN = 0.02
RATE_OUT = 0.15
ADAM_RATE = 0.5
BETA_ONE = 0.9
BETA_TWO = 0.999
ADAM_EPS = 1e-08
NS_EPS = 1e-07
COEF_A = 3.4445
COEF_B = -4.775
COEF_C = 2.0315


SUB = 24
PAIR = 2 * SUB
BLK = 256
MESH_IDS = pl.DeviceIdType.MESH


def place():
    flat = lax.axis_index("dp")
    return flat // 8, lax.axis_index("head"), (flat // 2) % 4, flat % 2


def device(x, y, z, core):
    return (y % 4, ((x % 4) * 4 + z % 4) * 2 + core)


def greet(others):
    barrier = pltpu.get_barrier_semaphore()
    for other in others:
        pl.semaphore_signal(barrier, inc=1, device_id=other, device_id_type=MESH_IDS)
    pl.semaphore_wait(barrier, len(others))


def send(source, target, sems, index, other):
    copy = pltpu.make_async_remote_copy(
        src_ref=source,
        dst_ref=target,
        send_sem=sems[0].at[index],
        recv_sem=sems[1].at[index],
        device_id=other,
        device_id_type=MESH_IDS,
    )
    copy.start()
    return copy


def rows(start, count):
    return pl.ds(pl.multiple_of(start, 8), count)


def split(values):
    high = values.astype(jnp.bfloat16)
    return high, (values - high.astype(jnp.float32)).astype(jnp.bfloat16)


def product(left, right, dims=(((1,), (0,)), ((), ()))):
    lh, ll = left
    rh, rl = right

    def dot(a, b):
        return lax.dot_general(a, b, dims, preferred_element_type=jnp.float32)

    return dot(lh, rh) + (dot(lh, rl) + dot(ll, rh))


SEQ = 1024
QUARTER = SEQ // 4
GROUP = D // 4
GROUP_HEADS = GROUP // HEAD_DIM
SCALE = HEAD_DIM ** (-0.5)
NT = (((1,), (1,)), ((), ()))
TN = (((0,), (0,)), ((), ()))
NN = (((1,), (0,)), ((), ()))
PARTS = (("yzx", 0, 384), ("yxz", 384, 384))
RS_PARTS = (("xzy", 0, 384), ("zxy", 384, 384))


def mul(a, b, dims=NN):
    return lax.dot_general(a, b, dims, preferred_element_type=jnp.float32)


def neighbours(x, y, z, core):
    return {
        "x": [device(x + k, y, z, core) for k in (1, 2, 3)],
        "y": [device(x, y + k, z, core) for k in (1, 2, 3)],
        "z": [device(x, y, z + k, core) for k in (1, 2, 3)],
    }


def cell(here, free, moved=None):
    moved = moved or {}
    return tuple(slice(None) if a in free else moved.get(a, here[a]) for a in "yxz")


class Counter:
    def __init__(self):
        self.count = 0

    def take(self, many=1):
        self.count += many
        return self.count - many


def wait_all(copies):
    for copy in copies:
        copy.wait()


def in_core_order(core, own, other):
    return jnp.concatenate(
        [jnp.where(core == 0, own, other), jnp.where(core == 0, other, own)], axis=-2
    )


def unit_rows(values):
    values = values.astype(jnp.float32)
    inverse = lax.rsqrt(jnp.mean(values * values, axis=-1, keepdims=True) + NORM_EPS)
    return values * inverse, inverse


def total_of(*pieces):
    total = pieces[0].astype(jnp.float32)
    for piece in pieces[1:]:
        total = total + piece.astype(jnp.float32)
    return total


def layer_kernel(
    length, tokens, cotangent_far, gains, conv, w_qkv, w_out, w_ffn_far,
    output_far, grad_middle_far, normed_part_far, small, ffn_pair, heads_pair,
    cotangent, w_ffn, output, grad_middle, normed_part, all_tokens, streams, projected, lse, taps, w_heads, swap_heads, swap_ffn, w_all, wo_all,
    attended, att_send, weights, raw_own, raw_send, raw_in, middle, normed_two, upstream,
    grad_rows, grad_heads, raw_out, f_one_a, f_one_b, f_two_a, f_two_b, f_three_a, f_three_b,
    o_one, o_two, o_three, out_part, key_grad, value_grad, key_turned, grad_stream, raw_conv,
    raw_qkv, qkv_low, qkv_half, q_one, q_two, gain_one, gain_two, pair_out, pair_in,
    small_own, small_in,
    send_sem, recv_sem, local_sem,
):
    x, y, z, core = place()
    here = {"x": x, "y": y, "z": z}
    sems = (send_sem, recv_sem)
    sibling = device(x, y, z, 1 - core)
    along = neighbours(x, y, z, core)
    count = Counter()
    f_one, f_two, f_three = (f_one_a, f_one_b), (f_two_a, f_two_b), (f_three_a, f_three_b)
    columns = [slice(c, c + w) for _, c, w in PARTS]

    def describe(source, target, number, other, number_there=None):
        return pltpu.make_async_remote_copy(
            src_ref=source,
            dst_ref=target,
            send_sem=send_sem.at[number],
            recv_sem=recv_sem.at[number if number_there is None else number_there],
            device_id=other,
            device_id_type=MESH_IDS,
        )

    def go(source, target, other):
        return send(source, target, sems, count.take(), other)

    def to(axis, k):
        return (here[axis] + k) % 4

    loads = [
        pltpu.make_async_copy(far, near, local_sem.at[6 + number])
        for number, (far, near) in enumerate(
            (
                (w_ffn_far, w_ffn),
                (w_qkv, w_heads.at[pl.ds(0, 3)]),
                (w_out, w_heads.at[3]),
                (tokens, all_tokens.at[y]),
                (cotangent_far, cotangent),
            )
        )
    ]
    for load in loads:
        load.start()
    greet([sibling] + along["x"] + along["y"] + along["z"])
    wait_all(loads)
    swaps = [
        go(w_ffn.at[1 - core], swap_ffn, sibling),
        go(w_heads.at[pl.ds(2 - 2 * core, 2)], swap_heads, sibling),
    ]
    for t in range(KW):
        taps[t] = sum(
            jnp.where(y == group, conv[t, :, group * GROUP : (group + 1) * GROUP], 0.0)
            for group in range(4)
        )
    wait_all(swaps)
    weights[core, y, x, z] = in_core_order(core, w_ffn[core], swap_ffn[...]).astype(jnp.bfloat16)
    kinds = pl.ds(2 * core, 2)
    w_all[kinds, x, z] = in_core_order(core, w_heads[kinds], swap_heads[...]).astype(jnp.bfloat16)
    ffn_one = []
    for (order, _, _), cols in zip(PARTS, columns):
        region = weights.at[core, y, x, z, :, cols]
        ffn_one += [go(region, region, other) for other in along[order[0]]]
    one = [device(x + k * (1 - core), y, z + k * core, core) for k in (1, 2, 3)]
    ahead, behind = along["y"][0], along["y"][2]
    spread = [go(all_tokens.at[y], all_tokens.at[y], other) for other in (ahead, behind)]
    heads_one = [go(w_all.at[kinds, x, z], w_all.at[kinds, x, z], other) for other in one]
    wait_all(heads_one)
    second = count.take(3)

    def heads_two(axis):
        at = (kinds, slice(None), z) if axis == "z" else (kinds, x)
        return [
            describe(w_all.at[at], w_all.at[at], second + k, along[axis][k]) for k in range(3)
        ]

    for number, axis in enumerate("zx"):

        @pl.when(core == number)
        def _():
            for copy in heads_two(axis):
                copy.start()

    wait_all(ffn_one)
    ffn_two = []
    for (order, _, _), cols in zip(PARTS, columns):
        region = weights.at[(core,) + cell(here, order[0]) + (slice(None), cols)]
        ffn_two += [go(region, region, other) for other in along[order[1]]]
    for number, axis in enumerate("zx"):

        @pl.when(core == number)
        def _():
            wait_all(heads_two(axis))

    heads_pair_copy = go(w_all.at[kinds], w_all.at[kinds], sibling)
    wait_all(ffn_two)
    ffn_three = []

    def last_hop():
        quarter = len(ffn_three)
        copies = []
        for (order, _, _), cols in zip(PARTS, columns):
            region = weights.at[
                (core,) + cell(here, order[1], {"y": quarter}) + (slice(None), cols)
            ]
            copies += [go(region, region, other) for other in along[order[2]]]
        ffn_three.append(copies)

    last_hop()
    last_hop()
    spread[0].wait()
    forwarded = [
        go(all_tokens.at[to("y", 3), pl.ds(0, 128)], all_tokens.at[to("y", 3), pl.ds(0, 128)], ahead)
    ]
    spread[1].wait()
    forwarded.append(
        go(all_tokens.at[to("y", 1), pl.ds(128, 128)], all_tokens.at[to("y", 1), pl.ds(128, 128)], behind)
    )
    heads_pair_copy.wait()
    half = pl.ds(2 * core, 2)
    wo_all[y] = w_all[3]
    projected[:, 0:8, :] = jnp.zeros((3, 8, GROUP), jnp.float32)
    key_ids = lax.broadcasted_iota(jnp.int32, (SEQ, 1), 0)
    bias = jnp.where(key_ids < length[0], 0.0, NEG_FILL)
    upper = (
        lax.broadcasted_iota(jnp.int32, (QUARTER, QUARTER), 0)
        <= lax.broadcasted_iota(jnp.int32, (QUARTER, QUARTER), 1)
    )

    def project(block):
        normed = (unit_rows(all_tokens[block])[0] * gains[0:1]).astype(jnp.bfloat16)
        for kind in range(3):
            projected[kind, rows(8 + block * QUARTER, QUARTER), :] = mul(
                normed, w_all[kind].reshape(D, GROUP)
            )

    def convolve(i):
        rows_i = slice(i * QUARTER, (i + 1) * QUARTER)
        for kind in range(3):
            base = 8 + i * QUARTER
            summed = taps[0, kind : kind + 1] * projected[kind, base : base + QUARTER, :]
            for t in range(1, KW):
                summed = summed + taps[t, kind : kind + 1] * projected[
                    kind, base - t : base - t + QUARTER, :
                ]
            stream = summed.astype(jnp.bfloat16)
            if kind == 0:
                stream = stream * jnp.bfloat16(SCALE)
            for head in range(GROUP_HEADS):
                streams[kind * GROUP_HEADS + head, rows_i, :] = stream[
                    :, head * HEAD_DIM : (head + 1) * HEAD_DIM
                ]

    for k in (0, 1, 3):
        project(to("y", k))
    wait_all(forwarded)
    wo_y = [go(w_all.at[3, half], wo_all.at[y, half], other) for other in along["y"]]
    project(to("y", 2))

    heads_send, heads_recv = count.take(4), count.take(4)

    def head_copy(i):
        return describe(
            att_send.at[i], attended.at[y], heads_send + i, device(x, i, z, core),
            heads_recv + (i - y + 3) % 4,
        )

    def attend(i):
        rows_i = slice(i * QUARTER, (i + 1) * QUARTER)
        keys = (i + 1) * QUARTER
        pieces = []
        for head in range(GROUP_HEADS):
            scores = mul(
                streams[GROUP_HEADS + head, :keys, :], streams[head, rows_i, :], NT
            ) + bias[:keys]
            corner = jnp.where(upper, scores[keys - QUARTER :], NEG_FILL)
            scores = corner if i == 0 else jnp.concatenate([scores[: keys - QUARTER], corner], 0)
            top = jnp.max(scores, axis=0, keepdims=True)
            lifted = jnp.exp(scores - top)
            total = jnp.sum(lifted, axis=0, keepdims=True)
            probs = (lifted * (1.0 / total)).astype(jnp.bfloat16)
            lse[head, :, rows_i] = top + jnp.log(total)
            pieces.append(mul(streams[2 * GROUP_HEADS + head, :keys, :], probs, TN).T)
        att_send[i] = jnp.concatenate(pieces, axis=1).astype(jnp.bfloat16)

        @pl.when(i != y)
        def _():
            head_copy(i).start()

    for i in range(4):
        convolve(i)
    attend(3)
    wait_all(wo_y)
    wo_pair = [
        go(wo_all.at[to("y", k), half], wo_all.at[to("y", k), half], sibling) for k in (1, 2, 3)
    ]
    pairing = []

    def pair_up(quarter):
        wait_all(ffn_three[quarter])
        pairing.append(go(weights.at[core, quarter], weights.at[core, quarter], sibling))

    pair_up(0)
    pair_up(1)
    last_hop()
    last_hop()
    attend(2)
    attend(1)
    attend(0)
    wait_all(wo_pair)
    attended[y] = att_send[y]
    for i in range(4):

        @pl.when(i != y)
        def _():
            head_copy(i).wait_send()

    for k in range(3):
        describe(
            att_send.at[0], attended.at[y], heads_send, along["y"][k], heads_recv + k
        ).wait_recv()

    mixed = all_tokens[y].astype(jnp.float32)
    for group in range(4):
        mixed = mixed + mul(attended[group], wo_all[group].reshape(D, GROUP), NT)
    middle[...] = mixed
    output[...] = mixed
    normed_two[...] = (unit_rows(mixed)[0] * gains[1:2]).astype(jnp.bfloat16)
    row_ids = lax.broadcasted_iota(jnp.int32, (QUARTER, 1), 0)
    real = row_ids + y * QUARTER < length[0]
    upstream[...] = jnp.where(real, cotangent[...].astype(jnp.float32), 0.0).astype(jnp.bfloat16)
    leaving = []
    stage_one = []
    right_own = jnp.where(core == 0, normed_two[...], upstream[...])
    right_other = jnp.where(core == 0, upstream[...], normed_two[...])

    def settle(quarter):
        leaving[quarter].wait()
        for step in range(4):
            raw_own[quarter, step] = total_of(
                raw_own[quarter, step], raw_in[quarter, step]
            ).astype(jnp.bfloat16)
        for number, ((order, _, _), cols) in enumerate(zip(RS_PARTS, columns)):
            for k in (1, 2, 3):
                index = cell(here, order[1], {"y": quarter, order[0]: to(order[0], k)})
                stage_one.append(
                    go(
                        raw_own.at[index + (slice(None), cols)],
                        f_one[number].at[k - 1, quarter],
                        along[order[0]][k - 1],
                    )
                )

    for quarter in range(4):
        pairing[quarter].wait()
        into = weights[0, quarter].reshape(D, D)
        back = weights[1, quarter].reshape(D, D)
        positive = jnp.maximum(mul(normed_two[...], into, NT), 0.0)
        active = (positive * positive).astype(jnp.bfloat16)
        grad_hidden = (mul(upstream[...], back, NT) * (2.0 * positive)).astype(jnp.bfloat16)
        output[...] += mul(active, back)
        grad_term = mul(grad_hidden, into)
        grad_middle[...] = grad_term if quarter == 0 else grad_middle[...] + grad_term
        left_own = jnp.where(core == 0, grad_hidden, active)
        left_other = jnp.where(core == 0, active, grad_hidden)
        shape = (4, 4, PAIR, D)
        raw_send[quarter % 2] = mul(left_other, right_other, TN).astype(jnp.bfloat16).reshape(shape)
        leaving.append(go(raw_send.at[quarter % 2], raw_in.at[quarter], sibling))
        raw_own[quarter] = mul(left_own, right_own, TN).astype(jnp.bfloat16).reshape(shape)
        if quarter >= 1:
            settle(quarter - 1)
        if quarter == 1:
            pair_up(2)
            pair_up(3)
    unit, inverse = unit_rows(middle[...])
    grad = grad_middle[...]
    gain_two[...] = jnp.sum(grad * unit, axis=0, keepdims=True)
    scaled = grad * gains[1:2]
    inner = jnp.mean(scaled * unit, axis=-1, keepdims=True)
    grad_all = jnp.where(real, cotangent[...].astype(jnp.float32), 0.0) + inverse * (
        scaled - unit * inner
    )
    grad_middle[...] = grad_all
    stores = []

    def store(near, far):
        copy = pltpu.make_async_copy(near, far, local_sem.at[len(stores)])
        copy.start()
        stores.append(copy)

    store(output, output_far)
    store(grad_middle, grad_middle_far)
    lower_rows = grad_all.astype(jnp.bfloat16)

    turned = []
    for k in (2, 1, 3):
        group = to("y", k)
        grad_rows[group] = mul(lower_rows, wo_all[group].reshape(D, GROUP)).astype(jnp.bfloat16)
        turned.append(go(grad_rows.at[group], grad_heads.at[y], along["y"][k - 1]))
    grad_heads[y] = mul(lower_rows, wo_all[y].reshape(D, GROUP)).astype(jnp.bfloat16)
    for group in range(4):
        raw_out[group] = (
            mul(lower_rows, attended[group], TN).astype(jnp.bfloat16).reshape(4, 4, PAIR, GROUP)
        )
    key_grad[...] = jnp.zeros_like(key_grad)
    value_grad[...] = jnp.zeros_like(value_grad)
    raw_conv[...] = jnp.zeros_like(raw_conv)
    raw_qkv[...] = jnp.zeros_like(raw_qkv)
    grad_stream[:, 0:8, :] = jnp.zeros((3, 8, GROUP), jnp.float32)
    for head in range(GROUP_HEADS):
        key_turned[head] = streams[GROUP_HEADS + head].T
    settle(3)
    wait_all(turned)
    out_one = [go(raw_out.at[to("y", k)], o_one.at[k - 1], along["y"][k - 1]) for k in (1, 2, 3)]

    def attend_back(i):
        rows_i = slice(i * QUARTER, (i + 1) * QUARTER)
        keys = (i + 1) * QUARTER
        grads = grad_heads[i]
        query_pieces = []
        for head in range(GROUP_HEADS):
            query = streams[head, rows_i, :]
            upstream_rows = grads[:, head * HEAD_DIM : (head + 1) * HEAD_DIM]
            scores = mul(streams[GROUP_HEADS + head, :keys, :], query, NT) + (
                bias[:keys] - lse[head, :, rows_i]
            )
            corner = jnp.where(upper, scores[keys - QUARTER :], NEG_FILL)
            scores = corner if i == 0 else jnp.concatenate([scores[: keys - QUARTER], corner], 0)
            probs = jnp.exp(scores)
            prob_grad = mul(streams[2 * GROUP_HEADS + head, :keys, :], upstream_rows, NT)
            centre = jnp.sum(prob_grad * probs, axis=0, keepdims=True)
            score_grad = (probs * (prob_grad - centre)).astype(jnp.bfloat16)
            query_pieces.append((mul(key_turned[head, :, :keys], score_grad) * SCALE).T)
            key_grad[head, :keys, :] += mul(score_grad, query)
            value_grad[head, :keys, :] += mul(probs.astype(jnp.bfloat16), upstream_rows)
        grad_stream[:, QUARTER:, :] = grad_stream[:, 0:8, :]
        for kind, pieces in (
            (0, query_pieces),
            (1, [key_grad[head, rows_i, :] for head in range(GROUP_HEADS)]),
            (2, [value_grad[head, rows_i, :] for head in range(GROUP_HEADS)]),
        ):
            grad_stream[kind, 0:QUARTER, :] = (
                jnp.concatenate(pieces, axis=1).astype(jnp.bfloat16).astype(jnp.float32)
            )
        unit_i = unit_rows(all_tokens[i])[0]
        normed_turned = (unit_i * gains[0:1]).astype(jnp.bfloat16).T
        total = None
        for kind in range(3):
            block = projected[kind, 8 + i * QUARTER : 8 + (i + 1) * QUARTER, :]
            summed = None
            for t in range(KW):
                shifted = grad_stream[kind, t : QUARTER + t, :]
                term = taps[t, kind : kind + 1] * shifted
                summed = term if summed is None else summed + term
                raw_conv[t, kind : kind + 1, :] += jnp.sum(shifted * block, axis=0, keepdims=True)
            lower = summed.astype(jnp.bfloat16)
            raw_qkv[kind] += mul(normed_turned, lower)
            term = mul(lower, w_all[kind].reshape(D, GROUP), NT)
            total = term if total is None else total + term
        normed_part[i] = total.astype(jnp.bfloat16)
        store(normed_part.at[i], normed_part_far.at[i])
        term = jnp.sum(total * unit_i, axis=0, keepdims=True)
        gain_one[...] = term if i == 3 else gain_one[...] + term

    attend_back(3)
    attend_back(2)
    wait_all(stage_one)
    stage_two = []
    for number, ((order, _, _), cols) in enumerate(zip(RS_PARTS, columns)):
        for quarter in range(4):
            index = cell(here, order[1], {"y": quarter}) + (slice(None), cols)
            raw_own[index] = total_of(
                raw_own[index], *(f_one[number][k, quarter] for k in range(3))
            ).astype(jnp.bfloat16)
        for k in (1, 2, 3):
            index = cell(here, order[2], {order[1]: to(order[1], k)})
            stage_two.append(
                go(
                    raw_own.at[index + (slice(None), cols)],
                    f_two[number].at[k - 1],
                    along[order[1]][k - 1],
                )
            )
    attend_back(1)
    wait_all(out_one)
    out_part[...] = total_of(raw_out[y], *(o_one[k] for k in range(3))).astype(jnp.bfloat16)
    out_two = [go(out_part.at[to("x", k)], o_two.at[k - 1], along["x"][k - 1]) for k in (1, 2, 3)]
    attend_back(0)
    qkv_low[...] = raw_qkv[...].reshape(3, 4, 4, PAIR, GROUP).astype(jnp.bfloat16)
    first_hop, second_hop = count.take(3), count.take(3)

    def qkv_one(axis):
        copies = []
        for k in (1, 2, 3):
            at = (slice(None), to("x", k)) if axis == "x" else (slice(None), slice(None), to("z", k))
            copies.append(
                describe(qkv_low.at[at], q_one.at[k - 1], first_hop + k - 1, along[axis][k - 1])
            )
        return copies

    def qkv_two(axis):
        return [
            describe(
                qkv_half.at[:, to(axis, k)], q_two.at[k - 1], second_hop + k - 1, along[axis][k - 1]
            )
            for k in (1, 2, 3)
        ]

    for number, axis in enumerate("xz"):

        @pl.when(core == number)
        def _():
            for copy in qkv_one(axis):
                copy.start()

    wait_all(out_two)
    out_part[x] = total_of(out_part[x], *(o_two[k] for k in range(3))).astype(jnp.bfloat16)
    out_three = [
        go(out_part.at[x, to("z", k)], o_three.at[k - 1], along["z"][k - 1]) for k in (1, 2, 3)
    ]
    small_own[...] = jnp.zeros_like(small_own)
    for row, gain in enumerate((gain_one[...], gain_two[...])):
        for group in range(4):
            small_own[4 * row + group : 4 * row + group + 1, :] = gain[
                :, group * GROUP : (group + 1) * GROUP
            ]
    for t in range(KW):
        small_own[8 + 3 * t : 11 + 3 * t, :] = raw_conv[t, 0:3, :]
    for number, axis in enumerate("xz"):

        @pl.when(core == number)
        def _():
            wait_all(qkv_one(axis))
            at = (slice(None), x) if axis == "x" else (slice(None), slice(None), z)
            qkv_half[...] = total_of(qkv_low[at], *(q_one[k] for k in range(3))).astype(jnp.bfloat16)
            for copy in qkv_two("zx"[number]):
                copy.start()

    wait_all(stage_two)
    stage_three = []
    for number, ((order, _, _), cols) in enumerate(zip(RS_PARTS, columns)):
        index = cell(here, order[2]) + (slice(None), cols)
        raw_own[index] = total_of(
            raw_own[index], *(f_two[number][k] for k in range(3))
        ).astype(jnp.bfloat16)
        for k in (1, 2, 3):
            index = cell(here, "", {order[2]: to(order[2], k)})
            stage_three.append(
                go(
                    raw_own.at[index + (slice(None), cols)],
                    f_three[number].at[k - 1],
                    along[order[2]][k - 1],
                )
            )
    wait_all(out_three)
    pair_out[3] = total_of(out_part[x, z], *(o_three[k] for k in range(3)))
    for number, axis in enumerate("zx"):

        @pl.when(core == number)
        def _():
            wait_all(qkv_two(axis))
            pair_out[0:3] = total_of(qkv_half[:, here[axis]], *(q_two[k] for k in range(3)))

    wait_all(stage_three)
    for number, cols in enumerate(columns):
        index = cell(here, "") + (slice(None), cols)
        ffn_pair[:, cols] = total_of(raw_own[index], *(f_three[number][k] for k in range(3)))
    lanes = jnp.sum(ffn_pair[...] * ffn_pair[...], axis=0, keepdims=True)
    squares = sum(lanes[:, group * GROUP : (group + 1) * GROUP] for group in range(4))
    small_own[17:18, :] = squares
    pairs = [go(pair_out, pair_in, sibling), go(small_own, small_in, sibling)]
    wait_all(pairs)
    heads_pair[...] = pair_out[...] + pair_in[...]
    lanes = jnp.sum(jnp.sum(heads_pair[...] * heads_pair[...], axis=0), axis=0, keepdims=True)
    row_ids = lax.broadcasted_iota(jnp.int32, (SMALL, GROUP), 0)
    small[...] = small_own[...] + small_in[...] + jnp.where(row_ids == 17, lanes, 0.0)
    wait_all(stores)


def layer(length, tokens, cotangent, gains, conv, w_qkv, w_out, w_ffn):
    f32, b16 = jnp.float32, jnp.bfloat16
    vmem = pl.BlockSpec(memory_space=pltpu.VMEM)
    far = pl.BlockSpec(memory_space=pl.ANY)
    blocks = (4, 4, PAIR)
    scratch = [
        pltpu.VMEM((QUARTER, D), b16),
        pltpu.VMEM((2, SUB, D), f32),
        pltpu.VMEM((QUARTER, D), f32),
        pltpu.VMEM((QUARTER, D), f32),
        pltpu.VMEM((4, QUARTER, D), b16),
        pltpu.VMEM((4, QUARTER, D), b16),
        pltpu.VMEM((3 * GROUP_HEADS, SEQ, HEAD_DIM), b16),
        pltpu.VMEM((3, SEQ + 8, GROUP), f32),
        pltpu.VMEM((GROUP_HEADS, 1, SEQ), f32),
        pltpu.VMEM((KW, 3, GROUP), f32),
        pltpu.VMEM((4, SUB, GROUP), f32),
        pltpu.VMEM((2, SUB, GROUP), f32),
        pltpu.VMEM((SUB, D), f32),
        pltpu.VMEM((4,) + blocks + (GROUP,), b16),
        pltpu.VMEM((4,) + blocks + (GROUP,), b16),
        pltpu.VMEM((4, QUARTER, GROUP), b16),
        pltpu.VMEM((4, QUARTER, GROUP), b16),
        pltpu.VMEM((2, 4) + blocks + (D,), b16),
        pltpu.VMEM((4,) + blocks + (D,), b16),
        pltpu.VMEM((2,) + blocks + (D,), b16),
        pltpu.VMEM((4,) + blocks + (D,), b16),
        pltpu.VMEM((QUARTER, D), f32),
        pltpu.VMEM((QUARTER, D), b16),
        pltpu.VMEM((QUARTER, D), b16),
        pltpu.VMEM((4, QUARTER, GROUP), b16),
        pltpu.VMEM((4, QUARTER, GROUP), b16),
        pltpu.VMEM((4,) + blocks + (GROUP,), b16),
    ]
    scratch += [pltpu.VMEM((3, 4, 4, PAIR, w), b16) for _, _, w in RS_PARTS]
    scratch += [pltpu.VMEM((3, 4, PAIR, w), b16) for _, _, w in RS_PARTS]
    scratch += [pltpu.VMEM((3, PAIR, w), b16) for _, _, w in RS_PARTS]
    scratch += [
        pltpu.VMEM((3,) + blocks + (GROUP,), b16),
        pltpu.VMEM((3, 4, PAIR, GROUP), b16),
        pltpu.VMEM((3, PAIR, GROUP), b16),
        pltpu.VMEM(blocks + (GROUP,), b16),
        pltpu.VMEM((GROUP_HEADS, SEQ, HEAD_DIM), f32),
        pltpu.VMEM((GROUP_HEADS, SEQ, HEAD_DIM), f32),
        pltpu.VMEM((GROUP_HEADS, HEAD_DIM, SEQ), b16),
        pltpu.VMEM((3, QUARTER + 8, GROUP), f32),
        pltpu.VMEM((KW, 8, GROUP), f32),
        pltpu.VMEM((3, D, GROUP), f32),
        pltpu.VMEM((3,) + blocks + (GROUP,), b16),
        pltpu.VMEM((3, 4, PAIR, GROUP), b16),
        pltpu.VMEM((3, 3, 4, PAIR, GROUP), b16),
        pltpu.VMEM((3, 3, PAIR, GROUP), b16),
        pltpu.VMEM((1, D), f32),
        pltpu.VMEM((1, D), f32),
        pltpu.VMEM((4, PAIR, GROUP), f32),
        pltpu.VMEM((4, PAIR, GROUP), f32),
        pltpu.VMEM((SMALL, GROUP), f32),
        pltpu.VMEM((SMALL, GROUP), f32),
        pltpu.SemaphoreType.DMA((160,)),
        pltpu.SemaphoreType.DMA((160,)),
        pltpu.SemaphoreType.DMA((11,)),
    ]
    return pl.pallas_call(
        layer_kernel,
        out_shape=[
            jax.ShapeDtypeStruct((QUARTER, D), f32),
            jax.ShapeDtypeStruct((QUARTER, D), f32),
            jax.ShapeDtypeStruct((4, QUARTER, D), b16),
            jax.ShapeDtypeStruct((SMALL, GROUP), f32),
            jax.ShapeDtypeStruct((PAIR, D), f32),
            jax.ShapeDtypeStruct((4, PAIR, GROUP), f32),
        ],
        in_specs=[pl.BlockSpec(memory_space=pltpu.SMEM)]
        + [far, far, vmem, vmem, far, far, far],
        out_specs=[pl.BlockSpec(memory_space=pl.ANY)] * 3 + [vmem] * 3,
        scratch_shapes=scratch,
        name="layer",
        compiler_params=pltpu.CompilerParams(
            collective_id=2, has_side_effects=True, vmem_limit_bytes=63 * 2**20
        ),
    )(length, tokens, cotangent, gains, conv, w_qkv, w_out, w_ffn)


UPPER = ((0, 0), (0, 1), (0, 2), (1, 1), (1, 2), (2, 2))
SUM_PARTS = ("xzy", "zyx", "yxz")
SMALL = 24


def adam(weight, gradient, moment_one, moment_two):
    first_new = BETA_ONE * moment_one + (1.0 - BETA_ONE) * gradient
    second_new = BETA_TWO * moment_two + (1.0 - BETA_TWO) * gradient * gradient
    stepped = (
        first_new
        / (1.0 - BETA_ONE**STEP)
        / (jnp.sqrt(second_new / (1.0 - BETA_TWO**STEP)) + ADAM_EPS)
    )
    return first_new, second_new, weight - ADAM_RATE * stepped


def tile(i):
    return slice(i * BLK, (i + 1) * BLK)


def optimizer_kernel(
    g_pair_far, g_heads_far, small_far, normed_part, m_ffn_far, m_qkv, m_out,
    wide, g_mine, o_ffn, o_heads, normed_in,
    g_pair, g_heads, small, m_ffn, m_heads, m_in, mh_in, s_x, s_z, s_y, iterate, head_iterate,
    part, gathered, r_one, r_two, r_three, hpart, hsum, hr_one, hr_two,
    g_high, g_low, z_high, z_low, t_high, t_low, gram, hgram,
    send_sem, recv_sem, local_sem,
):
    x, y, z, core = place()
    here = {"x": x, "y": y, "z": z}
    sems = (send_sem, recv_sem)
    sibling = device(x, y, z, 1 - core)
    along = neighbours(x, y, z, core)
    count = Counter()

    def go(source, target, other):
        return send(source, target, sems, count.take(), other)

    def to(axis, k):
        return (here[axis] + k) % 4

    own_rows = rows(core * SUB, SUB)
    their_rows = rows((1 - core) * SUB, SUB)
    loads = [
        pltpu.make_async_copy(far, near, local_sem.at[number])
        for number, (far, near) in enumerate(
            (
                (g_pair_far, g_pair),
                (g_heads_far, g_heads),
                (small_far, small),
                (m_ffn_far, m_ffn),
                (m_qkv, m_heads.at[pl.ds(0, 3)]),
                (m_out, m_heads.at[3]),
                (normed_part.at[y], normed_in.at[3]),
            )
        )
    ]
    for load in loads:
        load.start()
    greet([sibling] + along["x"] + along["y"] + along["z"])
    wait_all(loads)
    swaps = [
        go(g_pair.at[their_rows], g_mine.at[core], sibling),
        go(m_ffn.at[1 - core], m_in, sibling),
        go(m_heads.at[pl.ds(2 - 2 * core, 2)], mh_in, sibling),
    ]
    g_mine[core] = g_pair[own_rows, :]
    total = small[...]
    for slots, axis in ((s_x, "x"), (s_z, "z")):
        at = here[axis]
        slots[at] = total
        wait_all([go(slots.at[at], slots.at[at], other) for other in along[axis]])
        total = (slots[0] + slots[1]) + (slots[2] + slots[3])
    s_y[y] = total
    wait_all([go(s_y.at[y], s_y.at[y], other) for other in along["y"]])
    total = (s_y[0] + s_y[1]) + (s_y[2] + s_y[3])
    for group in range(4):
        lanes_of = slice(group * GROUP, (group + 1) * GROUP)
        for row in range(2):
            wide[row : row + 1, lanes_of] = total[4 * row + group : 4 * row + group + 1, :]
        wide[2:11, lanes_of] = s_y[group, 8:17, :]
    gain_sum = wide[0:2, :]
    conv_sum = wide[2:11, :]
    squared = (
        jnp.sum(gain_sum * gain_sum, axis=(0, 1), keepdims=True)
        + jnp.sum(conv_sum * conv_sum, axis=(0, 1), keepdims=True)
        + jnp.sum(total[17:18, :], axis=(0, 1), keepdims=True)
    )
    norm = jnp.sqrt(squared)
    wide[11:16, :] = jnp.broadcast_to(norm, (5, D))
    factor = CLIP_NORM / jnp.maximum(norm, CLIP_NORM)
    wait_all(swaps)
    for at, momentum in ((own_rows, m_ffn[core]), (their_rows, m_in[...])):
        iterate[at, :] = MOMENTUM * momentum + factor * g_pair[at, :]
    for kind in range(2):
        for at, momentum in ((own_rows, m_heads[2 * core + kind]), (their_rows, mh_in[kind])):
            head_iterate[kind, at, :] = MOMENTUM * momentum + factor * g_heads[2 * core + kind, at, :]
    transposed = (((0,), (0,)), ((), ()))
    for number, (i, j) in enumerate(UPPER):
        part[tile(number), :] = product(
            split(iterate[:, tile(i)]), split(iterate[:, tile(j)]), transposed
        )
    h_rows = lax.broadcasted_iota(jnp.int32, (GROUP, GROUP), 0)
    h_cols = lax.broadcasted_iota(jnp.int32, (GROUP, GROUP), 1)
    same = h_rows // HEAD_DIM == h_cols // HEAD_DIM
    h_eye = (h_rows == h_cols).astype(jnp.float32)
    packed = []
    for kind in range(2):
        pieces = split(head_iterate[kind])
        full = jnp.where(same, product(pieces, pieces, transposed), 0.0)
        folded = full[:, :HEAD_DIM]
        for head in range(1, GROUP_HEADS):
            folded = folded + full[:, head * HEAD_DIM : (head + 1) * HEAD_DIM]
        packed.append(folded)
    hpart[GROUP:, :] = jnp.zeros((BLK - GROUP, 2 * HEAD_DIM), jnp.float32)
    hpart[:GROUP, :] = jnp.concatenate(packed, axis=1)
    one = x + core * (z - x)
    two = z + core * (x - z)
    h_first = [device(x + k * (1 - core), y, z + k * core, core) for k in (1, 2, 3)]
    h_second = [device(x + k * core, y, z + k * (1 - core), core) for k in (1, 2, 3)]
    third = 6 * BLK // 3
    sizes = (third // 4, third // 16, third // 64)
    h_sizes = (BLK // 4, BLK // 16)
    bases = [number * third for number in range(3)]
    h_base = 0
    for stage, slots in enumerate((r_one, r_two, r_three)):
        size = sizes[stage]
        copies = [
            go(
                part.at[rows(bases[number] + to(order[stage], k) * size, size)],
                slots.at[number, k - 1],
                along[order[stage]][k - 1],
            )
            for number, order in enumerate(SUM_PARTS)
            for k in (1, 2, 3)
        ]
        if stage < 2:
            h_size, h_here = h_sizes[stage], (one, two)[stage]
            h_slots, h_others = ((hr_one, h_first), (hr_two, h_second))[stage]
            copies += [
                go(
                    hpart.at[rows(h_base + (h_here + k) % 4 * h_size, h_size)],
                    h_slots.at[k - 1],
                    h_others[k - 1],
                )
                for k in (1, 2, 3)
            ]
        wait_all(copies)
        target = gathered if stage == 2 else part
        for number, order in enumerate(SUM_PARTS):
            bases[number] = bases[number] + here[order[stage]] * size
            at = rows(bases[number], size)
            target[at, :] = part[at, :] + (
                (slots[number, 0] + slots[number, 1]) + slots[number, 2]
            )
        if stage < 2:
            h_base = h_base + h_here * h_size
            at = rows(h_base, h_size)
            (hsum if stage == 1 else hpart)[at, :] = hpart[at, :] + (
                (h_slots[0] + h_slots[1]) + h_slots[2]
            )
    for stage in (2, 1, 0):
        size = sizes[stage]
        copies = []
        for number, order in enumerate(SUM_PARTS):
            region = gathered.at[rows(bases[number], size)]
            copies += [go(region, region, other) for other in along[order[stage]]]
            bases[number] = bases[number] - here[order[stage]] * size
        if stage < 2:
            region = hsum.at[rows(h_base, h_sizes[stage])]
            copies += [go(region, region, other) for other in (h_first, h_second)[stage]]
            h_base = h_base - (one, two)[stage] * h_sizes[stage]
        wait_all(copies)
    rows_out = [
        go(normed_part.at[to("y", k)], normed_in.at[k - 1], along["y"][k - 1]) for k in (1, 2, 3)
    ]
    eye = (
        lax.broadcasted_iota(jnp.int32, (BLK, BLK), 0)
        == lax.broadcasted_iota(jnp.int32, (BLK, BLK), 1)
    ).astype(jnp.float32)
    trace = jnp.zeros((1, 1), jnp.float32)
    for number, (i, j) in enumerate(UPPER):
        if i == j:
            trace = trace + jnp.sum(gathered[tile(number), :] * eye, axis=(0, 1), keepdims=True)
    scale = 1.0 / (jnp.sqrt(trace) + NS_EPS)

    def keep(high, low, i, j, block):
        upper_pieces = split(block)
        for kept, piece in zip((high, low), upper_pieces):
            kept[tile(i), tile(j)] = piece
            if i != j:
                kept[tile(j), tile(i)] = piece.T

    def symmetric(left, right, use):
        number = 0
        for i in range(3):
            across = slice(i * BLK, D)
            row = product(
                (left[0][tile(i), :], left[1][tile(i), :]),
                (right[0][:, across], right[1][:, across]),
            )
            for j in range(i, 3):
                use(number, i, j, row[:, (j - i) * BLK : (j - i + 1) * BLK])
                number += 1

    for number, (i, j) in enumerate(UPPER):
        block = gathered[tile(number), :] * (scale * scale)
        gram[number] = block
        keep(g_high, g_low, i, j, block)
    iterate[...] = iterate[...] * scale
    for kind in range(2):
        folded = hsum[:GROUP, kind * HEAD_DIM : (kind + 1) * HEAD_DIM]
        full = jnp.where(same, jnp.concatenate([folded] * GROUP_HEADS, axis=1), 0.0)
        on_diagonal = full * h_eye
        by_column = jnp.sum(on_diagonal, axis=0, keepdims=True)
        by_row = jnp.sum(on_diagonal, axis=1, keepdims=True)
        trace_row = jnp.sum(jnp.where(same, by_column, 0.0), axis=1, keepdims=True)
        trace_column = jnp.sum(jnp.where(same, by_row, 0.0), axis=0, keepdims=True)
        scale_column = 1.0 / (jnp.sqrt(trace_column) + NS_EPS)
        scale_row = 1.0 / (jnp.sqrt(trace_row) + NS_EPS)
        hgram[kind] = full * scale_row * scale_column
        head_iterate[kind] = head_iterate[kind] * scale_column

    def sweep_heads(last):
        for kind in range(2):
            current = hgram[kind]
            pieces = split(current)
            poly = COEF_A * h_eye + COEF_B * current + COEF_C * product(pieces, pieces)
            poly_pieces = split(poly)
            head_iterate[kind] = product(split(head_iterate[kind]), poly_pieces)
            if not last:
                hgram[kind] = product(split(product(pieces, poly_pieces)), poly_pieces)

    def sweep(last):
        def use_square(number, i, j, block):
            poly = COEF_B * gram[number] + COEF_C * block
            keep(z_high, z_low, i, j, poly + COEF_A * eye if i == j else poly)

        def use_half(number, i, j, block):
            keep(t_high, t_low, i, j, block)

        def use_gram(number, i, j, block):
            gram[number] = block
            keep(g_high, g_low, i, j, block)

        symmetric((g_high, g_low), (g_high, g_low), use_square)
        sweep_heads(last)
        iterate[...] = product(split(iterate[...]), (z_high[...], z_low[...]))
        if not last:
            symmetric((g_high, g_low), (z_high, z_low), use_half)
            symmetric((t_high, t_low), (z_high, z_low), use_gram)

    def body(_, carry):
        sweep(False)
        return carry

    lax.fori_loop(0, NS_ITERS - 1, body, 0)
    sweep(True)
    copies = [go(iterate.at[their_rows], o_ffn.at[core], sibling)]
    for kind in range(2):
        copies.append(go(head_iterate.at[kind, their_rows], o_heads.at[2 * core + kind], sibling))
    o_ffn[core] = iterate[own_rows, :]
    for kind in range(2):
        o_heads[2 * core + kind] = head_iterate[kind, own_rows, :]
    wait_all(copies)
    wait_all(rows_out)


def optimizer(g_pair, g_heads, small, normed_part, *momenta):
    f32, b16 = jnp.float32, jnp.bfloat16
    vmem = pl.BlockSpec(memory_space=pltpu.VMEM)
    third = 6 * BLK // 3
    scratch = [
        pltpu.VMEM((PAIR, D), f32),
        pltpu.VMEM((4, PAIR, GROUP), f32),
        pltpu.VMEM((SMALL, GROUP), f32),
        pltpu.VMEM((2, SUB, D), f32),
        pltpu.VMEM((4, SUB, GROUP), f32),
        pltpu.VMEM((SUB, D), f32),
        pltpu.VMEM((2, SUB, GROUP), f32),
        pltpu.VMEM((4, SMALL, GROUP), f32),
        pltpu.VMEM((4, SMALL, GROUP), f32),
        pltpu.VMEM((4, SMALL, GROUP), f32),
        pltpu.VMEM((PAIR, D), f32),
        pltpu.VMEM((2, PAIR, GROUP), f32),
        pltpu.VMEM((6 * BLK, BLK), f32),
        pltpu.VMEM((6 * BLK, BLK), f32),
        pltpu.VMEM((3, 3, third // 4, BLK), f32),
        pltpu.VMEM((3, 3, third // 16, BLK), f32),
        pltpu.VMEM((3, 3, third // 64, BLK), f32),
        pltpu.VMEM((BLK, 2 * HEAD_DIM), f32),
        pltpu.VMEM((BLK, 2 * HEAD_DIM), f32),
        pltpu.VMEM((3, BLK // 4, 2 * HEAD_DIM), f32),
        pltpu.VMEM((3, BLK // 16, 2 * HEAD_DIM), f32),
    ]
    scratch += [pltpu.VMEM((D, D), b16)] * 6
    scratch += [
        pltpu.VMEM((6, BLK, BLK), f32),
        pltpu.VMEM((2, GROUP, GROUP), f32),
        pltpu.SemaphoreType.DMA((96,)),
        pltpu.SemaphoreType.DMA((96,)),
        pltpu.SemaphoreType.DMA((7,)),
    ]
    return pl.pallas_call(
        optimizer_kernel,
        out_shape=[
            jax.ShapeDtypeStruct((16, D), f32),
            jax.ShapeDtypeStruct((2, SUB, D), f32),
            jax.ShapeDtypeStruct((2, SUB, D), f32),
            jax.ShapeDtypeStruct((4, SUB, GROUP), f32),
            jax.ShapeDtypeStruct((4, QUARTER, D), b16),
        ],
        in_specs=[pl.BlockSpec(memory_space=pl.ANY)] * 7,
        out_specs=[vmem] * 5,
        scratch_shapes=scratch,
        name="optimizer",
        compiler_params=pltpu.CompilerParams(
            collective_id=0, has_side_effects=True, vmem_limit_bytes=63 * 2**20
        ),
    )(g_pair, g_heads, small, normed_part, *momenta)


def update_kernel(
    wide, g_ffn, g_heads, o_ffn, o_heads, normed_in, tokens, grad_middle, out_rows,
    m_ffn, m_qkv, m_out, w_ffn, w_qkv, w_out,
    gains, conv, gain_first, gain_second, conv_first, conv_second,
    output, input_grad, out_gains, out_conv, out_qkv, out_out, out_ffn, out_norm,
    new_m_qkv, new_m_out, new_m_ffn,
    new_gain_first, new_gain_second, new_conv_first, new_conv_second, new_gains, new_conv,
    new_qkv, new_out, new_ffn,
):
    core = lax.axis_index("dp") % 2
    output[...] = out_rows[...]
    grad = (
        normed_in[0].astype(jnp.float32)
        + normed_in[1].astype(jnp.float32)
        + normed_in[2].astype(jnp.float32)
        + normed_in[3].astype(jnp.float32)
    )
    unit, inverse = unit_rows(tokens[...])
    scaled = grad * gains[0:1]
    inner = jnp.mean(scaled * unit, axis=-1, keepdims=True)
    input_grad[...] = grad_middle[...] + inverse * (scaled - unit * inner)
    norm = wide[11:12, 0:1]
    out_norm[...] = norm
    factor = CLIP_NORM / jnp.maximum(norm, CLIP_NORM)
    grad = wide[0:2, :] * factor
    out_gains[...] = grad
    first, second, new = adam(gains[...], grad, gain_first[...], gain_second[...])
    new_gain_first[...], new_gain_second[...], new_gains[...] = first, second, new
    for t in range(KW):
        grad = wide[2 + 3 * t : 5 + 3 * t, :] * factor
        out_conv[t] = grad
        first, second, new = adam(conv[t], grad, conv_first[t], conv_second[t])
        new_conv_first[t], new_conv_second[t], new_conv[t] = first, second, new
    grad = g_ffn[...] * factor
    out_ffn[...] = grad
    new_m_ffn[...] = MOMENTUM * m_ffn[...] + grad
    new_ffn[...] = w_ffn[...] - RATE_IN * math.sqrt(max(FF, D)) * o_ffn[...]
    own_rows = rows(core * SUB, SUB)
    for kind in range(3):
        grad = g_heads[kind, own_rows, :] * factor
        out_qkv[kind] = grad
        new_m_qkv[kind] = MOMENTUM * m_qkv[kind] + grad
    new_qkv[...] = w_qkv[...] - RATE_IN * math.sqrt(D) * o_heads[0:3]
    grad = g_heads[3, own_rows, :] * factor
    out_out[...] = grad
    new_m_out[...] = MOMENTUM * m_out[...] + grad
    new_out[...] = w_out[...] - RATE_OUT * math.sqrt(D) * o_heads[3]


def update(*arrays):
    vmem = pl.BlockSpec(memory_space=pltpu.VMEM)
    m_ffn, m_qkv, m_out, _, _, _, gains, conv = arrays[9:17]
    rows_like = arrays[8]
    like = [rows_like, rows_like, gains, conv, m_qkv, m_out, m_ffn, None, m_qkv, m_out, m_ffn]
    like += [gains, gains, conv, conv, gains, conv, m_qkv, m_out, m_ffn]
    return pl.pallas_call(
        update_kernel,
        out_shape=[
            jax.ShapeDtypeStruct((1, 1) if entry is None else entry.shape, jnp.float32)
            for entry in like
        ],
        in_specs=[vmem] * len(arrays),
        out_specs=[vmem] * len(like),
        name="update",
        compiler_params=pltpu.CompilerParams(vmem_limit_bytes=63 * 2**20),
    )(*arrays)


def per_device(
    tokens,
    lengths,
    cotangent,
    gains,
    conv,
    w_qkv,
    w_out,
    ffn_weights,
    mom_qkv,
    mom_out,
    mom_ffn,
    gain_first,
    gain_second,
    conv_first,
    conv_second,
):
    rows_in = tokens[0]
    output, grad_middle, normed_part, small, ffn_pair, heads_pair = layer(
        lengths, rows_in, cotangent[0], gains, conv, w_qkv, w_out.T, ffn_weights
    )
    wide, g_ffn, o_ffn, o_heads, normed_in = optimizer(
        ffn_pair, heads_pair, small, normed_part, mom_ffn, mom_qkv, mom_out.T
    )
    updated = update(
        wide, g_ffn, heads_pair, o_ffn, o_heads, normed_in, rows_in, grad_middle, output,
        mom_ffn, mom_qkv, mom_out.T, ffn_weights, w_qkv, w_out.T,
        gains, conv, gain_first, gain_second, conv_first, conv_second,
    )
    updated = list(updated)
    for number in (5, 9, 18):
        updated[number] = updated[number].T
    return (updated[0][None], updated[1][None], *updated[2:7], updated[7][0, 0], *updated[8:])


def solution(mesh):
    placed = (
        P("dp", "head", None),
        P("dp"),
        P("dp", "head", None),
        P(),
        P(),
        P(None, "dp", "head"),
        P("head", "dp"),
        P(None, ("head", "dp"), None),
        P(None, "dp", "head"),
        P("head", "dp"),
        P(None, ("head", "dp"), None),
        P(),
        P(),
        P(),
        P(),
    )
    return jax.shard_map(
        per_device,
        mesh=mesh,
        in_specs=placed,
        out_specs=(
            P("dp", "head", None),
            P("dp", "head", None),
            P(),
            P(),
            P(None, "dp", "head"),
            P("head", "dp"),
            P(None, ("head", "dp"), None),
            P(),
            P(None, "dp", "head"),
            P("head", "dp"),
            P(None, ("head", "dp"), None),
            P(),
            P(),
            P(),
            P(),
            P(),
            P(),
            P(None, "dp", "head"),
            P("head", "dp"),
            P(None, ("head", "dp"), None),
        ),
        check_vma=False,
    )
```

```python
import math

import jax
import jax.numpy as jnp
from jax import lax
from jax.experimental import pallas as pl
from jax.experimental.pallas import tpu as pltpu
from jax.sharding import PartitionSpec as P

D = 768
HEADS = 12
HEAD_DIM = 64
FF = 3072
KW = 3
NS_ITERS = 5
STEP = 10


NORM_EPS = 1e-06
NEG_FILL = -1e30
CLIP_NORM = 1.0
MOMENTUM = 0.95
RATE_IN = 0.02
RATE_OUT = 0.15
ADAM_RATE = 0.5
BETA_ONE = 0.9
BETA_TWO = 0.999
ADAM_EPS = 1e-08
NS_EPS = 1e-07
COEF_A = 3.4445
COEF_B = -4.775
COEF_C = 2.0315


SUB = 24
PAIR = 2 * SUB
BLK = 256
MESH_IDS = pl.DeviceIdType.MESH


def place():
    flat = lax.axis_index("dp")
    return flat // 8, lax.axis_index("head"), (flat // 2) % 4, flat % 2


def device(x, y, z, core):
    return (y % 4, ((x % 4) * 4 + z % 4) * 2 + core)


def greet(others):
    barrier = pltpu.get_barrier_semaphore()
    for other in others:
        pl.semaphore_signal(barrier, inc=1, device_id=other, device_id_type=MESH_IDS)
    pl.semaphore_wait(barrier, len(others))


def send(source, target, sems, index, other):
    copy = pltpu.make_async_remote_copy(
        src_ref=source,
        dst_ref=target,
        send_sem=sems[0].at[index],
        recv_sem=sems[1].at[index],
        device_id=other,
        device_id_type=MESH_IDS,
    )
    copy.start()
    return copy


def rows(start, count):
    return pl.ds(pl.multiple_of(start, 8), count)


def split(values):
    high = values.astype(jnp.bfloat16)
    return high, (values - high.astype(jnp.float32)).astype(jnp.bfloat16)


def product(left, right, dims=(((1,), (0,)), ((), ()))):
    lh, ll = left
    rh, rl = right

    def dot(a, b):
        return lax.dot_general(a, b, dims, preferred_element_type=jnp.float32)

    return dot(lh, rh) + (dot(lh, rl) + dot(ll, rh))


SEQ = 1024
QUARTER = SEQ // 4
GROUP = D // 4
GROUP_HEADS = GROUP // HEAD_DIM
SCALE = HEAD_DIM ** (-0.5)
NT = (((1,), (1,)), ((), ()))
TN = (((0,), (0,)), ((), ()))
NN = (((1,), (0,)), ((), ()))
PARTS = (("yzx", 0, 384), ("yxz", 384, 384))
RS_PARTS = (("xzy", 0, 384), ("zxy", 384, 384))


def mul(a, b, dims=NN):
    return lax.dot_general(a, b, dims, preferred_element_type=jnp.float32)


def neighbours(x, y, z, core):
    return {
        "x": [device(x + k, y, z, core) for k in (1, 2, 3)],
        "y": [device(x, y + k, z, core) for k in (1, 2, 3)],
        "z": [device(x, y, z + k, core) for k in (1, 2, 3)],
    }


def cell(here, free, moved=None):
    moved = moved or {}
    return tuple(slice(None) if a in free else moved.get(a, here[a]) for a in "yxz")


class Counter:
    def __init__(self):
        self.count = 0

    def take(self, many=1):
        self.count += many
        return self.count - many


def wait_all(copies):
    for copy in copies:
        copy.wait()


def in_core_order(core, own, other):
    return jnp.concatenate(
        [jnp.where(core == 0, own, other), jnp.where(core == 0, other, own)], axis=-2
    )


def unit_rows(values):
    values = values.astype(jnp.float32)
    inverse = lax.rsqrt(jnp.mean(values * values, axis=-1, keepdims=True) + NORM_EPS)
    return values * inverse, inverse


def total_of(*pieces):
    total = pieces[0].astype(jnp.float32)
    for piece in pieces[1:]:
        total = total + piece.astype(jnp.float32)
    return total


def layer_kernel(
    length, tokens, cotangent_far, gains, conv, w_qkv, w_out, w_ffn_far,
    output_far, grad_middle_far, normed_part_far, small, ffn_pair, heads_pair,
    cotangent, w_ffn, output, grad_middle, normed_part, all_tokens, streams, projected, lse, taps, w_heads, swap_heads, swap_ffn, w_all, wo_all,
    attended, att_send, weights, raw_own, raw_send, raw_in, middle, normed_two, upstream,
    grad_rows, grad_heads, raw_out, f_one_a, f_one_b, f_two_a, f_two_b, f_three_a, f_three_b,
    o_one, o_two, o_three, out_part, key_grad, value_grad, key_turned, grad_stream, raw_conv,
    raw_qkv, qkv_low, qkv_half, q_one, q_two, gain_one, gain_two, pair_out, pair_in,
    small_own, small_in,
    send_sem, recv_sem, local_sem,
):
    x, y, z, core = place()
    here = {"x": x, "y": y, "z": z}
    sems = (send_sem, recv_sem)
    sibling = device(x, y, z, 1 - core)
    along = neighbours(x, y, z, core)
    count = Counter()
    f_one, f_two, f_three = (f_one_a, f_one_b), (f_two_a, f_two_b), (f_three_a, f_three_b)
    columns = [slice(c, c + w) for _, c, w in PARTS]

    def describe(source, target, number, other, number_there=None):
        return pltpu.make_async_remote_copy(
            src_ref=source,
            dst_ref=target,
            send_sem=send_sem.at[number],
            recv_sem=recv_sem.at[number if number_there is None else number_there],
            device_id=other,
            device_id_type=MESH_IDS,
        )

    def go(source, target, other):
        return send(source, target, sems, count.take(), other)

    def to(axis, k):
        return (here[axis] + k) % 4

    loads = [
        pltpu.make_async_copy(far, near, local_sem.at[6 + number])
        for number, (far, near) in enumerate(
            (
                (w_ffn_far, w_ffn),
                (w_qkv, w_heads.at[pl.ds(0, 3)]),
                (w_out, w_heads.at[3]),
                (tokens, all_tokens.at[y]),
                (cotangent_far, cotangent),
            )
        )
    ]
    for load in loads:
        load.start()
    greet([sibling] + along["x"] + along["y"] + along["z"])
    wait_all(loads)
    swaps = [
        go(w_ffn.at[1 - core], swap_ffn, sibling),
        go(w_heads.at[pl.ds(2 - 2 * core, 2)], swap_heads, sibling),
    ]
    for t in range(KW):
        taps[t] = sum(
            jnp.where(y == group, conv[t, :, group * GROUP : (group + 1) * GROUP], 0.0)
            for group in range(4)
        )
    wait_all(swaps)
    weights[core, y, x, z] = in_core_order(core, w_ffn[core], swap_ffn[...]).astype(jnp.bfloat16)
    kinds = pl.ds(2 * core, 2)
    w_all[kinds, x, z] = in_core_order(core, w_heads[kinds], swap_heads[...]).astype(jnp.bfloat16)
    ffn_one = []
    for (order, _, _), cols in zip(PARTS, columns):
        region = weights.at[core, y, x, z, :, cols]
        ffn_one += [go(region, region, other) for other in along[order[0]]]
    one = [device(x + k * (1 - core), y, z + k * core, core) for k in (1, 2, 3)]
    ahead, behind = along["y"][0], along["y"][2]
    spread = [go(all_tokens.at[y], all_tokens.at[y], other) for other in (ahead, behind)]
    heads_one = [go(w_all.at[kinds, x, z], w_all.at[kinds, x, z], other) for other in one]
    wait_all(heads_one)
    second = count.take(3)

    def heads_two(axis):
        at = (kinds, slice(None), z) if axis == "z" else (kinds, x)
        return [
            describe(w_all.at[at], w_all.at[at], second + k, along[axis][k]) for k in range(3)
        ]

    for number, axis in enumerate("zx"):

        @pl.when(core == number)
        def _():
            for copy in heads_two(axis):
                copy.start()

    wait_all(ffn_one)
    ffn_two = []
    for (order, _, _), cols in zip(PARTS, columns):
        region = weights.at[(core,) + cell(here, order[0]) + (slice(None), cols)]
        ffn_two += [go(region, region, other) for other in along[order[1]]]
    for number, axis in enumerate("zx"):

        @pl.when(core == number)
        def _():
            wait_all(heads_two(axis))

    heads_pair_copy = go(w_all.at[kinds], w_all.at[kinds], sibling)
    wait_all(ffn_two)
    ffn_three = []

    def last_hop():
        quarter = len(ffn_three)
        copies = []
        for (order, _, _), cols in zip(PARTS, columns):
            region = weights.at[
                (core,) + cell(here, order[1], {"y": quarter}) + (slice(None), cols)
            ]
            copies += [go(region, region, other) for other in along[order[2]]]
        ffn_three.append(copies)

    last_hop()
    last_hop()
    spread[0].wait()
    forwarded = [
        go(all_tokens.at[to("y", 3), pl.ds(0, 128)], all_tokens.at[to("y", 3), pl.ds(0, 128)], ahead)
    ]
    spread[1].wait()
    forwarded.append(
        go(all_tokens.at[to("y", 1), pl.ds(128, 128)], all_tokens.at[to("y", 1), pl.ds(128, 128)], behind)
    )
    heads_pair_copy.wait()
    half = pl.ds(2 * core, 2)
    wo_all[y] = w_all[3]
    projected[:, 0:8, :] = jnp.zeros((3, 8, GROUP), jnp.float32)
    key_ids = lax.broadcasted_iota(jnp.int32, (SEQ, 1), 0)
    bias = jnp.where(key_ids < length[0], 0.0, NEG_FILL)
    upper = (
        lax.broadcasted_iota(jnp.int32, (QUARTER, QUARTER), 0)
        <= lax.broadcasted_iota(jnp.int32, (QUARTER, QUARTER), 1)
    )

    def project(block):
        normed = (unit_rows(all_tokens[block])[0] * gains[0:1]).astype(jnp.bfloat16)
        for kind in range(3):
            projected[kind, rows(8 + block * QUARTER, QUARTER), :] = mul(
                normed, w_all[kind].reshape(D, GROUP)
            )

    def convolve(i):
        rows_i = slice(i * QUARTER, (i + 1) * QUARTER)
        for kind in range(3):
            base = 8 + i * QUARTER
            summed = taps[0, kind : kind + 1] * projected[kind, base : base + QUARTER, :]
            for t in range(1, KW):
                summed = summed + taps[t, kind : kind + 1] * projected[
                    kind, base - t : base - t + QUARTER, :
                ]
            stream = summed.astype(jnp.bfloat16)
            if kind == 0:
                stream = stream * jnp.bfloat16(SCALE)
            for head in range(GROUP_HEADS):
                streams[kind * GROUP_HEADS + head, rows_i, :] = stream[
                    :, head * HEAD_DIM : (head + 1) * HEAD_DIM
                ]

    for k in (0, 1, 3):
        project(to("y", k))
    wait_all(forwarded)
    wo_y = [go(w_all.at[3, half], wo_all.at[y, half], other) for other in along["y"]]
    project(to("y", 2))

    heads_send, heads_recv = count.take(4), count.take(4)

    def head_copy(i):
        return describe(
            att_send.at[i], attended.at[y], heads_send + i, device(x, i, z, core),
            heads_recv + (i - y + 3) % 4,
        )

    def attend(i):
        rows_i = slice(i * QUARTER, (i + 1) * QUARTER)
        keys = (i + 1) * QUARTER
        pieces = []
        for head in range(GROUP_HEADS):
            scores = mul(
                streams[GROUP_HEADS + head, :keys, :], streams[head, rows_i, :], NT
            ) + bias[:keys]
            corner = jnp.where(upper, scores[keys - QUARTER :], NEG_FILL)
            scores = corner if i == 0 else jnp.concatenate([scores[: keys - QUARTER], corner], 0)
            top = jnp.max(scores, axis=0, keepdims=True)
            lifted = jnp.exp(scores - top)
            total = jnp.sum(lifted, axis=0, keepdims=True)
            probs = (lifted * (1.0 / total)).astype(jnp.bfloat16)
            lse[head, :, rows_i] = top + jnp.log(total)
            pieces.append(mul(streams[2 * GROUP_HEADS + head, :keys, :], probs, TN).T)
        att_send[i] = jnp.concatenate(pieces, axis=1).astype(jnp.bfloat16)

        @pl.when(i != y)
        def _():
            head_copy(i).start()

    for i in range(4):
        convolve(i)
    attend(3)
    wait_all(wo_y)
    wo_pair = [
        go(wo_all.at[to("y", k), half], wo_all.at[to("y", k), half], sibling) for k in (1, 2, 3)
    ]
    pairing = []

    def pair_up(quarter):
        wait_all(ffn_three[quarter])
        pairing.append(go(weights.at[core, quarter], weights.at[core, quarter], sibling))

    pair_up(0)
    last_hop()
    pair_up(1)
    last_hop()
    attend(2)
    attend(1)
    attend(0)
    wait_all(wo_pair)
    attended[y] = att_send[y]
    for i in range(4):

        @pl.when(i != y)
        def _():
            head_copy(i).wait_send()

    for k in range(3):
        describe(
            att_send.at[0], attended.at[y], heads_send, along["y"][k], heads_recv + k
        ).wait_recv()

    mixed = all_tokens[y].astype(jnp.float32)
    for group in range(4):
        mixed = mixed + mul(attended[group], wo_all[group].reshape(D, GROUP), NT)
    middle[...] = mixed
    output[...] = mixed
    normed_two[...] = (unit_rows(mixed)[0] * gains[1:2]).astype(jnp.bfloat16)
    row_ids = lax.broadcasted_iota(jnp.int32, (QUARTER, 1), 0)
    real = row_ids + y * QUARTER < length[0]
    upstream[...] = jnp.where(real, cotangent[...].astype(jnp.float32), 0.0).astype(jnp.bfloat16)
    leaving = []
    stage_one = []
    right_own = jnp.where(core == 0, normed_two[...], upstream[...])
    right_other = jnp.where(core == 0, upstream[...], normed_two[...])

    def settle(quarter):
        leaving[quarter].wait()
        for step in range(4):
            raw_own[quarter, step] = total_of(
                raw_own[quarter, step], raw_in[quarter, step]
            ).astype(jnp.bfloat16)
        for number, ((order, _, _), cols) in enumerate(zip(RS_PARTS, columns)):
            for k in (1, 2, 3):
                index = cell(here, order[1], {"y": quarter, order[0]: to(order[0], k)})
                stage_one.append(
                    go(
                        raw_own.at[index + (slice(None), cols)],
                        f_one[number].at[k - 1, quarter],
                        along[order[0]][k - 1],
                    )
                )

    for quarter in range(4):
        pairing[quarter].wait()
        into = weights[0, quarter].reshape(D, D)
        back = weights[1, quarter].reshape(D, D)
        positive = jnp.maximum(mul(normed_two[...], into, NT), 0.0)
        active = (positive * positive).astype(jnp.bfloat16)
        grad_hidden = (mul(upstream[...], back, NT) * (2.0 * positive)).astype(jnp.bfloat16)
        output[...] += mul(active, back)
        grad_term = mul(grad_hidden, into)
        grad_middle[...] = grad_term if quarter == 0 else grad_middle[...] + grad_term
        left_own = jnp.where(core == 0, grad_hidden, active)
        left_other = jnp.where(core == 0, active, grad_hidden)
        shape = (4, 4, PAIR, D)
        raw_send[quarter % 2] = mul(left_other, right_other, TN).astype(jnp.bfloat16).reshape(shape)
        leaving.append(go(raw_send.at[quarter % 2], raw_in.at[quarter], sibling))
        raw_own[quarter] = mul(left_own, right_own, TN).astype(jnp.bfloat16).reshape(shape)
        if quarter >= 1:
            settle(quarter - 1)
        if quarter == 1:
            pair_up(2)
            pair_up(3)
    unit, inverse = unit_rows(middle[...])
    grad = grad_middle[...]
    gain_two[...] = jnp.sum(grad * unit, axis=0, keepdims=True)
    scaled = grad * gains[1:2]
    inner = jnp.mean(scaled * unit, axis=-1, keepdims=True)
    grad_all = jnp.where(real, cotangent[...].astype(jnp.float32), 0.0) + inverse * (
        scaled - unit * inner
    )
    grad_middle[...] = grad_all
    stores = []

    def store(near, far):
        copy = pltpu.make_async_copy(near, far, local_sem.at[len(stores)])
        copy.start()
        stores.append(copy)

    store(output, output_far)
    store(grad_middle, grad_middle_far)
    lower_rows = grad_all.astype(jnp.bfloat16)

    turned = []
    for k in (2, 1, 3):
        group = to("y", k)
        grad_rows[group] = mul(lower_rows, wo_all[group].reshape(D, GROUP)).astype(jnp.bfloat16)
        turned.append(go(grad_rows.at[group], grad_heads.at[y], along["y"][k - 1]))
    grad_heads[y] = mul(lower_rows, wo_all[y].reshape(D, GROUP)).astype(jnp.bfloat16)
    for group in range(4):
        raw_out[group] = (
            mul(lower_rows, attended[group], TN).astype(jnp.bfloat16).reshape(4, 4, PAIR, GROUP)
        )
    key_grad[...] = jnp.zeros_like(key_grad)
    value_grad[...] = jnp.zeros_like(value_grad)
    raw_conv[...] = jnp.zeros_like(raw_conv)
    raw_qkv[...] = jnp.zeros_like(raw_qkv)
    grad_stream[:, 0:8, :] = jnp.zeros((3, 8, GROUP), jnp.float32)
    for head in range(GROUP_HEADS):
        key_turned[head] = streams[GROUP_HEADS + head].T
    settle(3)
    wait_all(turned)
    out_one = [go(raw_out.at[to("y", k)], o_one.at[k - 1], along["y"][k - 1]) for k in (1, 2, 3)]

    def attend_back(i):
        rows_i = slice(i * QUARTER, (i + 1) * QUARTER)
        keys = (i + 1) * QUARTER
        grads = grad_heads[i]
        query_pieces = []
        for head in range(GROUP_HEADS):
            query = streams[head, rows_i, :]
            upstream_rows = grads[:, head * HEAD_DIM : (head + 1) * HEAD_DIM]
            scores = mul(streams[GROUP_HEADS + head, :keys, :], query, NT) + (
                bias[:keys] - lse[head, :, rows_i]
            )
            corner = jnp.where(upper, scores[keys - QUARTER :], NEG_FILL)
            scores = corner if i == 0 else jnp.concatenate([scores[: keys - QUARTER], corner], 0)
            probs = jnp.exp(scores)
            prob_grad = mul(streams[2 * GROUP_HEADS + head, :keys, :], upstream_rows, NT)
            centre = jnp.sum(prob_grad * probs, axis=0, keepdims=True)
            score_grad = (probs * (prob_grad - centre)).astype(jnp.bfloat16)
            query_pieces.append((mul(key_turned[head, :, :keys], score_grad) * SCALE).T)
            key_grad[head, :keys, :] += mul(score_grad, query)
            value_grad[head, :keys, :] += mul(probs.astype(jnp.bfloat16), upstream_rows)
        grad_stream[:, QUARTER:, :] = grad_stream[:, 0:8, :]
        for kind, pieces in (
            (0, query_pieces),
            (1, [key_grad[head, rows_i, :] for head in range(GROUP_HEADS)]),
            (2, [value_grad[head, rows_i, :] for head in range(GROUP_HEADS)]),
        ):
            grad_stream[kind, 0:QUARTER, :] = (
                jnp.concatenate(pieces, axis=1).astype(jnp.bfloat16).astype(jnp.float32)
            )
        unit_i = unit_rows(all_tokens[i])[0]
        normed_turned = (unit_i * gains[0:1]).astype(jnp.bfloat16).T
        total = None
        for kind in range(3):
            block = projected[kind, 8 + i * QUARTER : 8 + (i + 1) * QUARTER, :]
            summed = None
            for t in range(KW):
                shifted = grad_stream[kind, t : QUARTER + t, :]
                term = taps[t, kind : kind + 1] * shifted
                summed = term if summed is None else summed + term
                raw_conv[t, kind : kind + 1, :] += jnp.sum(shifted * block, axis=0, keepdims=True)
            lower = summed.astype(jnp.bfloat16)
            raw_qkv[kind] += mul(normed_turned, lower)
            term = mul(lower, w_all[kind].reshape(D, GROUP), NT)
            total = term if total is None else total + term
        normed_part[i] = total.astype(jnp.bfloat16)
        store(normed_part.at[i], normed_part_far.at[i])
        term = jnp.sum(total * unit_i, axis=0, keepdims=True)
        gain_one[...] = term if i == 3 else gain_one[...] + term

    attend_back(3)
    attend_back(2)
    wait_all(stage_one)
    stage_two = []
    for number, ((order, _, _), cols) in enumerate(zip(RS_PARTS, columns)):
        for quarter in range(4):
            index = cell(here, order[1], {"y": quarter}) + (slice(None), cols)
            raw_own[index] = total_of(
                raw_own[index], *(f_one[number][k, quarter] for k in range(3))
            ).astype(jnp.bfloat16)
        for k in (1, 2, 3):
            index = cell(here, order[2], {order[1]: to(order[1], k)})
            stage_two.append(
                go(
                    raw_own.at[index + (slice(None), cols)],
                    f_two[number].at[k - 1],
                    along[order[1]][k - 1],
                )
            )
    attend_back(1)
    wait_all(out_one)
    out_part[...] = total_of(raw_out[y], *(o_one[k] for k in range(3))).astype(jnp.bfloat16)
    out_two = [go(out_part.at[to("x", k)], o_two.at[k - 1], along["x"][k - 1]) for k in (1, 2, 3)]
    attend_back(0)
    qkv_low[...] = raw_qkv[...].reshape(3, 4, 4, PAIR, GROUP).astype(jnp.bfloat16)
    first_hop, second_hop = count.take(3), count.take(3)

    def qkv_one(axis):
        copies = []
        for k in (1, 2, 3):
            at = (slice(None), to("x", k)) if axis == "x" else (slice(None), slice(None), to("z", k))
            copies.append(
                describe(qkv_low.at[at], q_one.at[k - 1], first_hop + k - 1, along[axis][k - 1])
            )
        return copies

    def qkv_two(axis):
        return [
            describe(
                qkv_half.at[:, to(axis, k)], q_two.at[k - 1], second_hop + k - 1, along[axis][k - 1]
            )
            for k in (1, 2, 3)
        ]

    for number, axis in enumerate("xz"):

        @pl.when(core == number)
        def _():
            for copy in qkv_one(axis):
                copy.start()

    wait_all(out_two)
    out_part[x] = total_of(out_part[x], *(o_two[k] for k in range(3))).astype(jnp.bfloat16)
    out_three = [
        go(out_part.at[x, to("z", k)], o_three.at[k - 1], along["z"][k - 1]) for k in (1, 2, 3)
    ]
    small_own[...] = jnp.zeros_like(small_own)
    for row, gain in enumerate((gain_one[...], gain_two[...])):
        for group in range(4):
            small_own[4 * row + group : 4 * row + group + 1, :] = gain[
                :, group * GROUP : (group + 1) * GROUP
            ]
    for t in range(KW):
        small_own[8 + 3 * t : 11 + 3 * t, :] = raw_conv[t, 0:3, :]
    for number, axis in enumerate("xz"):

        @pl.when(core == number)
        def _():
            wait_all(qkv_one(axis))
            at = (slice(None), x) if axis == "x" else (slice(None), slice(None), z)
            qkv_half[...] = total_of(qkv_low[at], *(q_one[k] for k in range(3))).astype(jnp.bfloat16)
            for copy in qkv_two("zx"[number]):
                copy.start()

    wait_all(stage_two)
    stage_three = []
    for number, ((order, _, _), cols) in enumerate(zip(RS_PARTS, columns)):
        index = cell(here, order[2]) + (slice(None), cols)
        raw_own[index] = total_of(
            raw_own[index], *(f_two[number][k] for k in range(3))
        ).astype(jnp.bfloat16)
        for k in (1, 2, 3):
            index = cell(here, "", {order[2]: to(order[2], k)})
            stage_three.append(
                go(
                    raw_own.at[index + (slice(None), cols)],
                    f_three[number].at[k - 1],
                    along[order[2]][k - 1],
                )
            )
    wait_all(out_three)
    pair_out[3] = total_of(out_part[x, z], *(o_three[k] for k in range(3)))
    for number, axis in enumerate("zx"):

        @pl.when(core == number)
        def _():
            wait_all(qkv_two(axis))
            pair_out[0:3] = total_of(qkv_half[:, here[axis]], *(q_two[k] for k in range(3)))

    wait_all(stage_three)
    for number, cols in enumerate(columns):
        index = cell(here, "") + (slice(None), cols)
        ffn_pair[:, cols] = total_of(raw_own[index], *(f_three[number][k] for k in range(3)))
    lanes = jnp.sum(ffn_pair[...] * ffn_pair[...], axis=0, keepdims=True)
    squares = sum(lanes[:, group * GROUP : (group + 1) * GROUP] for group in range(4))
    small_own[17:18, :] = squares
    pairs = [go(pair_out, pair_in, sibling), go(small_own, small_in, sibling)]
    wait_all(pairs)
    heads_pair[...] = pair_out[...] + pair_in[...]
    lanes = jnp.sum(jnp.sum(heads_pair[...] * heads_pair[...], axis=0), axis=0, keepdims=True)
    row_ids = lax.broadcasted_iota(jnp.int32, (SMALL, GROUP), 0)
    small[...] = small_own[...] + small_in[...] + jnp.where(row_ids == 17, lanes, 0.0)
    wait_all(stores)


def layer(length, tokens, cotangent, gains, conv, w_qkv, w_out, w_ffn):
    f32, b16 = jnp.float32, jnp.bfloat16
    vmem = pl.BlockSpec(memory_space=pltpu.VMEM)
    far = pl.BlockSpec(memory_space=pl.ANY)
    blocks = (4, 4, PAIR)
    scratch = [
        pltpu.VMEM((QUARTER, D), b16),
        pltpu.VMEM((2, SUB, D), f32),
        pltpu.VMEM((QUARTER, D), f32),
        pltpu.VMEM((QUARTER, D), f32),
        pltpu.VMEM((4, QUARTER, D), b16),
        pltpu.VMEM((4, QUARTER, D), b16),
        pltpu.VMEM((3 * GROUP_HEADS, SEQ, HEAD_DIM), b16),
        pltpu.VMEM((3, SEQ + 8, GROUP), f32),
        pltpu.VMEM((GROUP_HEADS, 1, SEQ), f32),
        pltpu.VMEM((KW, 3, GROUP), f32),
        pltpu.VMEM((4, SUB, GROUP), f32),
        pltpu.VMEM((2, SUB, GROUP), f32),
        pltpu.VMEM((SUB, D), f32),
        pltpu.VMEM((4,) + blocks + (GROUP,), b16),
        pltpu.VMEM((4,) + blocks + (GROUP,), b16),
        pltpu.VMEM((4, QUARTER, GROUP), b16),
        pltpu.VMEM((4, QUARTER, GROUP), b16),
        pltpu.VMEM((2, 4) + blocks + (D,), b16),
        pltpu.VMEM((4,) + blocks + (D,), b16),
        pltpu.VMEM((2,) + blocks + (D,), b16),
        pltpu.VMEM((4,) + blocks + (D,), b16),
        pltpu.VMEM((QUARTER, D), f32),
        pltpu.VMEM((QUARTER, D), b16),
        pltpu.VMEM((QUARTER, D), b16),
        pltpu.VMEM((4, QUARTER, GROUP), b16),
        pltpu.VMEM((4, QUARTER, GROUP), b16),
        pltpu.VMEM((4,) + blocks + (GROUP,), b16),
    ]
    scratch += [pltpu.VMEM((3, 4, 4, PAIR, w), b16) for _, _, w in RS_PARTS]
    scratch += [pltpu.VMEM((3, 4, PAIR, w), b16) for _, _, w in RS_PARTS]
    scratch += [pltpu.VMEM((3, PAIR, w), b16) for _, _, w in RS_PARTS]
    scratch += [
        pltpu.VMEM((3,) + blocks + (GROUP,), b16),
        pltpu.VMEM((3, 4, PAIR, GROUP), b16),
        pltpu.VMEM((3, PAIR, GROUP), b16),
        pltpu.VMEM(blocks + (GROUP,), b16),
        pltpu.VMEM((GROUP_HEADS, SEQ, HEAD_DIM), f32),
        pltpu.VMEM((GROUP_HEADS, SEQ, HEAD_DIM), f32),
        pltpu.VMEM((GROUP_HEADS, HEAD_DIM, SEQ), b16),
        pltpu.VMEM((3, QUARTER + 8, GROUP), f32),
        pltpu.VMEM((KW, 8, GROUP), f32),
        pltpu.VMEM((3, D, GROUP), f32),
        pltpu.VMEM((3,) + blocks + (GROUP,), b16),
        pltpu.VMEM((3, 4, PAIR, GROUP), b16),
        pltpu.VMEM((3, 3, 4, PAIR, GROUP), b16),
        pltpu.VMEM((3, 3, PAIR, GROUP), b16),
        pltpu.VMEM((1, D), f32),
        pltpu.VMEM((1, D), f32),
        pltpu.VMEM((4, PAIR, GROUP), f32),
        pltpu.VMEM((4, PAIR, GROUP), f32),
        pltpu.VMEM((SMALL, GROUP), f32),
        pltpu.VMEM((SMALL, GROUP), f32),
        pltpu.SemaphoreType.DMA((160,)),
        pltpu.SemaphoreType.DMA((160,)),
        pltpu.SemaphoreType.DMA((11,)),
    ]
    return pl.pallas_call(
        layer_kernel,
        out_shape=[
            jax.ShapeDtypeStruct((QUARTER, D), f32),
            jax.ShapeDtypeStruct((QUARTER, D), f32),
            jax.ShapeDtypeStruct((4, QUARTER, D), b16),
            jax.ShapeDtypeStruct((SMALL, GROUP), f32),
            jax.ShapeDtypeStruct((PAIR, D), f32),
            jax.ShapeDtypeStruct((4, PAIR, GROUP), f32),
        ],
        in_specs=[pl.BlockSpec(memory_space=pltpu.SMEM)]
        + [far, far, vmem, vmem, far, far, far],
        out_specs=[pl.BlockSpec(memory_space=pl.ANY)] * 3 + [vmem] * 3,
        scratch_shapes=scratch,
        name="layer",
        compiler_params=pltpu.CompilerParams(
            collective_id=2, has_side_effects=True, vmem_limit_bytes=63 * 2**20
        ),
    )(length, tokens, cotangent, gains, conv, w_qkv, w_out, w_ffn)


UPPER = ((0, 0), (0, 1), (0, 2), (1, 1), (1, 2), (2, 2))
SUM_PARTS = ("xzy", "zyx", "yxz")
SMALL = 24


def adam(weight, gradient, moment_one, moment_two):
    first_new = BETA_ONE * moment_one + (1.0 - BETA_ONE) * gradient
    second_new = BETA_TWO * moment_two + (1.0 - BETA_TWO) * gradient * gradient
    stepped = (
        first_new
        / (1.0 - BETA_ONE**STEP)
        / (jnp.sqrt(second_new / (1.0 - BETA_TWO**STEP)) + ADAM_EPS)
    )
    return first_new, second_new, weight - ADAM_RATE * stepped


def tile(i):
    return slice(i * BLK, (i + 1) * BLK)


def optimizer_kernel(
    g_pair_far, g_heads_far, small_far, normed_part, m_ffn_far, m_qkv, m_out, tokens_far, grad_middle_far,
    gains, wide, g_mine, o_ffn, o_heads, input_grad,
    tokens, grad_middle, normed_in,
    g_pair, g_heads, small, m_ffn, m_heads, m_in, mh_in, s_x, s_z, s_y, iterate, head_iterate,
    part, gathered, r_one, r_two, r_three, hpart, hsum, hr_one, hr_two,
    g_high, g_low, z_high, z_low, t_high, t_low, gram, hgram,
    send_sem, recv_sem, local_sem,
):
    x, y, z, core = place()
    here = {"x": x, "y": y, "z": z}
    sems = (send_sem, recv_sem)
    sibling = device(x, y, z, 1 - core)
    along = neighbours(x, y, z, core)
    count = Counter()

    def go(source, target, other):
        return send(source, target, sems, count.take(), other)

    def to(axis, k):
        return (here[axis] + k) % 4

    own_rows = rows(core * SUB, SUB)
    their_rows = rows((1 - core) * SUB, SUB)
    loads = [
        pltpu.make_async_copy(far, near, local_sem.at[number])
        for number, (far, near) in enumerate(
            (
                (g_pair_far, g_pair),
                (g_heads_far, g_heads),
                (small_far, small),
                (m_ffn_far, m_ffn),
                (m_qkv, m_heads.at[pl.ds(0, 3)]),
                (m_out, m_heads.at[3]),
                (normed_part.at[y], normed_in.at[3]),
                (tokens_far, tokens),
                (grad_middle_far, grad_middle),
            )
        )
    ]
    for load in loads:
        load.start()
    greet([sibling] + along["x"] + along["y"] + along["z"])
    loads[2].wait()
    total = small[...]
    swaps = []
    for slots, axis in ((s_x, "x"), (s_z, "z")):
        at = here[axis]
        slots[at] = total
        copies = [go(slots.at[at], slots.at[at], other) for other in along[axis]]
        if not swaps:
            wait_all(loads[:2] + loads[3:])
            swaps = [
                go(g_pair.at[their_rows], g_mine.at[core], sibling),
                go(m_ffn.at[1 - core], m_in, sibling),
                go(m_heads.at[pl.ds(2 - 2 * core, 2)], mh_in, sibling),
            ]
            g_mine[core] = g_pair[own_rows, :]
        wait_all(copies)
        total = (slots[0] + slots[1]) + (slots[2] + slots[3])
    s_y[y] = total
    wait_all([go(s_y.at[y], s_y.at[y], other) for other in along["y"]])
    total = (s_y[0] + s_y[1]) + (s_y[2] + s_y[3])
    for group in range(4):
        lanes_of = slice(group * GROUP, (group + 1) * GROUP)
        for row in range(2):
            wide[row : row + 1, lanes_of] = total[4 * row + group : 4 * row + group + 1, :]
        wide[2:11, lanes_of] = s_y[group, 8:17, :]
    gain_sum = wide[0:2, :]
    conv_sum = wide[2:11, :]
    squared = (
        jnp.sum(gain_sum * gain_sum, axis=(0, 1), keepdims=True)
        + jnp.sum(conv_sum * conv_sum, axis=(0, 1), keepdims=True)
        + jnp.sum(total[17:18, :], axis=(0, 1), keepdims=True)
    )
    norm = jnp.sqrt(squared)
    wide[11:16, :] = jnp.broadcast_to(norm, (5, D))
    factor = CLIP_NORM / jnp.maximum(norm, CLIP_NORM)
    wait_all(swaps)
    for at, momentum in ((own_rows, m_ffn[core]), (their_rows, m_in[...])):
        iterate[at, :] = MOMENTUM * momentum + factor * g_pair[at, :]
    for kind in range(2):
        for at, momentum in ((own_rows, m_heads[2 * core + kind]), (their_rows, mh_in[kind])):
            head_iterate[kind, at, :] = MOMENTUM * momentum + factor * g_heads[2 * core + kind, at, :]
    transposed = (((0,), (0,)), ((), ()))
    for number, (i, j) in enumerate(UPPER):
        part[tile(number), :] = product(
            split(iterate[:, tile(i)]), split(iterate[:, tile(j)]), transposed
        )
    h_rows = lax.broadcasted_iota(jnp.int32, (GROUP, GROUP), 0)
    h_cols = lax.broadcasted_iota(jnp.int32, (GROUP, GROUP), 1)
    same = h_rows // HEAD_DIM == h_cols // HEAD_DIM
    h_eye = (h_rows == h_cols).astype(jnp.float32)
    packed = []
    for kind in range(2):
        pieces = split(head_iterate[kind])
        full = jnp.where(same, product(pieces, pieces, transposed), 0.0)
        folded = full[:, :HEAD_DIM]
        for head in range(1, GROUP_HEADS):
            folded = folded + full[:, head * HEAD_DIM : (head + 1) * HEAD_DIM]
        packed.append(folded)
    hpart[GROUP:, :] = jnp.zeros((BLK - GROUP, 2 * HEAD_DIM), jnp.float32)
    hpart[:GROUP, :] = jnp.concatenate(packed, axis=1)
    one = x + core * (z - x)
    two = z + core * (x - z)
    h_first = [device(x + k * (1 - core), y, z + k * core, core) for k in (1, 2, 3)]
    h_second = [device(x + k * core, y, z + k * (1 - core), core) for k in (1, 2, 3)]
    third = 6 * BLK // 3
    sizes = (third // 4, third // 16)
    h_sizes = (BLK // 4, BLK // 16)
    bases = [number * third for number in range(3)]
    h_base = 0
    for stage, slots in enumerate((r_one, r_two, r_three)):
        size = sizes[min(stage, 1)]
        copies = [
            go(
                part.at[rows(bases[number] + (to(order[stage], k) * size if stage < 2 else 0), size)],
                slots.at[number, k - 1],
                along[order[stage]][k - 1],
            )
            for number, order in enumerate(SUM_PARTS)
            for k in (1, 2, 3)
        ]
        if stage < 2:
            h_size, h_here = h_sizes[stage], (one, two)[stage]
            h_slots, h_others = ((hr_one, h_first), (hr_two, h_second))[stage]
            copies += [
                go(
                    hpart.at[rows(h_base + (h_here + k) % 4 * h_size, h_size)],
                    h_slots.at[k - 1],
                    h_others[k - 1],
                )
                for k in (1, 2, 3)
            ]
        wait_all(copies)
        target = gathered if stage == 2 else part
        for number, order in enumerate(SUM_PARTS):
            if stage < 2:
                bases[number] = bases[number] + here[order[stage]] * size
            at = rows(bases[number], size)
            target[at, :] = part[at, :] + (
                (slots[number, 0] + slots[number, 1]) + slots[number, 2]
            )
        if stage < 2:
            h_base = h_base + h_here * h_size
            at = rows(h_base, h_size)
            (hsum if stage == 1 else hpart)[at, :] = hpart[at, :] + (
                (h_slots[0] + h_slots[1]) + h_slots[2]
            )
    for stage in (1, 0):
        size = sizes[stage]
        copies = []
        for number, order in enumerate(SUM_PARTS):
            region = gathered.at[rows(bases[number], size)]
            copies += [go(region, region, other) for other in along[order[stage]]]
            bases[number] = bases[number] - here[order[stage]] * size
        region = hsum.at[rows(h_base, h_sizes[stage])]
        copies += [go(region, region, other) for other in (h_first, h_second)[stage]]
        h_base = h_base - (one, two)[stage] * h_sizes[stage]
        wait_all(copies)
    rows_out = [
        go(normed_part.at[to("y", k)], normed_in.at[k - 1], along["y"][k - 1]) for k in (1, 2, 3)
    ]
    eye = (
        lax.broadcasted_iota(jnp.int32, (BLK, BLK), 0)
        == lax.broadcasted_iota(jnp.int32, (BLK, BLK), 1)
    ).astype(jnp.float32)
    trace = jnp.zeros((1, 1), jnp.float32)
    for number, (i, j) in enumerate(UPPER):
        if i == j:
            trace = trace + jnp.sum(gathered[tile(number), :] * eye, axis=(0, 1), keepdims=True)
    scale = 1.0 / (jnp.sqrt(trace) + NS_EPS)

    def keep(high, low, i, j, block):
        upper_pieces = split(block)
        for kept, piece in zip((high, low), upper_pieces):
            kept[tile(i), tile(j)] = piece
            if i != j:
                kept[tile(j), tile(i)] = piece.T

    def symmetric(left, right, use, below=None):
        number = 0
        for i in range(3):
            across = slice(i * BLK, D)
            lines = (left[0][tile(i), :], left[1][tile(i), :])
            if i == 0 and below is not None:
                lines = [jnp.concatenate(pair, axis=0) for pair in zip(lines, split(below[...]))]
            row = product(lines, (right[0][:, across], right[1][:, across]))
            if i == 0 and below is not None:
                below[...] = row[BLK:]
                row = row[:BLK]
            for j in range(i, 3):
                use(number, i, j, row[:, (j - i) * BLK : (j - i + 1) * BLK])
                number += 1

    for number, (i, j) in enumerate(UPPER):
        block = gathered[tile(number), :] * (scale * scale)
        gram[number] = block
        keep(g_high, g_low, i, j, block)
    iterate[...] = iterate[...] * scale
    for kind in range(2):
        folded = hsum[:GROUP, kind * HEAD_DIM : (kind + 1) * HEAD_DIM]
        full = jnp.where(same, jnp.concatenate([folded] * GROUP_HEADS, axis=1), 0.0)
        on_diagonal = full * h_eye
        by_column = jnp.sum(on_diagonal, axis=0, keepdims=True)
        by_row = jnp.sum(on_diagonal, axis=1, keepdims=True)
        trace_row = jnp.sum(jnp.where(same, by_column, 0.0), axis=1, keepdims=True)
        trace_column = jnp.sum(jnp.where(same, by_row, 0.0), axis=0, keepdims=True)
        scale_column = 1.0 / (jnp.sqrt(trace_column) + NS_EPS)
        scale_row = 1.0 / (jnp.sqrt(trace_row) + NS_EPS)
        hgram[kind] = full * scale_row * scale_column
        head_iterate[kind] = head_iterate[kind] * scale_column

    def sweep_heads(last):
        for kind in range(2):
            current = hgram[kind]
            pieces = split(current)
            poly = COEF_A * h_eye + COEF_B * current + COEF_C * product(pieces, pieces)
            poly_pieces = split(poly)
            head_iterate[kind] = product(split(head_iterate[kind]), poly_pieces)
            if not last:
                hgram[kind] = product(split(product(pieces, poly_pieces)), poly_pieces)

    def sweep(last):
        def use_square(number, i, j, block):
            poly = COEF_B * gram[number] + COEF_C * block
            keep(z_high, z_low, i, j, poly + COEF_A * eye if i == j else poly)

        def use_half(number, i, j, block):
            keep(t_high, t_low, i, j, block)

        def use_gram(number, i, j, block):
            gram[number] = block
            keep(g_high, g_low, i, j, block)

        symmetric((g_high, g_low), (g_high, g_low), use_square)
        sweep_heads(last)
        if last:
            head_copies.extend(
                go(head_iterate.at[kind, their_rows], o_heads.at[2 * core + kind], sibling)
                for kind in range(2)
            )
        if last:
            iterate[...] = product(split(iterate[...]), (z_high[...], z_low[...]))
        else:
            symmetric((g_high, g_low), (z_high, z_low), use_half, iterate)
            symmetric((t_high, t_low), (z_high, z_low), use_gram)

    def body(_, carry):
        sweep(False)
        return carry

    head_copies = []
    lax.fori_loop(0, NS_ITERS - 1, body, 0)
    wait_all(rows_out)
    grad = total_of(*(normed_in[k] for k in range(4)))
    unit, inverse = unit_rows(tokens[...])
    scaled = grad * gains[0:1]
    inner = jnp.mean(scaled * unit, axis=-1, keepdims=True)
    input_grad[...] = grad_middle[...] + inverse * (scaled - unit * inner)
    sweep(True)
    copies = [go(iterate.at[their_rows], o_ffn.at[core], sibling)]
    o_ffn[core] = iterate[own_rows, :]
    for kind in range(2):
        o_heads[2 * core + kind] = head_iterate[kind, own_rows, :]
    wait_all(head_copies + copies)


def optimizer(g_pair, g_heads, small, normed_part, *others):
    f32, b16 = jnp.float32, jnp.bfloat16
    vmem = pl.BlockSpec(memory_space=pltpu.VMEM)
    third = 6 * BLK // 3
    scratch = [
        pltpu.VMEM((QUARTER, D), b16),
        pltpu.VMEM((QUARTER, D), f32),
        pltpu.VMEM((4, QUARTER, D), b16),
        pltpu.VMEM((PAIR, D), f32),
        pltpu.VMEM((4, PAIR, GROUP), f32),
        pltpu.VMEM((SMALL, GROUP), f32),
        pltpu.VMEM((2, SUB, D), f32),
        pltpu.VMEM((4, SUB, GROUP), f32),
        pltpu.VMEM((SUB, D), f32),
        pltpu.VMEM((2, SUB, GROUP), f32),
        pltpu.VMEM((4, SMALL, GROUP), f32),
        pltpu.VMEM((4, SMALL, GROUP), f32),
        pltpu.VMEM((4, SMALL, GROUP), f32),
        pltpu.VMEM((PAIR, D), f32),
        pltpu.VMEM((2, PAIR, GROUP), f32),
        pltpu.VMEM((6 * BLK, BLK), f32),
        pltpu.VMEM((6 * BLK, BLK), f32),
        pltpu.VMEM((3, 3, third // 4, BLK), f32),
        pltpu.VMEM((3, 3, third // 16, BLK), f32),
        pltpu.VMEM((3, 3, third // 16, BLK), f32),
        pltpu.VMEM((BLK, 2 * HEAD_DIM), f32),
        pltpu.VMEM((BLK, 2 * HEAD_DIM), f32),
        pltpu.VMEM((3, BLK // 4, 2 * HEAD_DIM), f32),
        pltpu.VMEM((3, BLK // 16, 2 * HEAD_DIM), f32),
    ]
    scratch += [pltpu.VMEM((D, D), b16)] * 6
    scratch += [
        pltpu.VMEM((6, BLK, BLK), f32),
        pltpu.VMEM((2, GROUP, GROUP), f32),
        pltpu.SemaphoreType.DMA((96,)),
        pltpu.SemaphoreType.DMA((96,)),
        pltpu.SemaphoreType.DMA((9,)),
    ]
    return pl.pallas_call(
        optimizer_kernel,
        out_shape=[
            jax.ShapeDtypeStruct((16, D), f32),
            jax.ShapeDtypeStruct((2, SUB, D), f32),
            jax.ShapeDtypeStruct((2, SUB, D), f32),
            jax.ShapeDtypeStruct((4, SUB, GROUP), f32),
            jax.ShapeDtypeStruct((QUARTER, D), f32),
        ],
        in_specs=[pl.BlockSpec(memory_space=pl.ANY)] * 9 + [vmem],
        out_specs=[vmem] * 5,
        scratch_shapes=scratch,
        name="optimizer",
        compiler_params=pltpu.CompilerParams(
            collective_id=0, has_side_effects=True, vmem_limit_bytes=63 * 2**20
        ),
    )(g_pair, g_heads, small, normed_part, *others)


def update_kernel(
    wide, g_ffn, g_heads, o_ffn, o_heads, grad_rows, out_rows,
    m_ffn, m_qkv, m_out, w_ffn, w_qkv, w_out,
    gains, conv, gain_first, gain_second, conv_first, conv_second,
    output, input_grad, out_gains, out_conv, out_qkv, out_out, out_ffn, out_norm,
    new_m_qkv, new_m_out, new_m_ffn,
    new_gain_first, new_gain_second, new_conv_first, new_conv_second, new_gains, new_conv,
    new_qkv, new_out, new_ffn,
):
    core = lax.axis_index("dp") % 2
    output[...] = out_rows[...]
    input_grad[...] = grad_rows[...]
    norm = wide[11:12, 0:1]
    out_norm[...] = norm
    factor = CLIP_NORM / jnp.maximum(norm, CLIP_NORM)
    grad = wide[0:2, :] * factor
    out_gains[...] = grad
    first, second, new = adam(gains[...], grad, gain_first[...], gain_second[...])
    new_gain_first[...], new_gain_second[...], new_gains[...] = first, second, new
    for t in range(KW):
        grad = wide[2 + 3 * t : 5 + 3 * t, :] * factor
        out_conv[t] = grad
        first, second, new = adam(conv[t], grad, conv_first[t], conv_second[t])
        new_conv_first[t], new_conv_second[t], new_conv[t] = first, second, new
    grad = g_ffn[...] * factor
    out_ffn[...] = grad
    new_m_ffn[...] = MOMENTUM * m_ffn[...] + grad
    new_ffn[...] = w_ffn[...] - RATE_IN * math.sqrt(max(FF, D)) * o_ffn[...]
    own_rows = rows(core * SUB, SUB)
    for kind in range(3):
        grad = g_heads[kind, own_rows, :] * factor
        out_qkv[kind] = grad
        new_m_qkv[kind] = MOMENTUM * m_qkv[kind] + grad
    new_qkv[...] = w_qkv[...] - RATE_IN * math.sqrt(D) * o_heads[0:3]
    grad = g_heads[3, own_rows, :] * factor
    out_out[...] = grad
    new_m_out[...] = MOMENTUM * m_out[...] + grad
    new_out[...] = w_out[...] - RATE_OUT * math.sqrt(D) * o_heads[3]


def update(*arrays):
    vmem = pl.BlockSpec(memory_space=pltpu.VMEM)
    m_ffn, m_qkv, m_out, _, _, _, gains, conv = arrays[7:15]
    rows_like = arrays[6]
    like = [rows_like, rows_like, gains, conv, m_qkv, m_out, m_ffn, None, m_qkv, m_out, m_ffn]
    like += [gains, gains, conv, conv, gains, conv, m_qkv, m_out, m_ffn]
    return pl.pallas_call(
        update_kernel,
        out_shape=[
            jax.ShapeDtypeStruct((1, 1) if entry is None else entry.shape, jnp.float32)
            for entry in like
        ],
        in_specs=[vmem] * len(arrays),
        out_specs=[vmem] * len(like),
        name="update",
        compiler_params=pltpu.CompilerParams(vmem_limit_bytes=63 * 2**20),
    )(*arrays)


def per_device(
    tokens,
    lengths,
    cotangent,
    gains,
    conv,
    w_qkv,
    w_out,
    ffn_weights,
    mom_qkv,
    mom_out,
    mom_ffn,
    gain_first,
    gain_second,
    conv_first,
    conv_second,
):
    rows_in = tokens[0]
    output, grad_middle, normed_part, small, ffn_pair, heads_pair = layer(
        lengths, rows_in, cotangent[0], gains, conv, w_qkv, w_out.T, ffn_weights
    )
    wide, g_ffn, o_ffn, o_heads, input_grad = optimizer(
        ffn_pair, heads_pair, small, normed_part, mom_ffn, mom_qkv, mom_out.T, rows_in, grad_middle, gains
    )
    updated = update(
        wide, g_ffn, heads_pair, o_ffn, o_heads, input_grad, output,
        mom_ffn, mom_qkv, mom_out.T, ffn_weights, w_qkv, w_out.T,
        gains, conv, gain_first, gain_second, conv_first, conv_second,
    )
    updated = list(updated)
    for number in (5, 9, 18):
        updated[number] = updated[number].T
    return (updated[0][None], updated[1][None], *updated[2:7], updated[7][0, 0], *updated[8:])


def solution(mesh):
    placed = (
        P("dp", "head", None),
        P("dp"),
        P("dp", "head", None),
        P(),
        P(),
        P(None, "dp", "head"),
        P("head", "dp"),
        P(None, ("head", "dp"), None),
        P(None, "dp", "head"),
        P("head", "dp"),
        P(None, ("head", "dp"), None),
        P(),
        P(),
        P(),
        P(),
    )
    return jax.shard_map(
        per_device,
        mesh=mesh,
        in_specs=placed,
        out_specs=(
            P("dp", "head", None),
            P("dp", "head", None),
            P(),
            P(),
            P(None, "dp", "head"),
            P("head", "dp"),
            P(None, ("head", "dp"), None),
            P(),
            P(None, "dp", "head"),
            P("head", "dp"),
            P(None, ("head", "dp"), None),
            P(),
            P(),
            P(),
            P(),
            P(),
            P(),
            P(None, "dp", "head"),
            P("head", "dp"),
            P(None, ("head", "dp"), None),
        ),
        check_vma=False,
    )
```

```python
import math

import jax
import jax.numpy as jnp
from jax import lax
from jax.experimental import pallas as pl
from jax.experimental.pallas import tpu as pltpu
from jax.sharding import PartitionSpec as P

D = 768
HEADS = 12
HEAD_DIM = 64
FF = 3072
KW = 3
NS_ITERS = 5
STEP = 10


NORM_EPS = 1e-06
NEG_FILL = -1e30
CLIP_NORM = 1.0
MOMENTUM = 0.95
RATE_IN = 0.02
RATE_OUT = 0.15
ADAM_RATE = 0.5
BETA_ONE = 0.9
BETA_TWO = 0.999
ADAM_EPS = 1e-08
NS_EPS = 1e-07
COEF_A = 3.4445
COEF_B = -4.775
COEF_C = 2.0315


SUB = 24
PAIR = 2 * SUB
BLK = 256
MESH_IDS = pl.DeviceIdType.MESH


def place():
    flat = lax.axis_index("dp")
    return flat // 8, lax.axis_index("head"), (flat // 2) % 4, flat % 2


def device(x, y, z, core):
    return (y % 4, ((x % 4) * 4 + z % 4) * 2 + core)


def greet(others):
    barrier = pltpu.get_barrier_semaphore()
    for other in others:
        pl.semaphore_signal(barrier, inc=1, device_id=other, device_id_type=MESH_IDS)
    pl.semaphore_wait(barrier, len(others))


def send(source, target, sems, index, other):
    copy = pltpu.make_async_remote_copy(
        src_ref=source,
        dst_ref=target,
        send_sem=sems[0].at[index],
        recv_sem=sems[1].at[index],
        device_id=other,
        device_id_type=MESH_IDS,
    )
    copy.start()
    return copy


def rows(start, count):
    return pl.ds(pl.multiple_of(start, 8), count)


def split(values):
    high = values.astype(jnp.bfloat16)
    return high, (values - high.astype(jnp.float32)).astype(jnp.bfloat16)


def product(left, right, dims=(((1,), (0,)), ((), ()))):
    lh, ll = left
    rh, rl = right

    def dot(a, b):
        return lax.dot_general(a, b, dims, preferred_element_type=jnp.float32)

    return dot(lh, rh) + (dot(lh, rl) + dot(ll, rh))


SEQ = 1024
QUARTER = SEQ // 4
GROUP = D // 4
GROUP_HEADS = GROUP // HEAD_DIM
SCALE = HEAD_DIM ** (-0.5)
NT = (((1,), (1,)), ((), ()))
TN = (((0,), (0,)), ((), ()))
NN = (((1,), (0,)), ((), ()))
PARTS = (("yzx", 0, 384), ("yxz", 384, 384))
RS_PARTS = (("xzy", 0, 384), ("zxy", 384, 384))


def mul(a, b, dims=NN):
    return lax.dot_general(a, b, dims, preferred_element_type=jnp.float32)


def neighbours(x, y, z, core):
    return {
        "x": [device(x + k, y, z, core) for k in (1, 2, 3)],
        "y": [device(x, y + k, z, core) for k in (1, 2, 3)],
        "z": [device(x, y, z + k, core) for k in (1, 2, 3)],
    }


def cell(here, free, moved=None):
    moved = moved or {}
    return tuple(slice(None) if a in free else moved.get(a, here[a]) for a in "yxz")


class Counter:
    def __init__(self):
        self.count = 0

    def take(self, many=1):
        self.count += many
        return self.count - many


def wait_all(copies):
    for copy in copies:
        copy.wait()


def in_core_order(core, own, other):
    return jnp.concatenate(
        [jnp.where(core == 0, own, other), jnp.where(core == 0, other, own)], axis=-2
    )


def unit_rows(values):
    values = values.astype(jnp.float32)
    inverse = lax.rsqrt(jnp.mean(values * values, axis=-1, keepdims=True) + NORM_EPS)
    return values * inverse, inverse


def total_of(*pieces):
    total = pieces[0].astype(jnp.float32)
    for piece in pieces[1:]:
        total = total + piece.astype(jnp.float32)
    return total


def layer_kernel(
    length, tokens, cotangent_far, gains, conv, w_qkv, w_out, w_ffn_far,
    output_far, grad_middle_far, normed_part_far, small, ffn_pair, heads_pair,
    cotangent, w_ffn, output, grad_middle, normed_part, all_tokens, streams, projected, lse, taps, w_heads, swap_heads, swap_ffn, w_all, wo_all,
    attended, att_send, weights, raw_own, raw_send, raw_in, middle, normed_two, upstream,
    grad_rows, grad_heads, raw_out, f_one_a, f_one_b, f_two_a, f_two_b, f_three_a, f_three_b,
    o_one, o_two, o_three, out_part, key_grad, value_grad, key_turned, grad_stream, raw_conv,
    raw_qkv, qkv_low, qkv_half, q_one, q_two, gain_one, gain_two, pair_out, pair_in,
    small_own, small_in,
    send_sem, recv_sem, local_sem,
):
    x, y, z, core = place()
    here = {"x": x, "y": y, "z": z}
    sems = (send_sem, recv_sem)
    sibling = device(x, y, z, 1 - core)
    along = neighbours(x, y, z, core)
    count = Counter()
    f_one, f_two, f_three = (f_one_a, f_one_b), (f_two_a, f_two_b), (f_three_a, f_three_b)
    columns = [slice(c, c + w) for _, c, w in PARTS]

    def describe(source, target, number, other, number_there=None):
        return pltpu.make_async_remote_copy(
            src_ref=source,
            dst_ref=target,
            send_sem=send_sem.at[number],
            recv_sem=recv_sem.at[number if number_there is None else number_there],
            device_id=other,
            device_id_type=MESH_IDS,
        )

    def go(source, target, other):
        return send(source, target, sems, count.take(), other)

    def to(axis, k):
        return (here[axis] + k) % 4

    loads = [
        pltpu.make_async_copy(far, near, local_sem.at[6 + number])
        for number, (far, near) in enumerate(
            (
                (w_ffn_far, w_ffn),
                (w_qkv, w_heads.at[pl.ds(0, 3)]),
                (w_out, w_heads.at[3]),
                (tokens, all_tokens.at[y]),
                (cotangent_far, cotangent),
            )
        )
    ]
    for load in loads:
        load.start()
    greet([sibling] + along["x"] + along["y"] + along["z"])
    wait_all(loads)
    swaps = [
        go(w_ffn.at[1 - core], swap_ffn, sibling),
        go(w_heads.at[pl.ds(2 - 2 * core, 2)], swap_heads, sibling),
    ]
    for t in range(KW):
        taps[t] = sum(
            jnp.where(y == group, conv[t, :, group * GROUP : (group + 1) * GROUP], 0.0)
            for group in range(4)
        )
    wait_all(swaps)
    weights[core, y, x, z] = in_core_order(core, w_ffn[core], swap_ffn[...]).astype(jnp.bfloat16)
    kinds = pl.ds(2 * core, 2)
    w_all[kinds, x, z] = in_core_order(core, w_heads[kinds], swap_heads[...]).astype(jnp.bfloat16)
    ffn_one = []
    for (order, _, _), cols in zip(PARTS, columns):
        region = weights.at[core, y, x, z, :, cols]
        ffn_one += [go(region, region, other) for other in along[order[0]]]
    one = [device(x + k * (1 - core), y, z + k * core, core) for k in (1, 2, 3)]
    ahead, behind = along["y"][0], along["y"][2]
    spread = [go(all_tokens.at[y], all_tokens.at[y], other) for other in (ahead, behind)]
    heads_one = [go(w_all.at[kinds, x, z], w_all.at[kinds, x, z], other) for other in one]
    wait_all(heads_one)
    second = count.take(3)

    def heads_two(axis):
        at = (kinds, slice(None), z) if axis == "z" else (kinds, x)
        return [
            describe(w_all.at[at], w_all.at[at], second + k, along[axis][k]) for k in range(3)
        ]

    for number, axis in enumerate("zx"):

        @pl.when(core == number)
        def _():
            for copy in heads_two(axis):
                copy.start()

    wait_all(ffn_one)
    ffn_two = []
    for (order, _, _), cols in zip(PARTS, columns):
        region = weights.at[(core,) + cell(here, order[0]) + (slice(None), cols)]
        ffn_two += [go(region, region, other) for other in along[order[1]]]
    for number, axis in enumerate("zx"):

        @pl.when(core == number)
        def _():
            wait_all(heads_two(axis))

    heads_pair_copy = go(w_all.at[kinds], w_all.at[kinds], sibling)
    wait_all(ffn_two)
    ffn_three = []

    def last_hop():
        quarter = len(ffn_three)
        copies = []
        for (order, _, _), cols in zip(PARTS, columns):
            region = weights.at[
                (core,) + cell(here, order[1], {"y": quarter}) + (slice(None), cols)
            ]
            copies += [go(region, region, other) for other in along[order[2]]]
        ffn_three.append(copies)

    last_hop()
    last_hop()
    spread[0].wait()
    forwarded = [
        go(all_tokens.at[to("y", 3), pl.ds(0, 128)], all_tokens.at[to("y", 3), pl.ds(0, 128)], ahead)
    ]
    spread[1].wait()
    forwarded.append(
        go(all_tokens.at[to("y", 1), pl.ds(128, 128)], all_tokens.at[to("y", 1), pl.ds(128, 128)], behind)
    )
    heads_pair_copy.wait()
    half = pl.ds(2 * core, 2)
    wo_all[y] = w_all[3]
    projected[:, 0:8, :] = jnp.zeros((3, 8, GROUP), jnp.float32)
    key_ids = lax.broadcasted_iota(jnp.int32, (SEQ, 1), 0)
    bias = jnp.where(key_ids < length[0], 0.0, NEG_FILL)
    upper = (
        lax.broadcasted_iota(jnp.int32, (QUARTER, QUARTER), 0)
        <= lax.broadcasted_iota(jnp.int32, (QUARTER, QUARTER), 1)
    )

    def project(block):
        normed = (unit_rows(all_tokens[block])[0] * gains[0:1]).astype(jnp.bfloat16)
        for kind in range(3):
            projected[kind, rows(8 + block * QUARTER, QUARTER), :] = mul(
                normed, w_all[kind].reshape(D, GROUP)
            )

    def convolve(i):
        rows_i = slice(i * QUARTER, (i + 1) * QUARTER)
        for kind in range(3):
            base = 8 + i * QUARTER
            summed = taps[0, kind : kind + 1] * projected[kind, base : base + QUARTER, :]
            for t in range(1, KW):
                summed = summed + taps[t, kind : kind + 1] * projected[
                    kind, base - t : base - t + QUARTER, :
                ]
            stream = summed.astype(jnp.bfloat16)
            if kind == 0:
                stream = stream * jnp.bfloat16(SCALE)
            for head in range(GROUP_HEADS):
                streams[kind * GROUP_HEADS + head, rows_i, :] = stream[
                    :, head * HEAD_DIM : (head + 1) * HEAD_DIM
                ]

    for k in (0, 1, 3):
        project(to("y", k))
    wait_all(forwarded)
    wo_y = [go(w_all.at[3, half], wo_all.at[y, half], other) for other in along["y"]]
    project(to("y", 2))

    heads_send, heads_recv = count.take(4), count.take(4)

    def head_copy(i):
        return describe(
            att_send.at[i], attended.at[y], heads_send + i, device(x, i, z, core),
            heads_recv + (i - y + 3) % 4,
        )

    def attend(i):
        rows_i = slice(i * QUARTER, (i + 1) * QUARTER)
        keys = (i + 1) * QUARTER
        pieces = []
        for head in range(GROUP_HEADS):
            scores = mul(
                streams[GROUP_HEADS + head, :keys, :], streams[head, rows_i, :], NT
            ) + bias[:keys]
            corner = jnp.where(upper, scores[keys - QUARTER :], NEG_FILL)
            scores = corner if i == 0 else jnp.concatenate([scores[: keys - QUARTER], corner], 0)
            top = jnp.max(scores, axis=0, keepdims=True)
            lifted = jnp.exp(scores - top)
            total = jnp.sum(lifted, axis=0, keepdims=True)
            probs = (lifted * (1.0 / total)).astype(jnp.bfloat16)
            lse[head, :, rows_i] = top + jnp.log(total)
            pieces.append(mul(streams[2 * GROUP_HEADS + head, :keys, :], probs, TN).T)
        att_send[i] = jnp.concatenate(pieces, axis=1).astype(jnp.bfloat16)

        @pl.when(i != y)
        def _():
            head_copy(i).start()

    for i in range(4):
        convolve(i)
    attend(3)
    wait_all(wo_y)
    wo_pair = [
        go(wo_all.at[to("y", k), half], wo_all.at[to("y", k), half], sibling) for k in (1, 2, 3)
    ]
    pairing = []

    def pair_up(quarter):
        wait_all(ffn_three[quarter])
        pairing.append(go(weights.at[core, quarter], weights.at[core, quarter], sibling))

    pair_up(0)
    last_hop()
    pair_up(1)
    last_hop()
    attend(2)
    attend(1)
    attend(0)
    wait_all(wo_pair)
    attended[y] = att_send[y]
    for i in range(4):

        @pl.when(i != y)
        def _():
            head_copy(i).wait_send()

    for k in range(3):
        describe(
            att_send.at[0], attended.at[y], heads_send, along["y"][k], heads_recv + k
        ).wait_recv()

    mixed = all_tokens[y].astype(jnp.float32)
    for group in range(4):
        mixed = mixed + mul(attended[group], wo_all[group].reshape(D, GROUP), NT)
    middle[...] = mixed
    output[...] = mixed
    normed_two[...] = (unit_rows(mixed)[0] * gains[1:2]).astype(jnp.bfloat16)
    row_ids = lax.broadcasted_iota(jnp.int32, (QUARTER, 1), 0)
    real = row_ids + y * QUARTER < length[0]
    upstream[...] = jnp.where(real, cotangent[...].astype(jnp.float32), 0.0).astype(jnp.bfloat16)
    leaving = []
    stage_one = []
    right_own = jnp.where(core == 0, normed_two[...], upstream[...])
    right_other = jnp.where(core == 0, upstream[...], normed_two[...])

    def settle(quarter):
        leaving[quarter].wait()
        for step in range(4):
            raw_own[quarter, step] = total_of(
                raw_own[quarter, step], raw_in[quarter, step]
            ).astype(jnp.bfloat16)
        for number, ((order, _, _), cols) in enumerate(zip(RS_PARTS, columns)):
            for k in (1, 2, 3):
                index = cell(here, order[1], {"y": quarter, order[0]: to(order[0], k)})
                stage_one.append(
                    go(
                        raw_own.at[index + (slice(None), cols)],
                        f_one[number].at[k - 1, quarter],
                        along[order[0]][k - 1],
                    )
                )

    for quarter in range(4):
        pairing[quarter].wait()
        into = weights[0, quarter].reshape(D, D)
        back = weights[1, quarter].reshape(D, D)
        positive = jnp.maximum(mul(normed_two[...], into, NT), 0.0)
        active = (positive * positive).astype(jnp.bfloat16)
        grad_hidden = (mul(upstream[...], back, NT) * (2.0 * positive)).astype(jnp.bfloat16)
        output[...] += mul(active, back)
        grad_term = mul(grad_hidden, into)
        grad_middle[...] = grad_term if quarter == 0 else grad_middle[...] + grad_term
        left_own = jnp.where(core == 0, grad_hidden, active)
        left_other = jnp.where(core == 0, active, grad_hidden)
        shape = (4, 4, PAIR, D)
        raw_send[quarter % 2] = mul(left_other, right_other, TN).astype(jnp.bfloat16).reshape(shape)
        leaving.append(go(raw_send.at[quarter % 2], raw_in.at[quarter], sibling))
        raw_own[quarter] = mul(left_own, right_own, TN).astype(jnp.bfloat16).reshape(shape)
        if quarter >= 1:
            settle(quarter - 1)
        if quarter == 1:
            pair_up(2)
            pair_up(3)
    unit, inverse = unit_rows(middle[...])
    grad = grad_middle[...]
    gain_two[...] = jnp.sum(grad * unit, axis=0, keepdims=True)
    scaled = grad * gains[1:2]
    inner = jnp.mean(scaled * unit, axis=-1, keepdims=True)
    grad_all = jnp.where(real, cotangent[...].astype(jnp.float32), 0.0) + inverse * (
        scaled - unit * inner
    )
    grad_middle[...] = grad_all
    stores = []

    def store(near, far):
        copy = pltpu.make_async_copy(near, far, local_sem.at[len(stores)])
        copy.start()
        stores.append(copy)

    store(output, output_far)
    store(grad_middle, grad_middle_far)
    lower_rows = grad_all.astype(jnp.bfloat16)

    turned = []
    for k in (2, 1, 3):
        group = to("y", k)
        grad_rows[group] = mul(lower_rows, wo_all[group].reshape(D, GROUP)).astype(jnp.bfloat16)
        turned.append(go(grad_rows.at[group], grad_heads.at[y], along["y"][k - 1]))
    grad_heads[y] = mul(lower_rows, wo_all[y].reshape(D, GROUP)).astype(jnp.bfloat16)
    settle(3)
    for group in range(4):
        raw_out[group] = (
            mul(lower_rows, attended[group], TN).astype(jnp.bfloat16).reshape(4, 4, PAIR, GROUP)
        )
    key_grad[...] = jnp.zeros_like(key_grad)
    value_grad[...] = jnp.zeros_like(value_grad)
    raw_conv[...] = jnp.zeros_like(raw_conv)
    raw_qkv[...] = jnp.zeros_like(raw_qkv)
    grad_stream[:, 0:8, :] = jnp.zeros((3, 8, GROUP), jnp.float32)
    for head in range(GROUP_HEADS):
        key_turned[head] = streams[GROUP_HEADS + head].T
    wait_all(turned)
    out_one = [go(raw_out.at[to("y", k)], o_one.at[k - 1], along["y"][k - 1]) for k in (1, 2, 3)]

    def attend_back(i):
        rows_i = slice(i * QUARTER, (i + 1) * QUARTER)
        keys = (i + 1) * QUARTER
        grads = grad_heads[i]
        query_pieces = []
        for head in range(GROUP_HEADS):
            query = streams[head, rows_i, :]
            upstream_rows = grads[:, head * HEAD_DIM : (head + 1) * HEAD_DIM]
            scores = mul(streams[GROUP_HEADS + head, :keys, :], query, NT) + (
                bias[:keys] - lse[head, :, rows_i]
            )
            corner = jnp.where(upper, scores[keys - QUARTER :], NEG_FILL)
            scores = corner if i == 0 else jnp.concatenate([scores[: keys - QUARTER], corner], 0)
            probs = jnp.exp(scores)
            prob_grad = mul(streams[2 * GROUP_HEADS + head, :keys, :], upstream_rows, NT)
            centre = jnp.sum(prob_grad * probs, axis=0, keepdims=True)
            score_grad = (probs * (prob_grad - centre)).astype(jnp.bfloat16)
            query_pieces.append((mul(key_turned[head, :, :keys], score_grad) * SCALE).T)
            key_grad[head, :keys, :] += mul(score_grad, query)
            value_grad[head, :keys, :] += mul(probs.astype(jnp.bfloat16), upstream_rows)
        grad_stream[:, QUARTER:, :] = grad_stream[:, 0:8, :]
        for kind, pieces in (
            (0, query_pieces),
            (1, [key_grad[head, rows_i, :] for head in range(GROUP_HEADS)]),
            (2, [value_grad[head, rows_i, :] for head in range(GROUP_HEADS)]),
        ):
            grad_stream[kind, 0:QUARTER, :] = (
                jnp.concatenate(pieces, axis=1).astype(jnp.bfloat16).astype(jnp.float32)
            )
        unit_i = unit_rows(all_tokens[i])[0]
        normed_turned = (unit_i * gains[0:1]).astype(jnp.bfloat16).T
        total = None
        for kind in range(3):
            block = projected[kind, 8 + i * QUARTER : 8 + (i + 1) * QUARTER, :]
            summed = None
            for t in range(KW):
                shifted = grad_stream[kind, t : QUARTER + t, :]
                term = taps[t, kind : kind + 1] * shifted
                summed = term if summed is None else summed + term
                raw_conv[t, kind : kind + 1, :] += jnp.sum(shifted * block, axis=0, keepdims=True)
            lower = summed.astype(jnp.bfloat16)
            raw_qkv[kind] += mul(normed_turned, lower)
            term = mul(lower, w_all[kind].reshape(D, GROUP), NT)
            total = term if total is None else total + term
        normed_part[i] = total.astype(jnp.bfloat16)
        store(normed_part.at[i], normed_part_far.at[i])
        term = jnp.sum(total * unit_i, axis=0, keepdims=True)
        gain_one[...] = term if i == 3 else gain_one[...] + term

    attend_back(3)
    attend_back(2)
    wait_all(stage_one)
    stage_two = []
    for number, ((order, _, _), cols) in enumerate(zip(RS_PARTS, columns)):
        for quarter in range(4):
            index = cell(here, order[1], {"y": quarter}) + (slice(None), cols)
            raw_own[index] = total_of(
                raw_own[index], *(f_one[number][k, quarter] for k in range(3))
            ).astype(jnp.bfloat16)
        for k in (1, 2, 3):
            index = cell(here, order[2], {order[1]: to(order[1], k)})
            stage_two.append(
                go(
                    raw_own.at[index + (slice(None), cols)],
                    f_two[number].at[k - 1],
                    along[order[1]][k - 1],
                )
            )
    attend_back(1)
    wait_all(out_one)
    out_part[...] = total_of(raw_out[y], *(o_one[k] for k in range(3))).astype(jnp.bfloat16)
    out_two = [go(out_part.at[to("x", k)], o_two.at[k - 1], along["x"][k - 1]) for k in (1, 2, 3)]
    attend_back(0)
    qkv_low[...] = raw_qkv[...].reshape(3, 4, 4, PAIR, GROUP).astype(jnp.bfloat16)
    first_hop, second_hop = count.take(3), count.take(3)

    def qkv_one(axis):
        copies = []
        for k in (1, 2, 3):
            at = (slice(None), to("x", k)) if axis == "x" else (slice(None), slice(None), to("z", k))
            copies.append(
                describe(qkv_low.at[at], q_one.at[k - 1], first_hop + k - 1, along[axis][k - 1])
            )
        return copies

    def qkv_two(axis):
        return [
            describe(
                qkv_half.at[:, to(axis, k)], q_two.at[k - 1], second_hop + k - 1, along[axis][k - 1]
            )
            for k in (1, 2, 3)
        ]

    for number, axis in enumerate("xz"):

        @pl.when(core == number)
        def _():
            for copy in qkv_one(axis):
                copy.start()

    wait_all(out_two)
    out_part[x] = total_of(out_part[x], *(o_two[k] for k in range(3))).astype(jnp.bfloat16)
    out_three = [
        go(out_part.at[x, to("z", k)], o_three.at[k - 1], along["z"][k - 1]) for k in (1, 2, 3)
    ]
    small_own[...] = jnp.zeros_like(small_own)
    for row, gain in enumerate((gain_one[...], gain_two[...])):
        for group in range(4):
            small_own[4 * row + group : 4 * row + group + 1, :] = gain[
                :, group * GROUP : (group + 1) * GROUP
            ]
    for t in range(KW):
        small_own[8 + 3 * t : 11 + 3 * t, :] = raw_conv[t, 0:3, :]
    for number, axis in enumerate("xz"):

        @pl.when(core == number)
        def _():
            wait_all(qkv_one(axis))
            at = (slice(None), x) if axis == "x" else (slice(None), slice(None), z)
            qkv_half[...] = total_of(qkv_low[at], *(q_one[k] for k in range(3))).astype(jnp.bfloat16)
            for copy in qkv_two("zx"[number]):
                copy.start()

    wait_all(stage_two)
    stage_three = []
    for number, ((order, _, _), cols) in enumerate(zip(RS_PARTS, columns)):
        index = cell(here, order[2]) + (slice(None), cols)
        raw_own[index] = total_of(
            raw_own[index], *(f_two[number][k] for k in range(3))
        ).astype(jnp.bfloat16)
        for k in (1, 2, 3):
            index = cell(here, "", {order[2]: to(order[2], k)})
            stage_three.append(
                go(
                    raw_own.at[index + (slice(None), cols)],
                    f_three[number].at[k - 1],
                    along[order[2]][k - 1],
                )
            )
    wait_all(out_three)
    pair_out[3] = total_of(out_part[x, z], *(o_three[k] for k in range(3)))
    for number, axis in enumerate("zx"):

        @pl.when(core == number)
        def _():
            wait_all(qkv_two(axis))
            pair_out[0:3] = total_of(qkv_half[:, here[axis]], *(q_two[k] for k in range(3)))

    wait_all(stage_three)
    for number, cols in enumerate(columns):
        index = cell(here, "") + (slice(None), cols)
        ffn_pair[:, cols] = total_of(raw_own[index], *(f_three[number][k] for k in range(3)))
    lanes = jnp.sum(ffn_pair[...] * ffn_pair[...], axis=0, keepdims=True)
    squares = sum(lanes[:, group * GROUP : (group + 1) * GROUP] for group in range(4))
    small_own[17:18, :] = squares
    pairs = [go(pair_out, pair_in, sibling), go(small_own, small_in, sibling)]
    wait_all(pairs)
    heads_pair[...] = pair_out[...] + pair_in[...]
    lanes = jnp.sum(jnp.sum(heads_pair[...] * heads_pair[...], axis=0), axis=0, keepdims=True)
    row_ids = lax.broadcasted_iota(jnp.int32, (SMALL, GROUP), 0)
    small[...] = small_own[...] + small_in[...] + jnp.where(row_ids == 17, lanes, 0.0)
    wait_all(stores)


def layer(length, tokens, cotangent, gains, conv, w_qkv, w_out, w_ffn):
    f32, b16 = jnp.float32, jnp.bfloat16
    vmem = pl.BlockSpec(memory_space=pltpu.VMEM)
    far = pl.BlockSpec(memory_space=pl.ANY)
    blocks = (4, 4, PAIR)
    scratch = [
        pltpu.VMEM((QUARTER, D), b16),
        pltpu.VMEM((2, SUB, D), f32),
        pltpu.VMEM((QUARTER, D), f32),
        pltpu.VMEM((QUARTER, D), f32),
        pltpu.VMEM((4, QUARTER, D), b16),
        pltpu.VMEM((4, QUARTER, D), b16),
        pltpu.VMEM((3 * GROUP_HEADS, SEQ, HEAD_DIM), b16),
        pltpu.VMEM((3, SEQ + 8, GROUP), f32),
        pltpu.VMEM((GROUP_HEADS, 1, SEQ), f32),
        pltpu.VMEM((KW, 3, GROUP), f32),
        pltpu.VMEM((4, SUB, GROUP), f32),
        pltpu.VMEM((2, SUB, GROUP), f32),
        pltpu.VMEM((SUB, D), f32),
        pltpu.VMEM((4,) + blocks + (GROUP,), b16),
        pltpu.VMEM((4,) + blocks + (GROUP,), b16),
        pltpu.VMEM((4, QUARTER, GROUP), b16),
        pltpu.VMEM((4, QUARTER, GROUP), b16),
        pltpu.VMEM((2, 4) + blocks + (D,), b16),
        pltpu.VMEM((4,) + blocks + (D,), b16),
        pltpu.VMEM((2,) + blocks + (D,), b16),
        pltpu.VMEM((4,) + blocks + (D,), b16),
        pltpu.VMEM((QUARTER, D), f32),
        pltpu.VMEM((QUARTER, D), b16),
        pltpu.VMEM((QUARTER, D), b16),
        pltpu.VMEM((4, QUARTER, GROUP), b16),
        pltpu.VMEM((4, QUARTER, GROUP), b16),
        pltpu.VMEM((4,) + blocks + (GROUP,), b16),
    ]
    scratch += [pltpu.VMEM((3, 4, 4, PAIR, w), b16) for _, _, w in RS_PARTS]
    scratch += [pltpu.VMEM((3, 4, PAIR, w), b16) for _, _, w in RS_PARTS]
    scratch += [pltpu.VMEM((3, PAIR, w), b16) for _, _, w in RS_PARTS]
    scratch += [
        pltpu.VMEM((3,) + blocks + (GROUP,), b16),
        pltpu.VMEM((3, 4, PAIR, GROUP), b16),
        pltpu.VMEM((3, PAIR, GROUP), b16),
        pltpu.VMEM(blocks + (GROUP,), b16),
        pltpu.VMEM((GROUP_HEADS, SEQ, HEAD_DIM), f32),
        pltpu.VMEM((GROUP_HEADS, SEQ, HEAD_DIM), f32),
        pltpu.VMEM((GROUP_HEADS, HEAD_DIM, SEQ), b16),
        pltpu.VMEM((3, QUARTER + 8, GROUP), f32),
        pltpu.VMEM((KW, 8, GROUP), f32),
        pltpu.VMEM((3, D, GROUP), f32),
        pltpu.VMEM((3,) + blocks + (GROUP,), b16),
        pltpu.VMEM((3, 4, PAIR, GROUP), b16),
        pltpu.VMEM((3, 3, 4, PAIR, GROUP), b16),
        pltpu.VMEM((3, 3, PAIR, GROUP), b16),
        pltpu.VMEM((1, D), f32),
        pltpu.VMEM((1, D), f32),
        pltpu.VMEM((4, PAIR, GROUP), f32),
        pltpu.VMEM((4, PAIR, GROUP), f32),
        pltpu.VMEM((SMALL, GROUP), f32),
        pltpu.VMEM((SMALL, GROUP), f32),
        pltpu.SemaphoreType.DMA((160,)),
        pltpu.SemaphoreType.DMA((160,)),
        pltpu.SemaphoreType.DMA((11,)),
    ]
    return pl.pallas_call(
        layer_kernel,
        out_shape=[
            jax.ShapeDtypeStruct((QUARTER, D), f32),
            jax.ShapeDtypeStruct((QUARTER, D), f32),
            jax.ShapeDtypeStruct((4, QUARTER, D), b16),
            jax.ShapeDtypeStruct((SMALL, GROUP), f32),
            jax.ShapeDtypeStruct((PAIR, D), f32),
            jax.ShapeDtypeStruct((4, PAIR, GROUP), f32),
        ],
        in_specs=[pl.BlockSpec(memory_space=pltpu.SMEM)]
        + [far, far, vmem, vmem, far, far, far],
        out_specs=[pl.BlockSpec(memory_space=pl.ANY)] * 3 + [vmem] * 3,
        scratch_shapes=scratch,
        name="layer",
        compiler_params=pltpu.CompilerParams(
            collective_id=2, has_side_effects=True, vmem_limit_bytes=63 * 2**20
        ),
    )(length, tokens, cotangent, gains, conv, w_qkv, w_out, w_ffn)


UPPER = ((0, 0), (0, 1), (0, 2), (1, 1), (1, 2), (2, 2))
SUM_PARTS = ("xzy", "zyx", "yxz")
SMALL = 24


def adam(weight, gradient, moment_one, moment_two):
    first_new = BETA_ONE * moment_one + (1.0 - BETA_ONE) * gradient
    second_new = BETA_TWO * moment_two + (1.0 - BETA_TWO) * gradient * gradient
    stepped = (
        first_new
        / (1.0 - BETA_ONE**STEP)
        / (jnp.sqrt(second_new / (1.0 - BETA_TWO**STEP)) + ADAM_EPS)
    )
    return first_new, second_new, weight - ADAM_RATE * stepped


def tile(i):
    return slice(i * BLK, (i + 1) * BLK)


def optimizer_kernel(
    g_pair_far, g_heads_far, small_far, normed_part, m_ffn_far, m_qkv, m_out, tokens_far, grad_middle_far,
    gains, wide, g_mine, o_ffn, o_heads, input_grad,
    tokens, grad_middle, normed_in,
    g_pair, g_heads, small, m_ffn, m_heads, m_in, mh_in, s_x, s_z, s_y, iterate, head_iterate,
    part, gathered, r_one, r_two, r_three, hpart, hsum, hr_one, hr_two,
    g_high, g_low, z_high, z_low, t_high, t_low, gram, hgram,
    send_sem, recv_sem, local_sem,
):
    x, y, z, core = place()
    here = {"x": x, "y": y, "z": z}
    sems = (send_sem, recv_sem)
    sibling = device(x, y, z, 1 - core)
    along = neighbours(x, y, z, core)
    count = Counter()

    def go(source, target, other):
        return send(source, target, sems, count.take(), other)

    def to(axis, k):
        return (here[axis] + k) % 4

    own_rows = rows(core * SUB, SUB)
    their_rows = rows((1 - core) * SUB, SUB)
    loads = [
        pltpu.make_async_copy(far, near, local_sem.at[number])
        for number, (far, near) in enumerate(
            (
                (g_pair_far, g_pair),
                (g_heads_far, g_heads),
                (small_far, small),
                (m_ffn_far, m_ffn),
                (m_qkv, m_heads.at[pl.ds(0, 3)]),
                (m_out, m_heads.at[3]),
                (normed_part.at[y], normed_in.at[3]),
                (tokens_far, tokens),
                (grad_middle_far, grad_middle),
            )
        )
    ]
    for load in loads:
        load.start()
    greet([sibling] + along["x"] + along["y"] + along["z"])
    loads[2].wait()
    total = small[...]
    swaps = []
    for slots, axis in ((s_x, "x"), (s_z, "z")):
        at = here[axis]
        slots[at] = total
        copies = [go(slots.at[at], slots.at[at], other) for other in along[axis]]
        if not swaps:
            wait_all(loads[:2] + loads[3:])
            swaps = [
                go(g_pair.at[their_rows], g_mine.at[core], sibling),
                go(m_ffn.at[1 - core], m_in, sibling),
                go(m_heads.at[pl.ds(2 - 2 * core, 2)], mh_in, sibling),
            ]
            g_mine[core] = g_pair[own_rows, :]
        wait_all(copies)
        total = (slots[0] + slots[1]) + (slots[2] + slots[3])
    s_y[y] = total
    wait_all([go(s_y.at[y], s_y.at[y], other) for other in along["y"]])
    total = (s_y[0] + s_y[1]) + (s_y[2] + s_y[3])
    for group in range(4):
        lanes_of = slice(group * GROUP, (group + 1) * GROUP)
        for row in range(2):
            wide[row : row + 1, lanes_of] = total[4 * row + group : 4 * row + group + 1, :]
        wide[2:11, lanes_of] = s_y[group, 8:17, :]
    gain_sum = wide[0:2, :]
    conv_sum = wide[2:11, :]
    squared = (
        jnp.sum(gain_sum * gain_sum, axis=(0, 1), keepdims=True)
        + jnp.sum(conv_sum * conv_sum, axis=(0, 1), keepdims=True)
        + jnp.sum(total[17:18, :], axis=(0, 1), keepdims=True)
    )
    norm = jnp.sqrt(squared)
    wide[11:16, :] = jnp.broadcast_to(norm, (5, D))
    factor = CLIP_NORM / jnp.maximum(norm, CLIP_NORM)
    wait_all(swaps)
    for at, momentum in ((own_rows, m_ffn[core]), (their_rows, m_in[...])):
        iterate[at, :] = MOMENTUM * momentum + factor * g_pair[at, :]
    for kind in range(2):
        for at, momentum in ((own_rows, m_heads[2 * core + kind]), (their_rows, mh_in[kind])):
            head_iterate[kind, at, :] = MOMENTUM * momentum + factor * g_heads[2 * core + kind, at, :]
    transposed = (((0,), (0,)), ((), ()))
    for number, (i, j) in enumerate(UPPER):
        part[tile(number), :] = product(
            split(iterate[:, tile(i)]), split(iterate[:, tile(j)]), transposed
        )
    h_rows = lax.broadcasted_iota(jnp.int32, (GROUP, GROUP), 0)
    h_cols = lax.broadcasted_iota(jnp.int32, (GROUP, GROUP), 1)
    same = h_rows // HEAD_DIM == h_cols // HEAD_DIM
    h_eye = (h_rows == h_cols).astype(jnp.float32)
    packed = []
    for kind in range(2):
        pieces = split(head_iterate[kind])
        full = jnp.where(same, product(pieces, pieces, transposed), 0.0)
        folded = full[:, :HEAD_DIM]
        for head in range(1, GROUP_HEADS):
            folded = folded + full[:, head * HEAD_DIM : (head + 1) * HEAD_DIM]
        packed.append(folded)
    hpart[GROUP:, :] = jnp.zeros((BLK - GROUP, 2 * HEAD_DIM), jnp.float32)
    hpart[:GROUP, :] = jnp.concatenate(packed, axis=1)
    one = x + core * (z - x)
    two = z + core * (x - z)
    h_first = [device(x + k * (1 - core), y, z + k * core, core) for k in (1, 2, 3)]
    h_second = [device(x + k * core, y, z + k * (1 - core), core) for k in (1, 2, 3)]
    third = 6 * BLK // 3
    sizes = (third // 4, third // 16)
    h_sizes = (BLK // 4, BLK // 16)
    bases = [number * third for number in range(3)]
    h_base = 0
    for stage, slots in enumerate((r_one, r_two, r_three)):
        size = sizes[min(stage, 1)]
        copies = [
            go(
                part.at[rows(bases[number] + (to(order[stage], k) * size if stage < 2 else 0), size)],
                slots.at[number, k - 1],
                along[order[stage]][k - 1],
            )
            for number, order in enumerate(SUM_PARTS)
            for k in (1, 2, 3)
        ]
        if stage < 2:
            h_size, h_here = h_sizes[stage], (one, two)[stage]
            h_slots, h_others = ((hr_one, h_first), (hr_two, h_second))[stage]
            copies += [
                go(
                    hpart.at[rows(h_base + (h_here + k) % 4 * h_size, h_size)],
                    h_slots.at[k - 1],
                    h_others[k - 1],
                )
                for k in (1, 2, 3)
            ]
        wait_all(copies)
        target = gathered if stage == 2 else part
        for number, order in enumerate(SUM_PARTS):
            if stage < 2:
                bases[number] = bases[number] + here[order[stage]] * size
            at = rows(bases[number], size)
            target[at, :] = part[at, :] + (
                (slots[number, 0] + slots[number, 1]) + slots[number, 2]
            )
        if stage < 2:
            h_base = h_base + h_here * h_size
            at = rows(h_base, h_size)
            (hsum if stage == 1 else hpart)[at, :] = hpart[at, :] + (
                (h_slots[0] + h_slots[1]) + h_slots[2]
            )
    for stage in (1, 0):
        size = sizes[stage]
        copies = []
        for number, order in enumerate(SUM_PARTS):
            region = gathered.at[rows(bases[number], size)]
            copies += [go(region, region, other) for other in along[order[stage]]]
            bases[number] = bases[number] - here[order[stage]] * size
        region = hsum.at[rows(h_base, h_sizes[stage])]
        copies += [go(region, region, other) for other in (h_first, h_second)[stage]]
        h_base = h_base - (one, two)[stage] * h_sizes[stage]
        wait_all(copies)
    rows_out = [
        go(normed_part.at[to("y", k)], normed_in.at[k - 1], along["y"][k - 1]) for k in (1, 2, 3)
    ]
    eye = (
        lax.broadcasted_iota(jnp.int32, (BLK, BLK), 0)
        == lax.broadcasted_iota(jnp.int32, (BLK, BLK), 1)
    ).astype(jnp.float32)
    trace = jnp.zeros((1, 1), jnp.float32)
    for number, (i, j) in enumerate(UPPER):
        if i == j:
            trace = trace + jnp.sum(gathered[tile(number), :] * eye, axis=(0, 1), keepdims=True)
    scale = 1.0 / (jnp.sqrt(trace) + NS_EPS)

    def keep(high, low, i, j, block):
        upper_pieces = split(block)
        for kept, piece in zip((high, low), upper_pieces):
            kept[tile(i), tile(j)] = piece
            if i != j:
                kept[tile(j), tile(i)] = piece.T

    def symmetric(left, right, use, below=None):
        number = 0
        for i in range(3):
            across = slice(i * BLK, D)
            lines = (left[0][tile(i), :], left[1][tile(i), :])
            if i == 0 and below is not None:
                lines = [jnp.concatenate(pair, axis=0) for pair in zip(lines, split(below[...]))]
            row = product(lines, (right[0][:, across], right[1][:, across]))
            if i == 0 and below is not None:
                below[...] = row[BLK:]
                row = row[:BLK]
            for j in range(i, 3):
                use(number, i, j, row[:, (j - i) * BLK : (j - i + 1) * BLK])
                number += 1

    for number, (i, j) in enumerate(UPPER):
        block = gathered[tile(number), :] * (scale * scale)
        gram[number] = block
        keep(g_high, g_low, i, j, block)
    iterate[...] = iterate[...] * scale
    for kind in range(2):
        folded = hsum[:GROUP, kind * HEAD_DIM : (kind + 1) * HEAD_DIM]
        full = jnp.where(same, jnp.concatenate([folded] * GROUP_HEADS, axis=1), 0.0)
        on_diagonal = full * h_eye
        by_column = jnp.sum(on_diagonal, axis=0, keepdims=True)
        by_row = jnp.sum(on_diagonal, axis=1, keepdims=True)
        trace_row = jnp.sum(jnp.where(same, by_column, 0.0), axis=1, keepdims=True)
        trace_column = jnp.sum(jnp.where(same, by_row, 0.0), axis=0, keepdims=True)
        scale_column = 1.0 / (jnp.sqrt(trace_column) + NS_EPS)
        scale_row = 1.0 / (jnp.sqrt(trace_row) + NS_EPS)
        hgram[kind] = full * scale_row * scale_column
        head_iterate[kind] = head_iterate[kind] * scale_column

    def sweep_heads(last):
        for kind in range(2):
            current = hgram[kind]
            pieces = split(current)
            poly = COEF_A * h_eye + COEF_B * current + COEF_C * product(pieces, pieces)
            poly_pieces = split(poly)
            head_iterate[kind] = product(split(head_iterate[kind]), poly_pieces)
            if not last:
                hgram[kind] = product(split(product(pieces, poly_pieces)), poly_pieces)

    def sweep(last):
        def use_square(number, i, j, block):
            poly = COEF_B * gram[number] + COEF_C * block
            keep(z_high, z_low, i, j, poly + COEF_A * eye if i == j else poly)

        def use_half(number, i, j, block):
            keep(t_high, t_low, i, j, block)

        def use_gram(number, i, j, block):
            gram[number] = block
            keep(g_high, g_low, i, j, block)

        symmetric((g_high, g_low), (g_high, g_low), use_square)
        sweep_heads(last)
        if last:
            head_copies.extend(
                go(head_iterate.at[kind, their_rows], o_heads.at[2 * core + kind], sibling)
                for kind in range(2)
            )
        if last:
            iterate[...] = product(split(iterate[...]), (z_high[...], z_low[...]))
        else:
            symmetric((g_high, g_low), (z_high, z_low), use_half, iterate)
            symmetric((t_high, t_low), (z_high, z_low), use_gram)

    def body(_, carry):
        sweep(False)
        return carry

    head_copies = []
    lax.fori_loop(0, NS_ITERS - 1, body, 0)
    wait_all(rows_out)
    grad = total_of(*(normed_in[k] for k in range(4)))
    unit, inverse = unit_rows(tokens[...])
    scaled = grad * gains[0:1]
    inner = jnp.mean(scaled * unit, axis=-1, keepdims=True)
    input_grad[...] = grad_middle[...] + inverse * (scaled - unit * inner)
    sweep(True)
    copies = [go(iterate.at[their_rows], o_ffn.at[core], sibling)]
    o_ffn[core] = iterate[own_rows, :]
    for kind in range(2):
        o_heads[2 * core + kind] = head_iterate[kind, own_rows, :]
    wait_all(head_copies + copies)


def optimizer(g_pair, g_heads, small, normed_part, *others):
    f32, b16 = jnp.float32, jnp.bfloat16
    vmem = pl.BlockSpec(memory_space=pltpu.VMEM)
    third = 6 * BLK // 3
    scratch = [
        pltpu.VMEM((QUARTER, D), b16),
        pltpu.VMEM((QUARTER, D), f32),
        pltpu.VMEM((4, QUARTER, D), b16),
        pltpu.VMEM((PAIR, D), f32),
        pltpu.VMEM((4, PAIR, GROUP), f32),
        pltpu.VMEM((SMALL, GROUP), f32),
        pltpu.VMEM((2, SUB, D), f32),
        pltpu.VMEM((4, SUB, GROUP), f32),
        pltpu.VMEM((SUB, D), f32),
        pltpu.VMEM((2, SUB, GROUP), f32),
        pltpu.VMEM((4, SMALL, GROUP), f32),
        pltpu.VMEM((4, SMALL, GROUP), f32),
        pltpu.VMEM((4, SMALL, GROUP), f32),
        pltpu.VMEM((PAIR, D), f32),
        pltpu.VMEM((2, PAIR, GROUP), f32),
        pltpu.VMEM((6 * BLK, BLK), f32),
        pltpu.VMEM((6 * BLK, BLK), f32),
        pltpu.VMEM((3, 3, third // 4, BLK), f32),
        pltpu.VMEM((3, 3, third // 16, BLK), f32),
        pltpu.VMEM((3, 3, third // 16, BLK), f32),
        pltpu.VMEM((BLK, 2 * HEAD_DIM), f32),
        pltpu.VMEM((BLK, 2 * HEAD_DIM), f32),
        pltpu.VMEM((3, BLK // 4, 2 * HEAD_DIM), f32),
        pltpu.VMEM((3, BLK // 16, 2 * HEAD_DIM), f32),
    ]
    scratch += [pltpu.VMEM((D, D), b16)] * 6
    scratch += [
        pltpu.VMEM((6, BLK, BLK), f32),
        pltpu.VMEM((2, GROUP, GROUP), f32),
        pltpu.SemaphoreType.DMA((96,)),
        pltpu.SemaphoreType.DMA((96,)),
        pltpu.SemaphoreType.DMA((9,)),
    ]
    return pl.pallas_call(
        optimizer_kernel,
        out_shape=[
            jax.ShapeDtypeStruct((16, D), f32),
            jax.ShapeDtypeStruct((2, SUB, D), f32),
            jax.ShapeDtypeStruct((2, SUB, D), f32),
            jax.ShapeDtypeStruct((4, SUB, GROUP), f32),
            jax.ShapeDtypeStruct((QUARTER, D), f32),
        ],
        in_specs=[pl.BlockSpec(memory_space=pl.ANY)] * 9 + [vmem],
        out_specs=[vmem] * 5,
        scratch_shapes=scratch,
        name="optimizer",
        compiler_params=pltpu.CompilerParams(
            collective_id=0, has_side_effects=True, vmem_limit_bytes=63 * 2**20
        ),
    )(g_pair, g_heads, small, normed_part, *others)


def update_kernel(
    wide, g_ffn, g_heads, o_ffn, o_heads, grad_rows, out_rows,
    m_ffn, m_qkv, m_out, w_ffn, w_qkv, w_out,
    gains, conv, gain_first, gain_second, conv_first, conv_second,
    output, input_grad, out_gains, out_conv, out_qkv, out_out, out_ffn, out_norm,
    new_m_qkv, new_m_out, new_m_ffn,
    new_gain_first, new_gain_second, new_conv_first, new_conv_second, new_gains, new_conv,
    new_qkv, new_out, new_ffn,
):
    core = lax.axis_index("dp") % 2
    output[...] = out_rows[...]
    input_grad[...] = grad_rows[...]
    norm = wide[11:12, 0:1]
    out_norm[...] = norm
    factor = CLIP_NORM / jnp.maximum(norm, CLIP_NORM)
    grad = wide[0:2, :] * factor
    out_gains[...] = grad
    first, second, new = adam(gains[...], grad, gain_first[...], gain_second[...])
    new_gain_first[...], new_gain_second[...], new_gains[...] = first, second, new
    for t in range(KW):
        grad = wide[2 + 3 * t : 5 + 3 * t, :] * factor
        out_conv[t] = grad
        first, second, new = adam(conv[t], grad, conv_first[t], conv_second[t])
        new_conv_first[t], new_conv_second[t], new_conv[t] = first, second, new
    grad = g_ffn[...] * factor
    out_ffn[...] = grad
    new_m_ffn[...] = MOMENTUM * m_ffn[...] + grad
    new_ffn[...] = w_ffn[...] - RATE_IN * math.sqrt(max(FF, D)) * o_ffn[...]
    own_rows = rows(core * SUB, SUB)
    for kind in range(3):
        grad = g_heads[kind, own_rows, :] * factor
        out_qkv[kind] = grad
        new_m_qkv[kind] = MOMENTUM * m_qkv[kind] + grad
    new_qkv[...] = w_qkv[...] - RATE_IN * math.sqrt(D) * o_heads[0:3]
    grad = g_heads[3, own_rows, :] * factor
    out_out[...] = grad
    new_m_out[...] = MOMENTUM * m_out[...] + grad
    new_out[...] = w_out[...] - RATE_OUT * math.sqrt(D) * o_heads[3]


def update(*arrays):
    vmem = pl.BlockSpec(memory_space=pltpu.VMEM)
    m_ffn, m_qkv, m_out, _, _, _, gains, conv = arrays[7:15]
    rows_like = arrays[6]
    like = [rows_like, rows_like, gains, conv, m_qkv, m_out, m_ffn, None, m_qkv, m_out, m_ffn]
    like += [gains, gains, conv, conv, gains, conv, m_qkv, m_out, m_ffn]
    return pl.pallas_call(
        update_kernel,
        out_shape=[
            jax.ShapeDtypeStruct((1, 1) if entry is None else entry.shape, jnp.float32)
            for entry in like
        ],
        in_specs=[vmem] * len(arrays),
        out_specs=[vmem] * len(like),
        name="update",
        compiler_params=pltpu.CompilerParams(vmem_limit_bytes=63 * 2**20),
    )(*arrays)


def per_device(
    tokens,
    lengths,
    cotangent,
    gains,
    conv,
    w_qkv,
    w_out,
    ffn_weights,
    mom_qkv,
    mom_out,
    mom_ffn,
    gain_first,
    gain_second,
    conv_first,
    conv_second,
):
    rows_in = tokens[0]
    output, grad_middle, normed_part, small, ffn_pair, heads_pair = layer(
        lengths, rows_in, cotangent[0], gains, conv, w_qkv, w_out.T, ffn_weights
    )
    wide, g_ffn, o_ffn, o_heads, input_grad = optimizer(
        ffn_pair, heads_pair, small, normed_part, mom_ffn, mom_qkv, mom_out.T, rows_in, grad_middle, gains
    )
    updated = update(
        wide, g_ffn, heads_pair, o_ffn, o_heads, input_grad, output,
        mom_ffn, mom_qkv, mom_out.T, ffn_weights, w_qkv, w_out.T,
        gains, conv, gain_first, gain_second, conv_first, conv_second,
    )
    updated = list(updated)
    for number in (5, 9, 18):
        updated[number] = updated[number].T
    return (updated[0][None], updated[1][None], *updated[2:7], updated[7][0, 0], *updated[8:])


def solution(mesh):
    placed = (
        P("dp", "head", None),
        P("dp"),
        P("dp", "head", None),
        P(),
        P(),
        P(None, "dp", "head"),
        P("head", "dp"),
        P(None, ("head", "dp"), None),
        P(None, "dp", "head"),
        P("head", "dp"),
        P(None, ("head", "dp"), None),
        P(),
        P(),
        P(),
        P(),
    )
    return jax.shard_map(
        per_device,
        mesh=mesh,
        in_specs=placed,
        out_specs=(
            P("dp", "head", None),
            P("dp", "head", None),
            P(),
            P(),
            P(None, "dp", "head"),
            P("head", "dp"),
            P(None, ("head", "dp"), None),
            P(),
            P(None, "dp", "head"),
            P("head", "dp"),
            P(None, ("head", "dp"), None),
            P(),
            P(),
            P(),
            P(),
            P(),
            P(),
            P(None, "dp", "head"),
            P("head", "dp"),
            P(None, ("head", "dp"), None),
        ),
        check_vma=False,
    )
```
